32 devices in a mesh: dp: 8 (over y, x, core), ctx: 4 (over z).
Axes of the slice: x: 2, y: 2, z: 4, core: 2. Of those that a mesh axis runs over, the one named last changes fastest.
Arguments:
- tokens: bfloat16 [32, 1024, 512], P(('dp', 'ctx')), may hold values from -6 to 6
- memory: bfloat16 [32, 1024, 512], P('dp', 'ctx'), may hold values from -6 to 6
- mem_mask: int32 [32, 1024], P('dp', 'ctx'), may hold values from 0 to 1, as said below
- segment_ids: int32 [32, 1024], P(('dp', 'ctx')), may hold values from 0 to 3, never falling along the last dimension, each value on 1 to 512 neighbouring positions
- cotangent: bfloat16 [32, 1024, 512], P(('dp', 'ctx')), may hold values from -6 to 6
- self_qkv: bfloat16 [512, 1536], replicated, may hold values from -0.25 to 0.25
- self_bias: bfloat16 [2, 512], replicated, may hold values from -2 to 2
- self_out: bfloat16 [512, 512], replicated, may hold values from -1.5 to 1.5
- self_out_bias: bfloat16 [512], replicated, may hold values from -2 to 2
- cross_q: bfloat16 [512, 512], replicated, may hold values from -0.25 to 0.25
- cross_kv: bfloat16 [512, 1024], replicated, may hold values from -0.25 to 0.25
- cross_bias: bfloat16 [2, 512], replicated, may hold values from -2 to 2
- cross_out: bfloat16 [512, 512], replicated, may hold values from -2 to 2
- cross_out_bias: bfloat16 [512], replicated, may hold values from -2 to 2
- ffn_in: bfloat16 [512, 2048], replicated, may hold values from -0.25 to 0.25
- ffn_in_bias: bfloat16 [2048], replicated, may hold values from -2 to 2
- ffn_out: bfloat16 [2048, 512], replicated, may hold values from -0.1875 to 0.1875
- ffn_out_bias: bfloat16 [512], replicated, may hold values from -2 to 2
- omegas: bfloat16 [3, 512], replicated, may hold values from 0.5 to 2
- ln_gains: bfloat16 [3, 512], replicated, may hold values from 0.5 to 1.5
- ln_biases: bfloat16 [3, 512], replicated, may hold values from -2 to 2
Outputs:
- activations: bfloat16 [32, 1024, 512], P(('dp', 'ctx'))
- token_grad: bfloat16 [32, 1024, 512], P(('dp', 'ctx'))
- memory_grad: bfloat16 [32, 1024, 512], P('dp', 'ctx')
- grad_self_qkv: float32 [512, 1536], replicated
- grad_self_bias: float32 [2, 512], replicated
- grad_self_out: float32 [512, 512], replicated
- grad_self_out_bias: float32 [512], replicated
- grad_cross_q: float32 [512, 512], replicated
- grad_cross_kv: float32 [512, 1024], replicated
- grad_cross_bias: float32 [2, 512], replicated
- grad_cross_out: float32 [512, 512], replicated
- grad_cross_out_bias: float32 [512], replicated
- grad_ffn_in: float32 [512, 2048], replicated
- grad_ffn_in_bias: float32 [2048], replicated
- grad_ffn_out: float32 [2048, 512], replicated
- grad_ffn_out_bias: float32 [512], replicated
- grad_omegas: float32 [3, 512], replicated
- grad_ln_gains: float32 [3, 512], replicated
- grad_ln_biases: float32 [3, 512], replicated
The draws below stay inside these ranges and needn't reach their ends.
Inputs may be any that keep to these rules, and one draw needn't show every extreme that they name: `mem_mask`: each row is 1 on a prefix of 512 or more positions and 0 after it; in each aligned block of 4 rows one row, drawn from the seed, is all ones. `segment_ids`: ids never fall along a row; a document holds 1 to 512 tokens.
All inputs are finite; a program needn't handle non-finite values.
Results may differ from the reference program's by a relative error of at most 0.02.
Values may be sent and summed in bfloat16 or wider, within the bound.
No kernel may reach another device: no remote copies, remote signals or barrier semaphores. Data moves between devices by JAX's collectives and lax.ppermute only.
A program may use at most 256 MiB of HBM per device.

```python
import math
import jax
import jax.numpy as jnp
import numpy as np
from jax import lax

D = 512
HEADS = 8
HEAD_DIM = 64
FF = 2048
TGT_LEN = 1024
MEM_LEN = 1024
GROUP_SEQS = 4
SEQS = 32


def draw_mem_mask(key, part):
    length_key, pick_key = jax.random.split(jax.random.fold_in(key, 17))
    lengths = jax.random.randint(length_key, (SEQS,), MEM_LEN // 2, MEM_LEN + 1)
    picked = jax.random.randint(pick_key, (SEQS // GROUP_SEQS,), 0, GROUP_SEQS)
    places = jnp.arange(SEQS) % GROUP_SEQS
    chosen = jnp.repeat(picked, GROUP_SEQS)
    lengths = jnp.where(places == chosen, MEM_LEN, lengths)
    return (jnp.arange(MEM_LEN)[None, :] < lengths[:, None]).astype(jnp.int32)


def levels(own_key, dims, pieces, low, largest):
    factor_of, own = 1.0, jax.random.fold_in(own_key, 6)
    for dim, shards_of in pieces:
        heights = jnp.exp(jax.random.uniform(jax.random.fold_in(own, dim), (shards_of,), jnp.float32, low / len(pieces), largest / len(pieces)))
        factor_of = factor_of * jnp.repeat(heights, dims[dim] // shards_of).reshape([-1 if axis == dim else 1 for axis in range(len(dims))])
    return factor_of


def profile(number_of, total, limit, slope):
    portions = [(1 << 20) // math.isqrt(rank ** slope) + 1 for rank in range(2, number_of + 1)]
    rest, counts = total - limit - (number_of - 1), [1] * (number_of - 1)
    while rest > 0:
        candidates = [i for i in range(number_of - 1) if counts[i] < limit]
        pool, left = sum([portions[i] for i in candidates]), rest
        for i in candidates:
            addition = min(limit - counts[i], max(1, left * portions[i] // pool), rest)
            counts[i] = counts[i] + addition
            rest = rest - addition
    return np.array([limit] + counts)


def uneven(rng, amount, total, most, lean):
    if amount == 2:
        one = jax.random.randint(rng, (), max(1, total - most), min(most, total - 1) + 1)
        return jnp.stack([one, total - one])
    sizes = jnp.asarray(profile(amount, total, most, lean), jnp.int32)
    twos = (amount - 1) // 2
    source_of, receiver = sizes[1:1 + 2 * twos:2], sizes[2:2 + 2 * twos:2]
    room = jnp.minimum(source_of - 1, most - receiver)
    passed = jax.random.randint(jax.random.fold_in(rng, 1), (twos,), 0, 1 << 20) % (room + 1)
    sizes = sizes.at[1:1 + 2 * twos:2].set(source_of - passed).at[2:2 + 2 * twos:2].set(receiver + passed)
    return sizes[jax.random.permutation(jax.random.fold_in(rng, 2), amount)]


def bell_draw(rng, extent, width, most, shards=(), dtype=jnp.bfloat16):
    factor_of = levels(rng, extent, shards, -0.22, 0.18) if shards else 1.0
    entries = jax.random.normal(rng, extent, jnp.float32) * width * factor_of
    return jnp.minimum(jnp.maximum(entries, -most), most).astype(dtype)


def setup_inputs(seed: int = 0) -> dict:
    keys = jax.random.split(jax.random.key(seed), 22)
    tokens = bell_draw(keys[0], (SEQS, TGT_LEN, D), 1.0, 6.0, ((0, 32),))
    memory = bell_draw(keys[1], (SEQS, MEM_LEN, D), 1.0, 6.0, ((0, 8), (1, 4)))
    mem_mask = draw_mem_mask(jax.random.fold_in(keys[21], 71), 0)
    segment_ids = jax.vmap(lambda own: jnp.searchsorted(jnp.cumsum(uneven(own, 4, TGT_LEN, TGT_LEN // 2, 1)), jnp.arange(TGT_LEN), side="right"))(jax.random.split(keys[3], SEQS)).reshape((SEQS, TGT_LEN)).astype(jnp.int32)
    cotangent = bell_draw(keys[4], (SEQS, TGT_LEN, D), 1.0, 6.0, ((0, 32),))
    self_qkv = bell_draw(keys[5], (D, 3 * D), D ** -0.5, 0.25)
    self_bias = bell_draw(keys[6], (2, D), 0.3, 2.0)
    self_out = bell_draw(keys[7], (D, D), (D // 32) ** -0.5, 1.5)
    self_out_bias = bell_draw(keys[8], (D,), 0.3, 2.0)
    cross_q = bell_draw(keys[9], (D, D), D ** -0.5, 0.25)
    cross_kv = bell_draw(keys[10], (D, 2 * D), D ** -0.5, 0.25)
    cross_bias = bell_draw(keys[11], (2, D), 0.3, 2.0)
    cross_out = bell_draw(keys[12], (D, D), (D // 64) ** -0.5, 2.0)
    cross_out_bias = bell_draw(keys[13], (D,), 0.3, 2.0)
    ffn_in = bell_draw(keys[14], (D, FF), D ** -0.5, 0.25)
    ffn_in_bias = bell_draw(keys[15], (FF,), 0.3, 2.0)
    ffn_out = bell_draw(keys[16], (FF, D), (FF // 2) ** -0.5, 0.1875)
    ffn_out_bias = bell_draw(keys[17], (D,), 0.3, 2.0)
    omegas = jnp.clip(jnp.exp(jax.random.uniform(keys[18], (3, D), jnp.float32, math.log(0.5), math.log(2.0))), 0.5, 2.0).astype(jnp.bfloat16)
    ln_gains = jnp.clip(1.0 + 0.1 * jax.random.normal(keys[19], (3, D), jnp.float32), 0.5, 1.5).astype(jnp.bfloat16)
    ln_biases = bell_draw(keys[20], (3, D), 0.3, 2.0)
    return {"tokens": tokens, "memory": memory, "mem_mask": mem_mask, "segment_ids": segment_ids, "cotangent": cotangent, "self_qkv": self_qkv, "self_bias": self_bias, "self_out": self_out, "self_out_bias": self_out_bias, "cross_q": cross_q, "cross_kv": cross_kv, "cross_bias": cross_bias, "cross_out": cross_out, "cross_out_bias": cross_out_bias, "ffn_in": ffn_in, "ffn_in_bias": ffn_in_bias, "ffn_out": ffn_out, "ffn_out_bias": ffn_out_bias, "omegas": omegas, "ln_gains": ln_gains, "ln_biases": ln_biases}


@jax.custom_vjp
def low(v):
    return lax.optimization_barrier(v.astype(jnp.bfloat16)).astype(jnp.float32)

@jax.custom_vjp
def low_back(v):
    return v

def low_keep(v):
    return (low(v), None)

def low_pass(kept, grad):
    return (grad,)

def back_keep(v):
    return (v, None)

def back_low(kept, grad):
    return (low(grad),)
low.defvjp(low_keep, low_pass)
low_back.defvjp(back_keep, back_low)

def rounded_both(value):
    return low_back(low(value))

def matmul_high(left, right):
    return jnp.dot(left, right, precision=lax.Precision.HIGHEST)

def layer_norm(summed, gain, shift):
    centered = summed - lax.optimization_barrier(jnp.mean(summed, axis=-1, keepdims=True))
    spread = lax.optimization_barrier(jnp.mean(centered * centered, axis=-1, keepdims=True))
    return centered * lax.rsqrt(spread + 1e-05) * gain + shift

def attend(query_rows, key_rows, value_rows, allowed):
    length = query_rows.shape[0]
    key_count = key_rows.shape[0]
    query_heads = query_rows.reshape(length, HEADS, HEAD_DIM)
    key_heads = key_rows.reshape(key_count, HEADS, HEAD_DIM)
    value_heads = value_rows.reshape(key_count, HEADS, HEAD_DIM)
    scores = jnp.einsum('qhe,khe->hqk', query_heads, key_heads, precision=lax.Precision.HIGHEST) * HEAD_DIM ** (-0.5)
    scores = low_back(scores)
    scores = jnp.where(allowed[None], scores, -1e+30)
    maximum = lax.optimization_barrier(jnp.max(scores, axis=-1, keepdims=True))
    weights = jnp.exp(scores - maximum)
    weights = weights / lax.optimization_barrier(jnp.sum(weights, axis=-1, keepdims=True))
    weights = low(weights)
    blended = jnp.einsum('hqk,khe->qhe', weights, value_heads, precision=lax.Precision.HIGHEST)
    return rounded_both(blended.reshape(length, HEADS * HEAD_DIM))

def sequence_layer(params, token_row, memory_row, mask_row, segment_row):
    self_qkv, self_bias, self_out, self_out_bias, cross_q, cross_kv, cross_bias, cross_out, cross_out_bias, ffn_in, ffn_in_bias, ffn_out, ffn_out_bias, omegas, ln_gains, ln_biases = params
    model_width = token_row.shape[-1]
    length = token_row.shape[0]
    queries = rounded_both(matmul_high(token_row, self_qkv[:, :model_width]) + self_bias[0])
    keys_self = rounded_both(matmul_high(token_row, self_qkv[:, model_width:2 * model_width]))
    values_self = rounded_both(matmul_high(token_row, self_qkv[:, 2 * model_width:]) + self_bias[1])
    positions = jnp.arange(length)
    allowed = (segment_row[:, None] == segment_row[None, :]) & (positions[None, :] <= positions[:, None])
    attended = attend(queries, keys_self, values_self, allowed)
    branch_one = low_back(matmul_high(attended, self_out) + self_out_bias)
    first = low(layer_norm(omegas[0] * token_row + branch_one, ln_gains[0], ln_biases[0]))
    cross_query = rounded_both(matmul_high(first, cross_q) + cross_bias[0])
    memory_keys = rounded_both(matmul_high(memory_row, cross_kv[:, :model_width]))
    memory_values = rounded_both(matmul_high(memory_row, cross_kv[:, model_width:]) + cross_bias[1])
    visible = jnp.broadcast_to(mask_row[None, :] > 0, (length, memory_row.shape[0]))
    crossed = attend(cross_query, memory_keys, memory_values, visible)
    branch_two = low_back(matmul_high(crossed, cross_out) + cross_out_bias)
    second = low(layer_norm(omegas[1] * first + branch_two, ln_gains[1], ln_biases[1]))
    hidden_pre = low_back(matmul_high(second, ffn_in) + ffn_in_bias)
    hidden = low(jax.nn.gelu(hidden_pre))
    branch_three = low_back(matmul_high(hidden, ffn_out) + ffn_out_bias)
    return layer_norm(omegas[2] * second + branch_three, ln_gains[2], ln_biases[2])

def reference(tokens, memory, mem_mask, segment_ids, cotangent, self_qkv, self_bias, self_out, self_out_bias, cross_q, cross_kv, cross_bias, cross_out, cross_out_bias, ffn_in, ffn_in_bias, ffn_out, ffn_out_bias, omegas, ln_gains, ln_biases):
    params = tuple((weight.astype(jnp.float32) for weight in (self_qkv, self_bias, self_out, self_out_bias, cross_q, cross_kv, cross_bias, cross_out, cross_out_bias, ffn_in, ffn_in_bias, ffn_out, ffn_out_bias, omegas, ln_gains, ln_biases)))

    def forward(param_set, token_rows, memory_rows):
        checked = jax.checkpoint(sequence_layer)

        def one_row(carry, items):
            return (carry, checked(param_set, items[0], items[1], items[2], items[3]))
        _, outputs = lax.scan(one_row, jnp.zeros((), jnp.float32), (token_rows, memory_rows, mem_mask, segment_ids))
        return outputs
    outputs, pullback = jax.vjp(forward, params, tokens.astype(jnp.float32), memory.astype(jnp.float32))
    param_grads, token_grad, memory_grad = pullback(cotangent.astype(jnp.float32))
    return (outputs.astype(jnp.bfloat16), token_grad.astype(jnp.bfloat16), memory_grad.astype(jnp.bfloat16), param_grads[0], param_grads[1], param_grads[2], param_grads[3], param_grads[4], param_grads[5], param_grads[6], param_grads[7], param_grads[8], param_grads[9], param_grads[10], param_grads[11], param_grads[12], param_grads[13], param_grads[14], param_grads[15])
```

```python
import functools

import jax
import jax.numpy as jnp
from jax import lax
from jax.experimental import pallas as pl
from jax.experimental.pallas import tpu as pltpu
from jax.sharding import PartitionSpec as P

HEADS = 8
LOG2E = 1.4426950408889634
LN2 = 0.6931471805599453
UNSEEN = -1e30
BLOCK = 256
REACH = 2
PAD = 16
VMEM = 60 * 2**20
bf16, f32 = jnp.bfloat16, jnp.float32

SELF_BIAS, SELF_OUT_BIAS, CROSS_BIAS, CROSS_OUT_BIAS = 0, 2, 3, 5
FFN_IN_BIAS, FFN_OUT_BIAS, OMEGA, GAIN, SHIFT, SMALL = 6, 10, 11, 14, 17, 24


def dot(left, right, left_dim, right_dim):
    return lax.dot_general(
        left, right, (((left_dim,), (right_dim,)), ((), ())), preferred_element_type=f32
    )


def column(row):
    return jnp.transpose(jnp.broadcast_to(row, (8, row.shape[1])))[:, :1]


def row_sum(value):
    return jnp.sum(value.astype(f32), axis=0, keepdims=True)


def feature_sum(value):
    ones = jnp.ones((PAD, value.shape[1]), bf16)
    return dot(ones, value, 1, 1)[:1]


def normalize(value):
    centered = value - jnp.mean(value, axis=-1, keepdims=True)
    spread = jnp.mean(centered * centered, axis=-1, keepdims=True)
    inverse = lax.rsqrt(spread + 1e-05)
    return centered * inverse, inverse


def normalize_back(grad, gain, normal, inverse):
    scaled = grad * gain
    mean = jnp.mean(scaled, axis=-1, keepdims=True)
    slope = jnp.mean(scaled * normal, axis=-1, keepdims=True)
    return (scaled - mean - normal * slope) * inverse


def self_forward_kernel(
    x_ref, seg_ref, par_ref, qkv_w, out_w, cross_w,
    qkv_ref, e_ref, inv_ref, o_ref, z_ref, h_ref, q_ref, q_mask, k_mask,
):
    head = pl.program_id(0)
    length, width = x_ref.shape
    size = width // HEADS
    scale = size**-0.5 * LOG2E

    @pl.when(head == 0)
    def _():
        x = x_ref[...]
        for part, row in ((0, 0), (1, None), (2, 1)):
            columns = slice(part * width, (part + 1) * width)
            value = dot(qkv_w[:, columns], x, 0, 1)
            if row is not None:
                value = value + column(par_ref[SELF_BIAS + row : SELF_BIAS + row + 1])
            if part == 0:
                value = value * scale
            qkv_ref[columns, :] = value.astype(bf16)
        same = lax.broadcasted_iota(jnp.int32, (PAD, length), 0) == seg_ref[...]
        q_mask[...] = jnp.where(same, 1.0, 0.0).astype(bf16)
        k_mask[...] = jnp.where(same, 0.0, UNSEEN).astype(bf16)

    base = pl.multiple_of(head * size, size)
    q = jnp.concatenate((qkv_ref[pl.ds(base, size), :], q_mask[...]), axis=0)
    k = jnp.concatenate((qkv_ref[pl.ds(width + base, size), :], k_mask[...]), axis=0)
    v = jnp.concatenate(
        (qkv_ref[pl.ds(2 * width + base, size), :], jnp.ones((PAD, length), bf16)), axis=0
    )
    causal = lax.broadcasted_iota(jnp.int32, (BLOCK, BLOCK), 0) <= lax.broadcasted_iota(
        jnp.int32, (BLOCK, BLOCK), 1
    )
    for j in range(length // BLOCK):
        mine = slice(j * BLOCK, (j + 1) * BLOCK)
        first = max(0, j - REACH)
        scores = [
            dot(k[:, i * BLOCK : (i + 1) * BLOCK], q[:, mine], 0, 0) for i in range(first, j + 1)
        ]
        scores[-1] = jnp.where(causal, scores[-1], UNSEEN)
        top = functools.reduce(jnp.maximum, [jnp.max(s, axis=0, keepdims=True) for s in scores])
        weights = [jnp.exp2(s - top).astype(bf16) for s in scores]
        for i, weight in zip(range(first, j + 1), weights):
            e_ref[0, i, :, (j - i) * BLOCK : (j - i + 1) * BLOCK] = weight
        mixed = dot(v[:, first * BLOCK : (j + 1) * BLOCK], jnp.concatenate(weights, axis=0), 1, 0)
        inverse = 1.0 / mixed[size : size + 1]
        o_ref[pl.ds(base, size), mine] = (mixed[:size] * inverse).astype(bf16)
        inv_ref[pl.ds(head, 1), mine] = inverse

    @pl.when(head == HEADS - 1)
    def _():
        z = (
            par_ref[OMEGA : OMEGA + 1] * x_ref[...].astype(f32)
            + dot(o_ref[...], out_w[...], 0, 0)
            + par_ref[SELF_OUT_BIAS : SELF_OUT_BIAS + 1]
        )
        z_ref[...] = z
        normal, _ = normalize(z)
        h = (normal * par_ref[GAIN : GAIN + 1] + par_ref[SHIFT : SHIFT + 1]).astype(bf16)
        h_ref[...] = h
        value = dot(cross_w[...], h, 0, 1) + column(par_ref[CROSS_BIAS : CROSS_BIAS + 1])
        q_ref[...] = (value * scale).astype(bf16)


def cross_forward_kernel(
    m_ref, q_ref, h1_ref, par_ref, kv_w, out_w,
    kv_ref, e_ref, inv_ref, o_ref, z_ref, h_ref, k_mask,
):
    head = pl.program_id(0)
    length, width = h1_ref.shape
    size = width // HEADS
    holders, part_rows = m_ref.shape[0], m_ref.shape[1] - PAD

    @pl.when(head == 0)
    def _():
        shift = column(par_ref[CROSS_BIAS + 1 : CROSS_BIAS + 2])
        first = lax.broadcasted_iota(jnp.int32, (PAD, part_rows), 0) == 0
        for b in range(holders):
            columns = slice(b * part_rows, (b + 1) * part_rows)
            m = m_ref[b, :part_rows, :]
            kv_ref[:width, columns] = dot(kv_w[:, :width], m, 0, 1).astype(bf16)
            kv_ref[width:, columns] = (dot(kv_w[:, width:], m, 0, 1) + shift).astype(bf16)
            seen = m_ref[b, part_rows:, :part_rows].astype(f32) > 0.5
            k_mask[:, columns] = jnp.where(first & ~seen, UNSEEN, 0.0).astype(bf16)

    base = pl.multiple_of(head * size, size)
    count = kv_ref.shape[1]
    q = jnp.concatenate((q_ref[pl.ds(base, size), :], jnp.ones((PAD, length), bf16)), axis=0)
    k = jnp.concatenate((kv_ref[pl.ds(base, size), :], k_mask[...]), axis=0)
    v = jnp.concatenate(
        (kv_ref[pl.ds(width + base, size), :], jnp.ones((PAD, count), bf16)), axis=0
    )
    step = length
    for j in range(length // step):
        mine = slice(j * step, (j + 1) * step)
        scores = dot(k, q[:, mine], 0, 0)
        top = jnp.max(scores, axis=0, keepdims=True)
        weights = jnp.exp2(scores - top).astype(bf16)
        e_ref[0, :, mine] = weights
        mixed = dot(v, weights, 1, 0)
        inverse = 1.0 / mixed[size : size + 1]
        o_ref[pl.ds(base, size), mine] = (mixed[:size] * inverse).astype(bf16)
        inv_ref[pl.ds(head, 1), mine] = inverse

    @pl.when(head == HEADS - 1)
    def _():
        z = (
            par_ref[OMEGA + 1 : OMEGA + 2] * h1_ref[...].astype(f32)
            + dot(o_ref[...], out_w[...], 0, 0)
            + par_ref[CROSS_OUT_BIAS : CROSS_OUT_BIAS + 1]
        )
        z_ref[...] = z
        normal, _ = normalize(z)
        h_ref[...] = (
            normal * par_ref[GAIN + 1 : GAIN + 2] + par_ref[SHIFT + 1 : SHIFT + 2]
        ).astype(bf16)


def ffn_kernel(
    h2_ref, h1_ref, z2_ref, cot_ref, par_ref, in_w, out_w,
    act_ref, dz_ref, grad_ref, small_ref, g_buf, slope_buf, e_buf, eu_buf,
):
    step = pl.program_id(0)
    rows, width = cot_ref.shape
    hidden = in_w.shape[1]
    chunks = hidden // width
    begin = pl.multiple_of(step * rows, rows)
    mine = pl.ds(begin, rows)

    @pl.when(step == 0)
    def _():
        small_ref[...] = jnp.zeros_like(small_ref)

    def add(row, value):
        small_ref[row : row + 1] += row_sum(value)

    h2 = h2_ref[mine, :]
    h2_wide = h2.astype(f32)
    for c in range(chunks):
        columns = slice(c * width, (c + 1) * width)
        u = dot(h2, in_w[:, columns], 1, 0) + par_ref[FFN_IN_BIAS + c : FFN_IN_BIAS + c + 1]
        rate = 0.7978845608028654
        square = u * u
        t = jnp.tanh(u * (rate + (rate * 0.044715) * square))
        half = 0.5 + 0.5 * t
        g_buf[mine, columns] = (u * half).astype(bf16)
        slope_buf[:, columns] = half + (0.5 * u) * (1.0 - t * t) * (
            rate + (3 * rate * 0.044715) * square
        )
    z3 = (
        par_ref[OMEGA + 2 : OMEGA + 3] * h2_wide
        + dot(g_buf[mine, :], out_w[...], 1, 0)
        + par_ref[FFN_OUT_BIAS : FFN_OUT_BIAS + 1]
    )
    normal, inverse = normalize(z3)
    gain = par_ref[GAIN + 2 : GAIN + 3]
    act_ref[...] = (normal * gain + par_ref[SHIFT + 2 : SHIFT + 3]).astype(bf16)
    dy = cot_ref[...].astype(f32)
    add(GAIN + 2, dy * normal)
    add(SHIFT + 2, dy)
    dz3 = normalize_back(dy, gain, normal, inverse)
    add(OMEGA + 2, dz3 * h2_wide)
    e3 = dz3.astype(bf16)
    e_buf[mine, :] = e3
    add(FFN_OUT_BIAS, e3)
    for c in range(chunks):
        columns = slice(c * width, (c + 1) * width)
        eu = (dot(e3, out_w[columns, :], 1, 1) * slope_buf[:, columns]).astype(bf16)
        eu_buf[mine, columns] = eu
        add(FFN_IN_BIAS + c, eu)
    dh2 = par_ref[OMEGA + 2 : OMEGA + 3] * dz3 + dot(eu_buf[mine, :], in_w[...], 1, 1)
    normal, inverse = normalize(z2_ref[...])
    add(GAIN + 1, dh2 * normal)
    add(SHIFT + 1, dh2)
    dz2 = normalize_back(dh2, par_ref[GAIN + 1 : GAIN + 2], normal, inverse)
    add(OMEGA + 1, dz2 * h1_ref[...].astype(f32))
    add(CROSS_OUT_BIAS, dz2.astype(bf16))
    dz_ref[...] = dz2

    @pl.when(step == pl.num_programs(0) - 1)
    def _():
        for c in range(chunks):
            columns = slice(c * width, (c + 1) * width)
            grad_ref[columns, :] = dot(g_buf[:, columns], e_buf[...], 0, 0).astype(bf16)
            grad_ref[hidden + c * width : hidden + (c + 1) * width, :] = dot(
                h2_ref[...], eu_buf[:, columns], 0, 0
            ).astype(bf16)


def back_head(do_rows, o_rows, length):
    delta = jnp.sum(do_rows.astype(f32) * o_rows.astype(f32), axis=0, keepdims=True)
    high = delta.astype(bf16).astype(f32)
    row = lax.broadcasted_iota(jnp.int32, (PAD, length), 0)
    extra = jnp.where(row == 0, -high, jnp.where(row == 1, high - delta, 0.0))
    return jnp.concatenate((do_rows, extra.astype(bf16)), axis=0)


def cross_backward_kernel(
    e_ref, inv_ref, o_ref, q_ref, kv_ref, dz2_ref, h1_ref, z1_ref, x_ref, m_ref, par_ref,
    out_w, q_w, kv_w,
    dz1_ref, mem_ref, grad_ref, small_ref, do_buf, dq_buf, dkv_buf,
):
    head = pl.program_id(0)
    length, width = x_ref.shape
    size = width // HEADS
    count = kv_ref.shape[1]
    holders, part_rows = m_ref.shape[0], m_ref.shape[1] - PAD

    @pl.when(head == 0)
    def _():
        small_ref[...] = jnp.zeros_like(small_ref)
        e2 = dz2_ref[...].astype(bf16)
        grad_ref[width : 2 * width, :] = dot(o_ref[...], e2, 1, 0).astype(bf16)
        for i in range(HEADS):
            rows = slice(i * size, (i + 1) * size)
            do_buf[rows, :] = (dot(out_w[rows, :], e2, 1, 1) * inv_ref[i : i + 1]).astype(bf16)

    base = pl.multiple_of(head * size, size)
    rows = pl.ds(base, size)
    do = back_head(do_buf[rows, :], o_ref[rows, :], length)
    q = q_ref[rows, :]
    k = kv_ref[rows, :]
    v = jnp.concatenate(
        (kv_ref[pl.ds(width + base, size), :], jnp.ones((PAD, count), bf16)), axis=0
    )
    dq = None
    for i in range(count // BLOCK):
        mine = slice(i * BLOCK, (i + 1) * BLOCK)
        weights = e_ref[0, mine, :]
        ds = (weights.astype(f32) * dot(v[:, mine], do, 0, 0)).astype(bf16)
        dkv_buf[pl.ds(width + base, size), mine] = dot(do[:size], weights, 1, 1).astype(bf16)
        dkv_buf[rows, mine] = (dot(q, ds, 1, 1) * LN2).astype(bf16)
        part = dot(k[:, mine], ds, 1, 0)
        dq = part if dq is None else dq + part
    dq_buf[rows, :] = (dq * size**-0.5).astype(bf16)

    @pl.when(head == HEADS - 1)
    def _():
        dq_all = dq_buf[...]
        small_ref[CROSS_BIAS : CROSS_BIAS + 1] = feature_sum(dq_all)
        small_ref[CROSS_BIAS + 1 : CROSS_BIAS + 2] = feature_sum(dkv_buf[width:, :])
        grad_ref[:width, :] = dot(h1_ref[...], dq_all, 0, 1).astype(bf16)
        key_grad = value_grad = None
        for b in range(holders):
            columns = slice(b * part_rows, (b + 1) * part_rows)
            m = m_ref[b, :part_rows, :]
            part = dkv_buf[:, columns]
            k_part, v_part = dot(m, part[:width], 0, 1), dot(m, part[width:], 0, 1)
            key_grad = k_part if b == 0 else key_grad + k_part
            value_grad = v_part if b == 0 else value_grad + v_part
            mem_ref[b] = dot(part, kv_w[...], 0, 1).astype(bf16)
        grad_ref[2 * width : 3 * width, :] = key_grad.astype(bf16)
        grad_ref[3 * width :, :] = value_grad.astype(bf16)
        dh1 = par_ref[OMEGA + 1 : OMEGA + 2] * dz2_ref[...] + dot(dq_all, q_w[...], 0, 1)
        normal, inverse = normalize(z1_ref[...])
        small_ref[GAIN : GAIN + 1] = row_sum(dh1 * normal)
        small_ref[SHIFT : SHIFT + 1] = row_sum(dh1)
        dz1 = normalize_back(dh1, par_ref[GAIN : GAIN + 1], normal, inverse)
        small_ref[OMEGA : OMEGA + 1] = row_sum(dz1 * x_ref[...].astype(f32))
        small_ref[SELF_OUT_BIAS : SELF_OUT_BIAS + 1] = row_sum(dz1.astype(bf16))
        dz1_ref[...] = dz1


def self_backward_kernel(
    e_ref, inv_ref, o_ref, qkv_ref, dz1_ref, x_ref, par_ref, out_w, qkv_w,
    token_ref, grad_ref, small_ref, do_buf, d_buf, dq_buf,
):
    head = pl.program_id(0)
    length, width = x_ref.shape
    size = width // HEADS
    blocks = length // BLOCK

    @pl.when(head == 0)
    def _():
        small_ref[...] = jnp.zeros_like(small_ref)
        e1 = dz1_ref[...].astype(bf16)
        grad_ref[:width, :] = dot(o_ref[...], e1, 1, 0).astype(bf16)
        for i in range(HEADS):
            rows = slice(i * size, (i + 1) * size)
            do_buf[rows, :] = (dot(out_w[rows, :], e1, 1, 1) * inv_ref[i : i + 1]).astype(bf16)

    base = pl.multiple_of(head * size, size)
    rows = pl.ds(base, size)
    do = back_head(do_buf[rows, :], o_ref[rows, :], length)
    q = qkv_ref[rows, :]
    k = qkv_ref[pl.ds(width + base, size), :]
    v = jnp.concatenate(
        (qkv_ref[pl.ds(2 * width + base, size), :], jnp.ones((PAD, length), bf16)), axis=0
    )
    for i in range(blocks):
        mine = slice(i * BLOCK, (i + 1) * BLOCK)
        last = min(blocks, i + REACH + 1)
        seen = slice(i * BLOCK, last * BLOCK)
        weights = e_ref[0, i, :, : (last - i) * BLOCK]
        ds = (weights.astype(f32) * dot(v[:, mine], do[:, seen], 0, 0)).astype(bf16)
        d_buf[pl.ds(2 * width + base, size), mine] = dot(do[:size, seen], weights, 1, 1).astype(
            bf16
        )
        d_buf[pl.ds(width + base, size), mine] = (dot(q[:, seen], ds, 1, 1) * LN2).astype(bf16)
        part = dot(k[:, mine], ds, 1, 0)
        fresh = slice(max(0, i + REACH) * BLOCK if i else 0, last * BLOCK)
        if i == 0:
            dq_buf[:, seen] = part
        else:
            old = slice(i * BLOCK, min(blocks, i + REACH) * BLOCK)
            reach = old.stop - old.start
            dq_buf[:, old] += part[:, :reach]
            if fresh.start < fresh.stop:
                dq_buf[:, fresh] = part[:, reach:]
    d_buf[rows, :] = (dq_buf[...] * size**-0.5).astype(bf16)

    @pl.when(head == HEADS - 1)
    def _():
        x = x_ref[...]
        d_all = d_buf[...]
        small_ref[SELF_BIAS : SELF_BIAS + 1] = feature_sum(d_all[:width])
        small_ref[SELF_BIAS + 1 : SELF_BIAS + 2] = feature_sum(d_all[2 * width :])
        for part in range(3):
            grad_ref[(part + 1) * width : (part + 2) * width, :] = dot(
                x, d_all[part * width : (part + 1) * width], 0, 1
            ).astype(bf16)
        token_ref[...] = (
            par_ref[OMEGA : OMEGA + 1] * dz1_ref[...] + dot(d_all, qkv_w[...], 0, 1)
        ).astype(bf16)


def call(kernel, steps, ins, outs, scratch=(), flops=0, moved=0):
    def whole(shape):
        return pl.BlockSpec(shape, lambda i: (0,) * len(shape), pipeline_mode=pl.Buffered(1))

    def whole_out(shape):
        return pl.BlockSpec(shape, lambda i: (0,) * len(shape))

    arrays, in_specs, shapes, out_specs = [], [], [], []
    for item in ins:
        if isinstance(item, tuple):
            arrays.append(item[0])
            in_specs.append(pl.BlockSpec(item[1], item[2]))
        else:
            arrays.append(item)
            in_specs.append(whole(item.shape))
    for shape, dtype, *block in outs:
        shapes.append(jax.ShapeDtypeStruct(shape, dtype))
        out_specs.append(pl.BlockSpec(*block) if block else whole_out(shape))
    return pl.pallas_call(
        kernel,
        grid=(steps,),
        in_specs=in_specs,
        out_specs=out_specs,
        out_shape=shapes,
        scratch_shapes=list(scratch),
        compiler_params=pltpu.CompilerParams(
            dimension_semantics=("arbitrary",), vmem_limit_bytes=VMEM
        ),
        cost_estimate=pl.CostEstimate(flops=flops, bytes_accessed=moved, transcendentals=0),
    )(*arrays)


def local(sizes, *args):
    (
        tokens, memory, mem_mask, segment_ids, cotangent, self_qkv, self_bias, self_out,
        self_out_bias, cross_q, cross_kv, cross_bias, cross_out, cross_out_bias, ffn_in,
        ffn_in_bias, ffn_out, ffn_out_bias, omegas, ln_gains, ln_biases,
    ) = args
    length, width = tokens.shape[1:]
    hidden = ffn_in.shape[1]
    size = width // HEADS
    holders, part_rows = memory.shape[:2]
    count = holders * part_rows
    x = tokens.reshape(length, width)
    cot = cotangent.reshape(length, width)
    seg = segment_ids.reshape(1, length)
    small = jnp.concatenate(
        [
            value.reshape(-1, width)
            for value in (
                self_bias, self_out_bias, cross_bias, cross_out_bias, ffn_in_bias, ffn_out_bias,
                omegas, ln_gains, ln_biases,
            )
        ]
        + [jnp.zeros((SMALL - 20, width), bf16)],
        axis=0,
    ).astype(f32)
    mask_rows = jnp.pad(mem_mask.astype(bf16)[:, None, :], ((0, 0), (0, 0), (0, width - part_rows)))
    packed = jnp.concatenate(
        (memory, jnp.broadcast_to(mask_rows, (holders, PAD, width))), axis=1
    )
    m = lax.all_to_all(packed, "ctx", split_axis=0, concat_axis=0, tiled=True)

    blocks = length // BLOCK
    head_block = lambda *shape: ((1, *shape), lambda i: (i,) + (0,) * len(shape))
    score = 2 * length * length * width
    dense = 2 * length * width * width
    qkv, e_self, inv_self, o, z1, h1, q2 = call(
        self_forward_kernel,
        HEADS,
        [x, seg, small, self_qkv, self_out, cross_q],
        [
            ((3 * width, length), bf16),
            ((HEADS, blocks, BLOCK, (REACH + 1) * BLOCK), bf16,
             *head_block(blocks, BLOCK, (REACH + 1) * BLOCK)),
            ((HEADS, length), f32),
            ((width, length), bf16),
            ((length, width), f32),
            ((length, width), bf16),
            ((width, length), bf16),
        ],
        [pltpu.VMEM((PAD, length), bf16)] * 2,
        flops=4 * score + 5 * dense,
        moved=25 * 2**20,
    )
    kv, e_cross, inv_cross, o2, z2, h2 = call(
        cross_forward_kernel,
        HEADS,
        [m, q2, h1, small, cross_kv, cross_out],
        [
            ((2 * width, count), bf16),
            ((HEADS, count, length), bf16, *head_block(count, length)),
            ((HEADS, length), f32),
            ((width, length), bf16),
            ((length, width), f32),
            ((length, width), bf16),
        ],
        [pltpu.VMEM((PAD, count), bf16)],
        flops=8 * score + 3 * dense,
        moved=25 * 2**20,
    )
    rows = BLOCK
    row_block = ((rows, width), lambda i: (i, 0))
    activations, dz2, ffn_grad, small_ffn = call(
        ffn_kernel,
        length // rows,
        [h2, (h1, *row_block), (z2, *row_block), (cot, *row_block), small, ffn_in, ffn_out],
        [
            ((length, width), bf16, *row_block),
            ((length, width), f32, *row_block),
            ((2 * hidden, width), bf16),
            ((SMALL, width), f32),
        ],
        [
            pltpu.VMEM((length, hidden), bf16),
            pltpu.VMEM((rows, hidden), f32),
            pltpu.VMEM((length, width), bf16),
            pltpu.VMEM((length, hidden), bf16),
        ],
        flops=24 * dense,
        moved=16 * 2**20,
    )
    dz1, mem_part, cross_grad, small_cross = call(
        cross_backward_kernel,
        HEADS,
        [
            (e_cross, *head_block(count, length)), inv_cross, o2, q2, kv, dz2, h1, z1, x, m, small,
            cross_out, cross_q, cross_kv,
        ],
        [
            ((length, width), f32),
            ((holders, part_rows, width), bf16),
            ((4 * width, width), bf16),
            ((SMALL, width), f32),
        ],
        [
            pltpu.VMEM((width, length), bf16),
            pltpu.VMEM((width, length), bf16),
            pltpu.VMEM((2 * width, count), bf16),
        ],
        flops=16 * score + 8 * dense,
        moved=30 * 2**20,
    )
    memory_grad = lax.all_to_all(mem_part, "ctx", split_axis=0, concat_axis=0, tiled=True)
    token_grad, self_grad, small_self = call(
        self_backward_kernel,
        HEADS,
        [
            (e_self, *head_block(blocks, BLOCK, (REACH + 1) * BLOCK)), inv_self, o, qkv, dz1, x,
            small, self_out, self_qkv,
        ],
        [
            ((length, width), bf16),
            ((4 * width, width), bf16),
            ((SMALL, width), f32),
        ],
        [
            pltpu.VMEM((width, length), bf16),
            pltpu.VMEM((3 * width, length), bf16),
            pltpu.VMEM((size, length), f32),
        ],
        flops=8 * score + 8 * dense,
        moved=20 * 2**20,
    )
    small_grad = small_ffn + small_cross + small_self
    ffn_grad, cross_grad, self_grad = (
        reduce_rows(value, sizes) for value in (ffn_grad, cross_grad, self_grad)
    )
    for axis, bit in phases(sizes):
        small_grad = small_grad + swap(small_grad, axis, bit, sizes)

    def beside(value, begin, parts):
        value = value[begin * width : (begin + parts) * width].reshape(parts, width, width)
        return jnp.concatenate([value[i] for i in range(parts)], axis=1).astype(f32)

    rows_of = lambda begin, n: small_grad[begin : begin + n]
    return (
        activations.reshape(tokens.shape),
        token_grad.reshape(tokens.shape),
        memory_grad,
        beside(self_grad, 1, 3),
        rows_of(SELF_BIAS, 2),
        self_grad[:width].astype(f32),
        small_grad[SELF_OUT_BIAS],
        cross_grad[:width].astype(f32),
        beside(cross_grad, 2, 2),
        rows_of(CROSS_BIAS, 2),
        cross_grad[width : 2 * width].astype(f32),
        small_grad[CROSS_OUT_BIAS],
        beside(ffn_grad, hidden // width, hidden // width),
        rows_of(FFN_IN_BIAS, hidden // width).reshape(-1),
        ffn_grad[:hidden].astype(f32),
        small_grad[FFN_OUT_BIAS],
        rows_of(OMEGA, 3),
        rows_of(GAIN, 3),
        rows_of(SHIFT, 3),
    )


def phases(sizes):
    return [
        (axis, bit) for axis in ("dp", "ctx") for bit in range((sizes[axis] - 1).bit_length())
    ]


def swap(value, axis, bit, sizes):
    return lax.ppermute(value, axis, [(i, i ^ (1 << bit)) for i in range(sizes[axis])])


def reduce_rows(value, sizes):
    order = phases(sizes)
    for axis, bit in order:
        mine = (lax.axis_index(axis) >> bit) & 1
        halves = value.reshape(2, value.shape[0] // 2, value.shape[1])
        keep = lax.dynamic_index_in_dim(halves, mine, 0, keepdims=False)
        send = lax.dynamic_index_in_dim(halves, 1 - mine, 0, keepdims=False)
        value = (keep.astype(f32) + swap(send, axis, bit, sizes).astype(f32)).astype(bf16)
    for axis, bit in reversed(order):
        mine = (lax.axis_index(axis) >> bit) & 1
        other = swap(value, axis, bit, sizes)
        value = jnp.where(
            mine == 0,
            jnp.concatenate((value, other), axis=0),
            jnp.concatenate((other, value), axis=0),
        )
    return value


def solution(mesh):
    sizes = dict(mesh.shape)
    both = P(("dp", "ctx"), None, None)
    return jax.shard_map(
        functools.partial(local, sizes),
        mesh=mesh,
        in_specs=(both, P("dp", "ctx", None), P("dp", "ctx"), P(("dp", "ctx"), None), both)
        + (P(),) * 16,
        out_specs=(both, both, P("dp", "ctx", None)) + (P(),) * 16,
        check_vma=False,
    )
```

```python
import functools

import jax
import jax.numpy as jnp
from jax import lax
from jax.experimental import pallas as pl
from jax.experimental.pallas import tpu as pltpu
from jax.sharding import PartitionSpec as P

HEADS = 8
PAIR = 2
LOG2E = 1.4426950408889634
LN2 = 0.6931471805599453
UNSEEN = -1e30
BLOCK = 256
REACH = 2
PAD = 16
VMEM = 60 * 2**20
SMALL_VMEM = 24 * 2**20
bf16, f32 = jnp.bfloat16, jnp.float32

SELF_BIAS, SELF_OUT_BIAS, CROSS_BIAS, CROSS_OUT_BIAS = 0, 2, 3, 5
FFN_IN_BIAS, FFN_OUT_BIAS, OMEGA, GAIN, SHIFT, SMALL = 6, 10, 11, 14, 17, 24
LANES = 128


def dot(left, right, left_dim, right_dim):
    return lax.dot_general(
        left, right, (((left_dim,), (right_dim,)), ((), ())), preferred_element_type=f32
    )


def column(row):
    return jnp.transpose(jnp.broadcast_to(row, (8, row.shape[1])))[:, :1]


def row_sum(value):
    return jnp.sum(value.astype(f32), axis=0, keepdims=True)


def feature_sum(value):
    ones = jnp.ones((PAD, value.shape[1]), bf16)
    return dot(ones, value, 1, 1)[:1]


def normalize(value):
    centered = value - jnp.mean(value, axis=-1, keepdims=True)
    spread = jnp.mean(centered * centered, axis=-1, keepdims=True)
    inverse = lax.rsqrt(spread + 1e-05)
    return centered * inverse, inverse


def normalize_back(grad, gain, normal, inverse):
    scaled = grad * gain
    mean = jnp.mean(scaled, axis=-1, keepdims=True)
    slope = jnp.mean(scaled * normal, axis=-1, keepdims=True)
    return (scaled - mean - normal * slope) * inverse


def with_ones(rows):
    return jnp.concatenate((rows, jnp.ones((PAD, rows.shape[1]), bf16)), axis=0)


def start(copies):
    for copy in copies:
        copy.start()


def wait(copies):
    for copy in copies:
        copy.wait()


def self_forward_kernel(
    digit_ref, x_ref, seg_ref, par_ref, qkv_w, out_hbm, cross_hbm,
    qkv_hbm, e_ref, inv_ref, o_hbm, z_hbm, h_hbm, q_hbm,
    qkv_ref, o_ref, z_ref, h_ref, q_ref, out_w, cross_w, q_mask, k_mask, sems,
):
    step = pl.program_id(0)
    last = pl.num_programs(0) - 1
    length, width = x_ref.shape
    size = width // HEADS
    scale = size**-0.5 * LOG2E
    copy = pltpu.make_async_copy
    loads = [copy(out_hbm, out_w, sems.at[0]), copy(cross_hbm, cross_w, sems.at[1])]
    projected = copy(qkv_ref, qkv_hbm, sems.at[2])

    @pl.when(step == 0)
    def _():
        start(loads)
        x = x_ref[...]
        for part, row in ((0, 0), (1, None), (2, 1)):
            columns = slice(part * width, (part + 1) * width)
            value = dot(qkv_w[:, columns], x, 0, 1)
            if row is not None:
                value = value + column(par_ref[SELF_BIAS + row : SELF_BIAS + row + 1])
            if part == 0:
                value = value * scale
            qkv_ref[columns, :] = value.astype(bf16)
        projected.start()
        same = lax.broadcasted_iota(jnp.int32, (PAD, length), 0) == seg_ref[...]
        q_mask[...] = jnp.where(same, 1.0, 0.0).astype(bf16)
        k_mask[...] = jnp.where(same, 0.0, UNSEEN).astype(bf16)

    causal = lax.broadcasted_iota(jnp.int32, (BLOCK, BLOCK), 0) <= lax.broadcasted_iota(
        jnp.int32, (BLOCK, BLOCK), 1
    )
    blocks = length // BLOCK
    for one in range(PAIR):
        head = step * PAIR + one
        base = pl.multiple_of(head * size, size)
        q = jnp.concatenate((qkv_ref[pl.ds(base, size), :], q_mask[...]), axis=0)
        k = jnp.concatenate((qkv_ref[pl.ds(width + base, size), :], k_mask[...]), axis=0)
        v = with_ones(qkv_ref[pl.ds(2 * width + base, size), :])
        scores, tops, mixed = [], [None] * blocks, [None] * blocks
        for i in range(blocks):
            s = dot(k[:, i * BLOCK : (i + 1) * BLOCK], q[:, i * BLOCK : (i + REACH + 1) * BLOCK], 0, 0)
            diagonal = jnp.where(causal, s[:, :BLOCK], UNSEEN)
            if s.shape[1] > BLOCK:
                diagonal = jnp.concatenate((diagonal, s[:, BLOCK:]), axis=1)
            scores.append(diagonal)
            top = jnp.max(diagonal, axis=0, keepdims=True)
            for b in range(s.shape[1] // BLOCK):
                part = top[:, b * BLOCK : (b + 1) * BLOCK]
                old = tops[i + b]
                tops[i + b] = part if old is None else jnp.maximum(old, part)
        for i, s in enumerate(scores):
            several = s.shape[1] // BLOCK
            weights = jnp.exp2(s - jnp.concatenate(tops[i : i + several], axis=1)).astype(bf16)
            e_ref[one, i, :, : several * BLOCK] = weights
            part = dot(v[:, i * BLOCK : (i + 1) * BLOCK], weights, 1, 0)
            for b in range(several):
                piece = part[:, b * BLOCK : (b + 1) * BLOCK]
                mixed[i + b] = piece if mixed[i + b] is None else mixed[i + b] + piece
        for j, value in enumerate(mixed):
            mine = slice(j * BLOCK, (j + 1) * BLOCK)
            inverse = 1.0 / value[size : size + 1]
            o_ref[pl.ds(base, size), mine] = (value[:size] * inverse).astype(bf16)
            inv_ref[pl.ds(head, 1), mine] = inverse

    @pl.when(step == last)
    def _():
        outs = [
            copy(o_ref, o_hbm, sems.at[3]),
            copy(z_ref, z_hbm, sems.at[4]),
            copy(h_ref, h_hbm, sems.at[5]),
            copy(q_ref, q_hbm, sems.at[6]),
        ]
        outs[0].start()
        wait(loads)
        z = (
            par_ref[OMEGA : OMEGA + 1] * x_ref[...].astype(f32)
            + dot(o_ref[...], out_w[...], 0, 0)
            + par_ref[SELF_OUT_BIAS : SELF_OUT_BIAS + 1]
        )
        z_ref[...] = z
        outs[1].start()
        normal, _ = normalize(z)
        h = (normal * par_ref[GAIN : GAIN + 1] + par_ref[SHIFT : SHIFT + 1]).astype(bf16)
        h_ref[...] = h
        outs[2].start()
        value = dot(cross_w[...], h, 0, 1) + column(par_ref[CROSS_BIAS : CROSS_BIAS + 1])
        q_ref[...] = (value * scale).astype(bf16)
        outs[3].start()
        wait([projected, *outs])


def cross_forward_kernel(
    digit_ref, m_ref, q_ref, par_ref, kv_w, h1_hbm, out_hbm,
    kv_hbm, e_ref, inv_ref, o_hbm, z_hbm, h_hbm,
    kv_ref, o_ref, z_ref, h_ref, h1_ref, out_w, k_mask, sems,
):
    step = pl.program_id(0)
    last = pl.num_programs(0) - 1
    length, width = h1_ref.shape
    size = width // HEADS
    holders, part_rows = m_ref.shape[0], m_ref.shape[1] - PAD
    copy = pltpu.make_async_copy
    loads = [copy(h1_hbm, h1_ref, sems.at[0]), copy(out_hbm, out_w, sems.at[1])]
    projected = copy(kv_ref, kv_hbm, sems.at[2])

    @pl.when(step == 0)
    def _():
        start(loads)
        shift = column(par_ref[CROSS_BIAS + 1 : CROSS_BIAS + 2])
        first = lax.broadcasted_iota(jnp.int32, (PAD, part_rows), 0) == 0
        for b in range(holders):
            columns = slice(b * part_rows, (b + 1) * part_rows)
            m = m_ref[b, :part_rows, :]
            kv_ref[:width, columns] = dot(kv_w[:, :width], m, 0, 1).astype(bf16)
            kv_ref[width:, columns] = (dot(kv_w[:, width:], m, 0, 1) + shift).astype(bf16)
            seen = m_ref[b, part_rows:, :part_rows].astype(f32) > 0.5
            k_mask[:, columns] = jnp.where(first & ~seen, UNSEEN, 0.0).astype(bf16)
        projected.start()

    for one in range(PAIR):
        head = step * PAIR + one
        base = pl.multiple_of(head * size, size)
        q = with_ones(q_ref[one * size : (one + 1) * size, :])
        k = jnp.concatenate((kv_ref[pl.ds(base, size), :], k_mask[...]), axis=0)
        v = with_ones(kv_ref[pl.ds(width + base, size), :])
        scores = dot(k, q, 0, 0)
        weights = jnp.exp2(scores - jnp.max(scores, axis=0, keepdims=True)).astype(bf16)
        e_ref[one] = weights
        mixed = dot(v, weights, 1, 0)
        inverse = 1.0 / mixed[size : size + 1]
        o_ref[pl.ds(base, size), :] = (mixed[:size] * inverse).astype(bf16)
        inv_ref[pl.ds(head, 1), :] = inverse

    @pl.when(step == last)
    def _():
        outs = [
            copy(o_ref, o_hbm, sems.at[3]),
            copy(z_ref, z_hbm, sems.at[4]),
            copy(h_ref, h_hbm, sems.at[5]),
        ]
        outs[0].start()
        wait(loads)
        z = (
            par_ref[OMEGA + 1 : OMEGA + 2] * h1_ref[...].astype(f32)
            + dot(o_ref[...], out_w[...], 0, 0)
            + par_ref[CROSS_OUT_BIAS : CROSS_OUT_BIAS + 1]
        )
        z_ref[...] = z
        outs[1].start()
        normal, _ = normalize(z)
        h_ref[...] = (
            normal * par_ref[GAIN + 1 : GAIN + 2] + par_ref[SHIFT + 1 : SHIFT + 2]
        ).astype(bf16)
        outs[2].start()
        wait([projected, *outs])


def ffn_kernel(
    digit_ref, h2_ref, h1_ref, z2_ref, cot_ref, par_ref, in_w, out_hbm,
    act_ref, dz_ref, grad_hbm, small_ref,
    h_buf, g_buf, slope_buf, e_buf, eu_buf, grad_buf, out_w, sems,
):
    step = pl.program_id(0)
    rows, width = cot_ref.shape
    hidden = in_w.shape[1]
    chunks = hidden // width
    begin = pl.multiple_of(step * rows, rows)
    mine = pl.ds(begin, rows)
    load = pltpu.make_async_copy(out_hbm, out_w, sems.at[2 * chunks])

    @pl.when(step == 0)
    def _():
        load.start()
        small_ref[...] = jnp.zeros_like(small_ref)

    def add(row, value):
        small_ref[row : row + 1] += row_sum(value)

    h2 = h2_ref[...]
    h_buf[mine, :] = h2
    h2_wide = h2.astype(f32)
    for c in range(chunks):
        columns = slice(c * width, (c + 1) * width)
        u = dot(h2, in_w[:, columns], 1, 0) + par_ref[FFN_IN_BIAS + c : FFN_IN_BIAS + c + 1]
        rate = 0.7978845608028654
        square = u * u
        t = jnp.tanh(u * (rate + (rate * 0.044715) * square))
        half = 0.5 + 0.5 * t
        g_buf[mine, columns] = (u * half).astype(bf16)
        slope_buf[:, columns] = half + (0.5 * u) * (1.0 - t * t) * (
            rate + (3 * rate * 0.044715) * square
        )

    @pl.when(step == 0)
    def _():
        load.wait()

    z3 = (
        par_ref[OMEGA + 2 : OMEGA + 3] * h2_wide
        + dot(g_buf[mine, :], out_w[...], 1, 0)
        + par_ref[FFN_OUT_BIAS : FFN_OUT_BIAS + 1]
    )
    normal, inverse = normalize(z3)
    gain = par_ref[GAIN + 2 : GAIN + 3]
    act_ref[...] = (normal * gain + par_ref[SHIFT + 2 : SHIFT + 3]).astype(bf16)
    dy = cot_ref[...].astype(f32)
    add(GAIN + 2, dy * normal)
    add(SHIFT + 2, dy)
    dz3 = normalize_back(dy, gain, normal, inverse)
    add(OMEGA + 2, dz3 * h2_wide)
    e3 = dz3.astype(bf16)
    e_buf[mine, :] = e3
    add(FFN_OUT_BIAS, e3)
    for c in range(chunks):
        columns = slice(c * width, (c + 1) * width)
        eu = (dot(e3, out_w[columns, :], 1, 1) * slope_buf[:, columns]).astype(bf16)
        eu_buf[mine, columns] = eu
        add(FFN_IN_BIAS + c, eu)
    dh2 = par_ref[OMEGA + 2 : OMEGA + 3] * dz3 + dot(eu_buf[mine, :], in_w[...], 1, 1)
    normal, inverse = normalize(z2_ref[...])
    add(GAIN + 1, dh2 * normal)
    add(SHIFT + 1, dh2)
    dz2 = normalize_back(dh2, par_ref[GAIN + 1 : GAIN + 2], normal, inverse)
    add(OMEGA + 1, dz2 * h1_ref[...].astype(f32))
    add(CROSS_OUT_BIAS, dz2.astype(bf16))
    dz_ref[...] = dz2

    @pl.when(step == pl.num_programs(0) - 1)
    def _():
        outs = []
        for c in range(2 * chunks):
            columns = slice(c % chunks * width, (c % chunks + 1) * width)
            place = slice(c * width, (c + 1) * width)
            if c < chunks:
                value = dot(g_buf[:, columns], e_buf[...], 0, 0)
            else:
                value = dot(h_buf[...], eu_buf[:, columns], 0, 0)
            grad_buf[place, :] = value.astype(bf16)
            outs.append(
                pltpu.make_async_copy(grad_buf.at[place], grad_hbm.at[place], sems.at[c])
            )
            outs[-1].start()
        wait(outs)


def back_heads(do_ref, out_w, e, inv_ref):
    value = dot(out_w[...], e, 1, 1)
    size = value.shape[0] // HEADS
    for i in range(HEADS):
        rows = slice(i * size, (i + 1) * size)
        do_ref[rows, :] = (value[rows] * inv_ref[i : i + 1]).astype(bf16)


def back_head(do_rows, o_rows):
    length = do_rows.shape[1]
    delta = jnp.sum(do_rows.astype(f32) * o_rows.astype(f32), axis=0, keepdims=True)
    high = delta.astype(bf16).astype(f32)
    row = lax.broadcasted_iota(jnp.int32, (PAD, length), 0)
    extra = jnp.where(row == 0, -high, jnp.where(row == 1, high - delta, 0.0))
    return jnp.concatenate((do_rows, extra.astype(bf16)), axis=0)


def cross_backward_kernel(
    digit_ref, e_ref, inv_ref, o_ref, q_ref, k_ref, v_ref, dz2_ref, par_ref, old_ref, out_w,
    z1_hbm, h1_hbm, x_hbm, m_hbm, qw_hbm,
    dz1_hbm, dkv_hbm, keep_hbm, send_hbm, small_ref,
    z1_ref, h1_ref, x_ref, m_ref, q_w, do_buf, o_buf, dq_buf, dkv_buf, dz_buf, grad_buf, sems,
):
    step = pl.program_id(0)
    last = pl.num_programs(0) - 1
    length, width = x_ref.shape
    size = width // HEADS
    count = k_ref.shape[1]
    pair = PAIR * size
    holders, part_rows = m_ref.shape[0], m_ref.shape[1] - PAD
    copy = pltpu.make_async_copy
    loads = [
        copy(source, target, sems.at[i])
        for i, (source, target) in enumerate(
            ((z1_hbm, z1_ref), (h1_hbm, h1_ref), (x_hbm, x_ref), (m_hbm, m_ref), (qw_hbm, q_w))
        )
    ]
    first = len(loads)

    def part_out(at, which):
        rows = pl.ds(pl.multiple_of(which * width + at * pair, pair), pair)
        return copy(dkv_buf.at[rows], dkv_hbm.at[rows], sems.at[first + 2 * at + which])

    @pl.when(step == 0)
    def _():
        start(loads)
        small_ref[...] = old_ref[...]
        back_heads(do_buf, out_w, dz2_ref[...].astype(bf16), inv_ref)

    base = pl.multiple_of(step * pair, pair)
    o_buf[pl.ds(base, pair), :] = o_ref[...]
    heads = []
    for one in range(PAIR):
        here = slice(one * size, (one + 1) * size)
        heads.append(
            (
                back_head(do_buf[pl.ds(base + one * size, size), :], o_ref[here, :]),
                q_ref[here, :],
                k_ref[here, :],
                with_ones(v_ref[here, :]),
            )
        )
    dq = [None] * PAIR
    for i in range(count // BLOCK):
        mine = slice(i * BLOCK, (i + 1) * BLOCK)
        for one, (do, q, k, v) in enumerate(heads):
            weights = e_ref[one, mine, :]
            ds = (weights.astype(f32) * dot(v[:, mine], do, 0, 0)).astype(bf16)
            begin = base + one * size
            dkv_buf[pl.ds(width + begin, size), mine] = dot(do[:size], weights, 1, 1).astype(bf16)
            dkv_buf[pl.ds(begin, size), mine] = (dot(q, ds, 1, 1) * LN2).astype(bf16)
            part = dot(k[:, mine], ds, 1, 0)
            dq[one] = part if i == 0 else dq[one] + part
    for one in range(PAIR):
        dq_buf[pl.ds(base + one * size, size), :] = (dq[one] * size**-0.5).astype(bf16)
    start([part_out(step, 0), part_out(step, 1)])

    @pl.when(step == last)
    def _():
        wait(loads)
        after = first + 2 * (HEADS // PAIR)
        dq_all = dq_buf[...]
        dh1 = par_ref[OMEGA + 1 : OMEGA + 2] * dz2_ref[...] + dot(dq_all, q_w[...], 0, 1)
        normal, inverse = normalize(z1_ref[...])
        small_ref[GAIN : GAIN + 1] = row_sum(dh1 * normal)
        small_ref[SHIFT : SHIFT + 1] = row_sum(dh1)
        dz1 = normalize_back(dh1, par_ref[GAIN : GAIN + 1], normal, inverse)
        small_ref[OMEGA : OMEGA + 1] = row_sum(dz1 * x_ref[...].astype(f32))
        small_ref[SELF_OUT_BIAS : SELF_OUT_BIAS + 1] = row_sum(dz1.astype(bf16))
        dz_buf[...] = dz1
        outs = [copy(dz_buf, dz1_hbm, sems.at[after])]
        outs[0].start()
        small_ref[CROSS_BIAS : CROSS_BIAS + 1] = feature_sum(dq_all)
        small_ref[CROSS_BIAS + 1 : CROSS_BIAS + 2] = feature_sum(dkv_buf[width:, :])
        grad_buf[:, :width] = dot(h1_ref[...], dq_all, 0, 1).astype(bf16)
        grad_buf[:, width : 2 * width] = dot(
            o_buf[...], dz2_ref[...].astype(bf16), 1, 0
        ).astype(bf16)
        key_grad = value_grad = None
        for b in range(holders):
            columns = slice(b * part_rows, (b + 1) * part_rows)
            m = m_ref[b, :part_rows, :]
            k_part = dot(m, dkv_buf[:width, columns], 0, 1)
            v_part = dot(m, dkv_buf[width:, columns], 0, 1)
            key_grad = k_part if b == 0 else key_grad + k_part
            value_grad = v_part if b == 0 else value_grad + v_part
        grad_buf[:, 2 * width : 3 * width] = key_grad.astype(bf16)
        grad_buf[:, 3 * width :] = value_grad.astype(bf16)
        outs += halves(digit_ref, grad_buf, keep_hbm, send_hbm, sems, after + 1)
        wait(outs)
        wait([part_out(at, which) for at in range(HEADS // PAIR) for which in range(2)])


def halves(digit_ref, grad_buf, keep_hbm, send_hbm, sems, at):
    rows = grad_buf.shape[0] // 2
    result = []
    for i, target in enumerate((keep_hbm, send_hbm)):
        source = grad_buf.at[pl.ds(pl.multiple_of((digit_ref[0] ^ i) * rows, rows), rows)]
        result.append(pltpu.make_async_copy(source, target, sems.at[at + i]))
        result[-1].start()
    return result


def self_backward_kernel(
    digit_ref, e_ref, inv_ref, o_ref, q_ref, k_ref, v_ref, dz1_ref, out_w,
    dq_ref, dk_ref, dv_ref, do_buf,
):
    step = pl.program_id(0)
    pair, length = q_ref.shape
    size = pair // PAIR
    blocks = length // BLOCK

    @pl.when(step == 0)
    def _():
        back_heads(do_buf, out_w, dz1_ref[...].astype(bf16), inv_ref)

    base = pl.multiple_of(step * pair, pair)
    for one in range(PAIR):
        here = slice(one * size, (one + 1) * size)
        do = back_head(do_buf[pl.ds(base + one * size, size), :], o_ref[here, :])
        q, k, v = q_ref[here, :], k_ref[here, :], with_ones(v_ref[here, :])
        dq = [None] * blocks
        for i in range(blocks):
            mine = slice(i * BLOCK, (i + 1) * BLOCK)
            several = min(blocks - i, REACH + 1)
            seen = slice(i * BLOCK, (i + several) * BLOCK)
            weights = e_ref[one, i, :, : several * BLOCK]
            ds = (weights.astype(f32) * dot(v[:, mine], do[:, seen], 0, 0)).astype(bf16)
            dv_ref[here, mine] = dot(do[:size, seen], weights, 1, 1).astype(bf16)
            dk_ref[here, mine] = (dot(q[:, seen], ds, 1, 1) * LN2).astype(bf16)
            part = dot(k[:, mine], ds, 1, 0)
            for b in range(several):
                piece = part[:, b * BLOCK : (b + 1) * BLOCK]
                dq[i + b] = piece if dq[i + b] is None else dq[i + b] + piece
        for j in range(blocks):
            dq_ref[here, j * BLOCK : (j + 1) * BLOCK] = (dq[j] * size**-0.5).astype(bf16)


def self_weights_kernel(
    digit_ref, old_ref, x_hbm, dq_hbm, dk_hbm, dv_hbm, dz1_hbm, o_hbm,
    keep_hbm, send_hbm,
    x_ref, dq_ref, dk_ref, dv_ref, dz1_ref, o_ref, grad_buf, sems,
):
    width = x_ref.shape[1]
    refs = (x_ref, dq_ref, dk_ref, dv_ref, dz1_ref, o_ref)
    loads = [
        pltpu.make_async_copy(source, target, sems.at[i])
        for i, (source, target) in enumerate(
            zip((x_hbm, dq_hbm, dk_hbm, dv_hbm, dz1_hbm, o_hbm), refs)
        )
    ]
    start(loads)
    loads[0].wait()
    sums = []
    for part, ref in enumerate((dq_ref, dk_ref, dv_ref)):
        loads[1 + part].wait()
        d = ref[...]
        grad_buf[:, (part + 1) * width : (part + 2) * width] = dot(x_ref[...], d, 0, 1).astype(bf16)
        sums.append(feature_sum(d) if part != 1 else None)
    row = lax.broadcasted_iota(jnp.int32, old_ref.shape, 0)
    small = jnp.where(row == SELF_BIAS, sums[0], old_ref[...])
    small = jnp.where(row == SELF_BIAS + 1, sums[2], small)
    small = jnp.concatenate((small, jnp.zeros((LANES - SMALL, width), f32)), axis=0)
    grad_buf[:, 4 * width :] = jnp.transpose(small).astype(bf16)
    wait(loads[4:])
    grad_buf[:, :width] = dot(o_ref[...], dz1_ref[...].astype(bf16), 1, 0).astype(bf16)
    wait(halves(digit_ref, grad_buf, keep_hbm, send_hbm, sems, len(loads)))


def memory_kernel(digit_ref, dkv_ref, kv_w, mem_ref):
    mem_ref[0] = dot(dkv_ref[...], kv_w[...], 0, 1).astype(bf16)


def token_kernel(digit_ref, dq_ref, dk_ref, dv_ref, dz1_ref, par_ref, qkv_w, token_ref):
    width = dz1_ref.shape[1]
    total = par_ref[OMEGA : OMEGA + 1] * dz1_ref[...]
    for part, ref in enumerate((dq_ref, dk_ref, dv_ref)):
        total = total + dot(ref[...], qkv_w[:, part * width : (part + 1) * width], 0, 1)
    token_ref[...] = total.astype(bf16)


def tree_sum(values):
    while len(values) > 1:
        values = [a + b for a, b in zip(values[::2], values[1::2])]
    return values[0]


def combine_kernel(stage, outs, groups, *refs):
    sources, results = refs[1 : 1 + sum(groups)], refs[1 + sum(groups) :]
    rows = results[0].shape[0]
    for d in range(outs):
        begin = 0 if outs == 1 else pl.multiple_of((refs[0][stage] ^ d) * rows, rows)
        left, column = list(sources), 0
        for count in groups:
            group, left = left[:count], left[count:]
            total = tree_sum([ref[pl.ds(begin, rows), :].astype(f32) for ref in group])
            width = total.shape[1]
            results[d][:, column : column + width] = total.astype(bf16)
            column += width


def place_kernel(stage, ins, *refs):
    digit, sources, result = refs[0][stage], refs[1 : 1 + ins], refs[1 + ins]
    rows = sources[0].shape[0]
    for d in range(ins):
        result[pl.ds(pl.multiple_of((digit ^ d) * rows, rows), rows), :] = sources[d][...]


def finish_kernel(
    digit_ref, mine_ref, other_ref, cross_q, cross_out, cross_kv, self_out, self_qkv,
    self_bias, self_out_bias, cross_bias, cross_out_bias, in_bias, out_bias, omega, gain, shift,
):
    rows, width = mine_ref.shape[0], cross_q.shape[1]
    for i in range(2):

        @pl.when(digit_ref[0] == i)
        def _(i=i):
            for half, source in ((i, mine_ref), (1 - i, other_ref)):
                here = slice(half * rows, (half + 1) * rows)
                begin = 0
                for target in (cross_q, cross_out, cross_kv, self_out, self_qkv):
                    count = target.shape[1]
                    target[here, :] = source[:, begin : begin + count].astype(f32)
                    begin += count
                part = jnp.transpose(source[:, begin:].astype(f32))
                begin = 0
                for target in (
                    self_bias, self_out_bias, cross_bias, cross_out_bias, in_bias, out_bias,
                    omega, gain, shift,
                ):
                    count = target.shape[0]
                    target[:, here] = part[begin : begin + count]
                    begin += count


def copy_kernel(digit_ref, source, target):
    target[...] = source[...]


def ffn_finish_kernel(digit_ref, out_sum, in_sum, out_ref, in_ref):
    out_ref[...] = out_sum[...].astype(f32)
    in_ref[...] = in_sum[...].astype(f32)


class Order:
    def __init__(self, digits):
        self.digits = digits

    def after(self, value):
        return lax.optimization_barrier((value, self.digits))[0]

    def through(self, value):
        value, self.digits = lax.optimization_barrier((value, self.digits))
        return value

    def __call__(self, kernel, steps, ins, outs, scratch=(), vmem=VMEM):
        def whole(shape):
            return pl.BlockSpec(shape, lambda i: (0,) * len(shape), pipeline_mode=pl.Buffered(1))

        arrays, in_specs, shapes, out_specs = (
            [self.digits], [pl.BlockSpec(memory_space=pltpu.SMEM)], [], []
        )
        anywhere = pl.BlockSpec(memory_space=pl.ANY)
        for item in ins:
            if isinstance(item, tuple):
                arrays.append(item[0])
                in_specs.append(pl.BlockSpec(*item[1:]) if item[1:] else anywhere)
            else:
                arrays.append(item)
                in_specs.append(whole(item.shape))
        for shape, dtype, *block in outs:
            shapes.append(jax.ShapeDtypeStruct(shape, dtype))
            if block == [None]:
                out_specs.append(anywhere)
            elif block:
                out_specs.append(pl.BlockSpec(*block))
            else:
                out_specs.append(pl.BlockSpec(shape, lambda i, n=len(shape): (0,) * n))
        result = pl.pallas_call(
            kernel,
            grid=(steps,),
            in_specs=in_specs,
            out_specs=out_specs,
            out_shape=shapes,
            scratch_shapes=list(scratch),
            compiler_params=pltpu.CompilerParams(
                dimension_semantics=("arbitrary",), vmem_limit_bytes=vmem
            ),
        )(*arrays)
        self.digits = lax.optimization_barrier((self.digits, result[0]))[0]
        return result


def stages_of(sizes):
    result = []
    for axis in ("dp", "ctx"):
        stride = 1
        while stride < sizes[axis]:
            left = sizes[axis] // stride
            count = 2 if (axis == "dp" and stride == 1) or left % 4 else 4
            result.append((axis, stride, count))
            stride *= count
    return result


class Sum:
    def __init__(self, order, stages, sizes, pieces):
        self.order, self.stages, self.sizes = order, stages, sizes
        self.stage, self.spread, self.pieces, self.others = 0, [], pieces, []
        self.send(0)

    def send(self, stage):
        axis, stride, count = self.stages[stage]
        pieces = self.pieces if len(self.pieces) > 1 else self.pieces * count
        self.got = [
            lax.ppermute(
                pieces[d], axis, [(i, i ^ (d * stride)) for i in range(self.sizes[axis])]
            )
            for d in range(1, count)
        ]

    def settle(self):
        self.spread.append(self.stage)
        self.stage += 1
        group = [self.pieces[0], *self.got]
        self.pieces, self.got = self.order(
            functools.partial(combine_kernel, self.stage, 1, [len(group)]), 1, group,
            [(group[0].shape, bf16)], vmem=SMALL_VMEM,
        ), []

    def join(self, other):
        self.others.append(other)

    def step(self):
        groups = [[one.pieces[0], *one.got] for one in (*self.others, self)]
        rows = groups[0][0].shape[0]
        width = sum(group[0].shape[1] for group in groups)
        outs = 1
        if self.stage < len(self.stages):
            if len(self.pieces) > 1:
                self.spread.append(self.stage)
            self.stage += 1
            if self.stage < len(self.stages):
                count = self.stages[self.stage][2]
                outs = count if rows % (PAD * count) == 0 else 1
            kernel = functools.partial(
                combine_kernel, self.stage, outs, [len(group) for group in groups]
            )
            rows //= outs
        else:
            stage = self.spread.pop()
            kernel = functools.partial(place_kernel, stage, len(groups[0]))
            rows *= len(groups[0])
        self.others = []
        self.pieces = self.order(
            kernel, 1, sum(groups, []), [((rows, width), bf16)] * outs, vmem=SMALL_VMEM
        )
        self.send(self.stage if self.stage < len(self.stages) else self.spread[-1])

    @property
    def last(self):
        return self.stage == len(self.stages) and len(self.spread) == 1


def local(sizes, *args):
    (
        tokens, memory, mem_mask, segment_ids, cotangent, self_qkv, self_bias, self_out,
        self_out_bias, cross_q, cross_kv, cross_bias, cross_out, cross_out_bias, ffn_in,
        ffn_in_bias, ffn_out, ffn_out_bias, omegas, ln_gains, ln_biases,
    ) = args
    length, width = tokens.shape[1:]
    hidden = ffn_in.shape[1]
    size = width // HEADS
    holders, part_rows = memory.shape[:2]
    count = holders * part_rows
    x = tokens.reshape(length, width)
    cot = cotangent.reshape(length, width)
    seg = segment_ids.reshape(1, length)
    small = jnp.concatenate(
        [
            value.reshape(-1, width)
            for value in (
                self_bias, self_out_bias, cross_bias, cross_out_bias, ffn_in_bias, ffn_out_bias,
                omegas, ln_gains, ln_biases,
            )
        ]
        + [jnp.zeros((SMALL - 20, width), bf16)],
        axis=0,
    ).astype(f32)
    mask_rows = jnp.pad(mem_mask.astype(bf16)[:, None, :], ((0, 0), (0, 0), (0, width - part_rows)))
    packed = jnp.concatenate(
        (memory, jnp.broadcast_to(mask_rows, (holders, PAD, width))), axis=1
    )
    m = lax.all_to_all(packed, "ctx", split_axis=0, concat_axis=0, tiled=True)
    stages = stages_of(sizes)
    digits = [(lax.axis_index(axis) // stride) % several for axis, stride, several in stages]
    first_ctx = [axis for axis, _, _ in stages].index("ctx")
    order = Order(jnp.stack(digits).astype(jnp.int32))

    blocks = length // BLOCK
    reach = (REACH + 1) * BLOCK

    pairs, pair = HEADS // PAIR, PAIR * size

    def scores_in(array):
        shape = (PAIR, *array.shape[1:])
        return (array, shape, lambda i: (i,) + (0,) * (len(shape) - 1))

    def scores_out(*shape):
        return ((HEADS, *shape), bf16, (PAIR, *shape), lambda i: (i,) + (0,) * len(shape))

    def pair_in(array, part=0):
        return (array, (pair, array.shape[1]), lambda i: (part * pairs + i, 0))

    def vmem(*shape, dtype=bf16):
        return pltpu.VMEM(shape, dtype)

    dma = pltpu.SemaphoreType.DMA
    tall, wide = (width, length), (length, width)
    qkv, e_self, inv_self, o, z1, h1, q2 = order(
        self_forward_kernel,
        pairs,
        [x, seg, small, self_qkv, (self_out,), (cross_q,)],
        [
            ((3 * width, length), bf16, None),
            scores_out(blocks, BLOCK, reach),
            ((HEADS, length), f32),
            (tall, bf16, None),
            (wide, f32, None),
            (wide, bf16, None),
            (tall, bf16, None),
        ],
        [
            vmem(3 * width, length), vmem(*tall), vmem(*wide, dtype=f32), vmem(*wide), vmem(*tall),
            vmem(width, width), vmem(width, width), vmem(PAD, length), vmem(PAD, length), dma((7,)),
        ],
    )
    kv, e_cross, inv_cross, o2, z2, h2 = order(
        cross_forward_kernel,
        pairs,
        [m, pair_in(q2), small, cross_kv, (h1,), (cross_out,)],
        [
            ((2 * width, count), bf16, None),
            scores_out(count, length),
            ((HEADS, length), f32),
            (tall, bf16, None),
            (wide, f32, None),
            (wide, bf16, None),
        ],
        [
            vmem(2 * width, count), vmem(*tall), vmem(*wide, dtype=f32), vmem(*wide), vmem(*wide),
            vmem(width, width), vmem(PAD, count), dma((6,)),
        ],
    )
    rows = BLOCK
    chunks = hidden // width
    row_block = ((rows, width), lambda i: (i, 0))
    activations, dz2, ffn_grad, small_grad = order(
        ffn_kernel,
        length // rows,
        [
            (h2, *row_block), (h1, *row_block), (z2, *row_block), (cot, *row_block), small, ffn_in,
            (ffn_out,),
        ],
        [
            (wide, bf16, *row_block),
            (wide, f32, *row_block),
            ((2 * hidden, width), bf16, None),
            ((SMALL, width), f32),
        ],
        [
            vmem(*wide), vmem(length, hidden), vmem(rows, hidden, dtype=f32), vmem(*wide),
            vmem(length, hidden), vmem(2 * hidden, width), vmem(hidden, width),
            dma((2 * chunks + 1,)),
        ],
    )
    ffn_part = lax.psum_scatter(ffn_grad, "dp", scatter_dimension=0, tiled=True)
    dz1, dkv, keep, send, small_grad = order(
        cross_backward_kernel,
        pairs,
        [
            scores_in(e_cross), inv_cross, pair_in(o2), pair_in(q2), pair_in(kv), pair_in(kv, 1),
            dz2, small, small_grad, cross_out, (z1,), (h1,), (x,), (m,), (cross_q,),
        ],
        [
            (wide, f32, None),
            ((2 * width, count), bf16, None),
            ((width // 2, 4 * width), bf16, None),
            ((width // 2, 4 * width), bf16, None),
            ((SMALL, width), f32),
        ],
        [
            vmem(*wide, dtype=f32), vmem(*wide), vmem(*wide), vmem(*m.shape), vmem(width, width),
            vmem(*tall), vmem(*tall), vmem(*tall), vmem(2 * width, count), vmem(*wide, dtype=f32),
            vmem(width, 4 * width), dma((5 + 2 * pairs + 3,)),
        ],
    )
    cross_sum = Sum(order, stages, sizes, [keep, send])
    (mem_part,) = order(
        memory_kernel,
        holders,
        [(dkv, (2 * width, part_rows), lambda i: (0, i)), cross_kv],
        [((holders, part_rows, width), bf16, (1, part_rows, width), lambda i: (i, 0, 0))],
    )
    memory_grad = lax.all_to_all(mem_part, "ctx", split_axis=0, concat_axis=0, tiled=True)
    cross_sum.step()
    total = 4 * width + LANES
    pair_out = (tall, bf16, (pair, length), lambda i: (i, 0))
    dq, dk, dv = order(
        self_backward_kernel,
        pairs,
        [
            scores_in(e_self), inv_self, pair_in(o), pair_in(qkv), pair_in(qkv, 1), pair_in(qkv, 2),
            dz1, self_out,
        ],
        [pair_out] * 3,
        [vmem(*tall)],
    )
    for _ in range(first_ctx - 2):
        cross_sum.step()
    cross_sum.settle()
    keep, send = order(
        self_weights_kernel,
        1,
        [small_grad, (x,), (dq,), (dk,), (dv,), (dz1,), (o,)],
        [((width // 2, total), bf16, None)] * 2,
        [
            vmem(*wide), vmem(*tall), vmem(*tall), vmem(*tall), vmem(*wide, dtype=f32), vmem(*tall),
            vmem(width, total), dma((8,)),
        ],
    )
    self_sum = Sum(order, stages, sizes, [keep, send])
    memory_grad = order.through(memory_grad)
    ffn_part = lax.psum_scatter(order.after(ffn_part), "ctx", scatter_dimension=0, tiled=True)
    (memory_grad,) = order(
        copy_kernel, 1, [memory_grad], [(memory.shape, bf16)], vmem=SMALL_VMEM
    )
    for _ in range(first_ctx - 1):
        self_sum.step()
    turned = ((width, rows), lambda i: (0, i))
    (token_grad,) = order(
        token_kernel,
        length // rows,
        [(dq, *turned), (dk, *turned), (dv, *turned), (dz1, *row_block), small, self_qkv],
        [(wide, bf16, *row_block)],
    )
    self_sum.join(cross_sum)
    self_sum.step()
    ffn_sum = lax.all_gather(order.after(ffn_part), ("dp", "ctx"), axis=0, tiled=True)
    while not self_sum.last:
        self_sum.step()
    shapes = [(width, several * width) for several in (1, 1, 2, 1, 3)]
    shapes += [(several, width) for several in (2, 1, 2, 1, chunks, 1, 3, 3, 3)]
    grad_cross_q, grad_cross_out, grad_cross_kv, grad_out, grad_qkv, *smalls = order(
        finish_kernel,
        1,
        [self_sum.pieces[0], *self_sum.got],
        [(shape, f32) for shape in shapes],
        vmem=SMALL_VMEM,
    )
    square = (width, width)
    grad_ffn_out, grad_ffn_in = order(
        ffn_finish_kernel,
        chunks,
        [(ffn_sum, square, lambda i: (i, 0)), (ffn_sum, square, lambda i: (chunks + i, 0))],
        [
            ((hidden, width), f32, square, lambda i: (i, 0)),
            ((width, hidden), f32, square, lambda i: (0, i)),
        ],
    )
    (
        self_bias, self_out_bias, cross_bias, cross_out_bias, in_bias, out_bias, omega, gain, shift
    ) = smalls
    return (
        activations.reshape(tokens.shape),
        token_grad.reshape(tokens.shape),
        memory_grad,
        grad_qkv,
        self_bias,
        grad_out,
        self_out_bias.reshape(-1),
        grad_cross_q,
        grad_cross_kv,
        cross_bias,
        grad_cross_out,
        cross_out_bias.reshape(-1),
        grad_ffn_in,
        in_bias.reshape(-1),
        grad_ffn_out,
        out_bias.reshape(-1),
        omega,
        gain,
        shift,
    )


def solution(mesh):
    sizes = dict(mesh.shape)
    both = P(("dp", "ctx"), None, None)
    return jax.shard_map(
        functools.partial(local, sizes),
        mesh=mesh,
        in_specs=(both, P("dp", "ctx", None), P("dp", "ctx"), P(("dp", "ctx"), None), both)
        + (P(),) * 16,
        out_specs=(both, both, P("dp", "ctx", None)) + (P(),) * 16,
        check_vma=False,
    )
```

```python
import functools

import jax
import jax.numpy as jnp
from jax import lax
from jax.experimental import pallas as pl
from jax.experimental.pallas import tpu as pltpu
from jax.sharding import PartitionSpec as P

HEADS = 8
PAIR = 2
LOG2E = 1.4426950408889634
LN2 = 0.6931471805599453
UNSEEN = -1e30
BLOCK = 256
REACH = 2
PAD = 16
VMEM = 60 * 2**20
SMALL_VMEM = 24 * 2**20
bf16, f32 = jnp.bfloat16, jnp.float32

SELF_BIAS, SELF_OUT_BIAS, CROSS_BIAS, CROSS_OUT_BIAS = 0, 2, 3, 5
FFN_IN_BIAS, FFN_OUT_BIAS, OMEGA, GAIN, SHIFT, SMALL = 6, 10, 11, 14, 17, 24
LANES = 128


def dot(left, right, left_dim, right_dim):
    return lax.dot_general(
        left, right, (((left_dim,), (right_dim,)), ((), ())), preferred_element_type=f32
    )


def column(row):
    return jnp.transpose(jnp.broadcast_to(row, (8, row.shape[1])))[:, :1]


def row_sum(value):
    return jnp.sum(value.astype(f32), axis=0, keepdims=True)


def feature_sum(value):
    ones = jnp.ones((PAD, value.shape[1]), bf16)
    return dot(ones, value, 1, 1)[:1]


def normalize(value):
    centered = value - jnp.mean(value, axis=-1, keepdims=True)
    spread = jnp.mean(centered * centered, axis=-1, keepdims=True)
    inverse = lax.rsqrt(spread + 1e-05)
    return centered * inverse, inverse


def normalize_back(grad, gain, normal, inverse):
    scaled = grad * gain
    mean = jnp.mean(scaled, axis=-1, keepdims=True)
    slope = jnp.mean(scaled * normal, axis=-1, keepdims=True)
    return (scaled - mean - normal * slope) * inverse


def with_ones(rows):
    return jnp.concatenate((rows, jnp.ones((PAD, rows.shape[1]), bf16)), axis=0)


def start(copies):
    for copy in copies:
        copy.start()


def wait(copies):
    for copy in copies:
        copy.wait()


def prepare_kernel(stage, digit_ref, memory_ref, mask_ref, *refs):
    _, part_rows, width = memory_ref.shape
    params, par_ref, pieces = refs[:9], refs[9], refs[10:]
    row = 0
    for ref in params:
        value = ref[...].astype(f32)
        if value.ndim == 2:
            par_ref[row : row + value.shape[0], :] = value
            row += value.shape[0]
        else:
            for begin in range(0, value.shape[0], width):
                par_ref[row : row + 1, :] = value[begin : begin + width].reshape(1, width)
                row += 1
    par_ref[row:, :] = jnp.zeros((par_ref.shape[0] - row, width), f32)
    for d, piece in enumerate(pieces):
        index = digit_ref[stage] ^ d
        piece[:part_rows, :] = memory_ref[index]
        mask = mask_ref[pl.ds(index, 1), :].astype(f32)
        mask = jnp.concatenate((mask, jnp.zeros((1, width - part_rows), f32)), axis=1)
        piece[part_rows:, :] = jnp.broadcast_to(mask, (PAD, width)).astype(bf16)


def self_forward_kernel(
    digit_ref, x_ref, seg_ref, par_ref, qkv_w, out_hbm, cross_hbm,
    qkv_hbm, e_ref, inv_ref, o_hbm, z_hbm, h_hbm, q_hbm,
    qkv_ref, o_ref, z_ref, h_ref, q_ref, out_w, cross_w, q_mask, k_mask, sems,
):
    step = pl.program_id(0)
    last = pl.num_programs(0) - 1
    length, width = x_ref.shape
    size = width // HEADS
    scale = size**-0.5 * LOG2E
    copy = pltpu.make_async_copy
    loads = [copy(out_hbm, out_w, sems.at[0]), copy(cross_hbm, cross_w, sems.at[1])]
    projected = copy(qkv_ref, qkv_hbm, sems.at[2])

    @pl.when(step == 0)
    def _():
        start(loads)
        x = x_ref[...]
        for part, row in ((0, 0), (1, None), (2, 1)):
            columns = slice(part * width, (part + 1) * width)
            value = dot(qkv_w[:, columns], x, 0, 1)
            if row is not None:
                value = value + column(par_ref[SELF_BIAS + row : SELF_BIAS + row + 1])
            if part == 0:
                value = value * scale
            qkv_ref[columns, :] = value.astype(bf16)
        projected.start()
        same = lax.broadcasted_iota(jnp.int32, (PAD, length), 0) == seg_ref[...]
        q_mask[...] = jnp.where(same, 1.0, 0.0).astype(bf16)
        k_mask[...] = jnp.where(same, 0.0, UNSEEN).astype(bf16)

    causal = lax.broadcasted_iota(jnp.int32, (BLOCK, BLOCK), 0) <= lax.broadcasted_iota(
        jnp.int32, (BLOCK, BLOCK), 1
    )
    blocks = length // BLOCK
    for one in range(PAIR):
        head = step * PAIR + one
        base = pl.multiple_of(head * size, size)
        q = jnp.concatenate((qkv_ref[pl.ds(base, size), :], q_mask[...]), axis=0)
        k = jnp.concatenate((qkv_ref[pl.ds(width + base, size), :], k_mask[...]), axis=0)
        v = with_ones(qkv_ref[pl.ds(2 * width + base, size), :])
        scores, tops, mixed = [], [None] * blocks, [None] * blocks
        for i in range(blocks):
            s = dot(k[:, i * BLOCK : (i + 1) * BLOCK], q[:, i * BLOCK : (i + REACH + 1) * BLOCK], 0, 0)
            diagonal = jnp.where(causal, s[:, :BLOCK], UNSEEN)
            if s.shape[1] > BLOCK:
                diagonal = jnp.concatenate((diagonal, s[:, BLOCK:]), axis=1)
            scores.append(diagonal)
            top = jnp.max(diagonal, axis=0, keepdims=True)
            for b in range(s.shape[1] // BLOCK):
                part = top[:, b * BLOCK : (b + 1) * BLOCK]
                old = tops[i + b]
                tops[i + b] = part if old is None else jnp.maximum(old, part)
        for i, s in enumerate(scores):
            several = s.shape[1] // BLOCK
            weights = jnp.exp2(s - jnp.concatenate(tops[i : i + several], axis=1)).astype(bf16)
            e_ref[one, i, :, : several * BLOCK] = weights
            part = dot(v[:, i * BLOCK : (i + 1) * BLOCK], weights, 1, 0)
            for b in range(several):
                piece = part[:, b * BLOCK : (b + 1) * BLOCK]
                mixed[i + b] = piece if mixed[i + b] is None else mixed[i + b] + piece
        for j, value in enumerate(mixed):
            mine = slice(j * BLOCK, (j + 1) * BLOCK)
            inverse = 1.0 / value[size : size + 1]
            o_ref[pl.ds(base, size), mine] = (value[:size] * inverse).astype(bf16)
            inv_ref[pl.ds(head, 1), mine] = inverse

    @pl.when(step == last)
    def _():
        outs = [
            copy(o_ref, o_hbm, sems.at[3]),
            copy(z_ref, z_hbm, sems.at[4]),
            copy(h_ref, h_hbm, sems.at[5]),
            copy(q_ref, q_hbm, sems.at[6]),
        ]
        outs[0].start()
        wait(loads)
        z = (
            par_ref[OMEGA : OMEGA + 1] * x_ref[...].astype(f32)
            + dot(o_ref[...], out_w[...], 0, 0)
            + par_ref[SELF_OUT_BIAS : SELF_OUT_BIAS + 1]
        )
        z_ref[...] = z
        outs[1].start()
        normal, _ = normalize(z)
        h = (normal * par_ref[GAIN : GAIN + 1] + par_ref[SHIFT : SHIFT + 1]).astype(bf16)
        h_ref[...] = h
        outs[2].start()
        value = dot(cross_w[...], h, 0, 1) + column(par_ref[CROSS_BIAS : CROSS_BIAS + 1])
        q_ref[...] = (value * scale).astype(bf16)
        outs[3].start()
        wait([projected, *outs])


def cross_forward_kernel(
    holders, digit_ref, q_ref, par_ref, kv_w, h1_hbm, out_hbm, *refs
):
    pieces, refs = refs[:holders], refs[holders:]
    kv_hbm, e_ref, inv_ref, o_hbm, z_hbm, h_hbm, *refs = refs
    kv_ref, o_ref, z_ref, h_ref, h1_ref, out_w, k_mask, sems = refs
    step = pl.program_id(0)
    last = pl.num_programs(0) - 1
    length, width = h1_ref.shape
    size = width // HEADS
    part_rows = pieces[0].shape[0] - PAD
    copy = pltpu.make_async_copy
    loads = [copy(h1_hbm, h1_ref, sems.at[0]), copy(out_hbm, out_w, sems.at[1])]
    projected = copy(kv_ref, kv_hbm, sems.at[2])

    @pl.when(step == 0)
    def _():
        start(loads)
        shift = column(par_ref[CROSS_BIAS + 1 : CROSS_BIAS + 2])
        first = lax.broadcasted_iota(jnp.int32, (PAD, part_rows), 0) == 0
        for b, piece in enumerate(pieces):
            columns = slice(b * part_rows, (b + 1) * part_rows)
            m = piece[:part_rows, :]
            kv_ref[:width, columns] = dot(kv_w[:, :width], m, 0, 1).astype(bf16)
            kv_ref[width:, columns] = (dot(kv_w[:, width:], m, 0, 1) + shift).astype(bf16)
            seen = piece[part_rows:, :part_rows].astype(f32) > 0.5
            k_mask[:, columns] = jnp.where(first & ~seen, UNSEEN, 0.0).astype(bf16)
        projected.start()

    for one in range(PAIR):
        head = step * PAIR + one
        base = pl.multiple_of(head * size, size)
        q = with_ones(q_ref[one * size : (one + 1) * size, :])
        k = jnp.concatenate((kv_ref[pl.ds(base, size), :], k_mask[...]), axis=0)
        v = with_ones(kv_ref[pl.ds(width + base, size), :])
        scores = dot(k, q, 0, 0)
        weights = jnp.exp2(scores - jnp.max(scores, axis=0, keepdims=True)).astype(bf16)
        e_ref[one] = weights
        mixed = dot(v, weights, 1, 0)
        inverse = 1.0 / mixed[size : size + 1]
        o_ref[pl.ds(base, size), :] = (mixed[:size] * inverse).astype(bf16)
        inv_ref[pl.ds(head, 1), :] = inverse

    @pl.when(step == last)
    def _():
        outs = [
            copy(o_ref, o_hbm, sems.at[3]),
            copy(z_ref, z_hbm, sems.at[4]),
            copy(h_ref, h_hbm, sems.at[5]),
        ]
        outs[0].start()
        wait(loads)
        z = (
            par_ref[OMEGA + 1 : OMEGA + 2] * h1_ref[...].astype(f32)
            + dot(o_ref[...], out_w[...], 0, 0)
            + par_ref[CROSS_OUT_BIAS : CROSS_OUT_BIAS + 1]
        )
        z_ref[...] = z
        outs[1].start()
        normal, _ = normalize(z)
        h_ref[...] = (
            normal * par_ref[GAIN + 1 : GAIN + 2] + par_ref[SHIFT + 1 : SHIFT + 2]
        ).astype(bf16)
        outs[2].start()
        wait([projected, *outs])


def ffn_kernel(
    digit_ref, h2_ref, h1_ref, z2_ref, cot_ref, par_ref, in_w, out_hbm,
    act_ref, dz_ref, keep_hbm, send_hbm, small_ref,
    h_buf, g_buf, slope_buf, e_buf, eu_buf, grad_buf, out_w, sems,
):
    step = pl.program_id(0)
    rows, width = cot_ref.shape
    hidden = in_w.shape[1]
    chunks = hidden // width
    begin = pl.multiple_of(step * rows, rows)
    mine = pl.ds(begin, rows)
    load = pltpu.make_async_copy(out_hbm, out_w, sems.at[2 * chunks])

    @pl.when(step == 0)
    def _():
        load.start()
        small_ref[...] = jnp.zeros_like(small_ref)

    def add(row, value):
        small_ref[row : row + 1] += row_sum(value)

    h2 = h2_ref[...]
    h_buf[mine, :] = h2
    h2_wide = h2.astype(f32)
    for c in range(chunks):
        columns = slice(c * width, (c + 1) * width)
        u = dot(h2, in_w[:, columns], 1, 0) + par_ref[FFN_IN_BIAS + c : FFN_IN_BIAS + c + 1]
        rate = 0.7978845608028654
        square = u * u
        t = jnp.tanh(u * (rate + (rate * 0.044715) * square))
        half = 0.5 + 0.5 * t
        g_buf[mine, columns] = (u * half).astype(bf16)
        slope_buf[:, columns] = half + (0.5 * u) * (1.0 - t * t) * (
            rate + (3 * rate * 0.044715) * square
        )

    @pl.when(step == 0)
    def _():
        load.wait()

    z3 = (
        par_ref[OMEGA + 2 : OMEGA + 3] * h2_wide
        + dot(g_buf[mine, :], out_w[...], 1, 0)
        + par_ref[FFN_OUT_BIAS : FFN_OUT_BIAS + 1]
    )
    normal, inverse = normalize(z3)
    gain = par_ref[GAIN + 2 : GAIN + 3]
    act_ref[...] = (normal * gain + par_ref[SHIFT + 2 : SHIFT + 3]).astype(bf16)
    dy = cot_ref[...].astype(f32)
    add(GAIN + 2, dy * normal)
    add(SHIFT + 2, dy)
    dz3 = normalize_back(dy, gain, normal, inverse)
    add(OMEGA + 2, dz3 * h2_wide)
    e3 = dz3.astype(bf16)
    e_buf[mine, :] = e3
    add(FFN_OUT_BIAS, e3)
    for c in range(chunks):
        columns = slice(c * width, (c + 1) * width)
        eu = (dot(e3, out_w[columns, :], 1, 1) * slope_buf[:, columns]).astype(bf16)
        eu_buf[mine, columns] = eu
        add(FFN_IN_BIAS + c, eu)
    dh2 = par_ref[OMEGA + 2 : OMEGA + 3] * dz3 + dot(eu_buf[mine, :], in_w[...], 1, 1)
    normal, inverse = normalize(z2_ref[...])
    add(GAIN + 1, dh2 * normal)
    add(SHIFT + 1, dh2)
    dz2 = normalize_back(dh2, par_ref[GAIN + 1 : GAIN + 2], normal, inverse)
    add(OMEGA + 1, dz2 * h1_ref[...].astype(f32))
    add(CROSS_OUT_BIAS, dz2.astype(bf16))
    dz_ref[...] = dz2

    @pl.when(step == pl.num_programs(0) - 1)
    def _():
        outs = []
        for half in range(2):
            mine = [c for c in range(chunks) if c // (chunks // 2) == half]
            for i, c in enumerate(mine + [chunks + c for c in mine]):
                columns = slice(c % chunks * width, (c % chunks + 1) * width)
                if c < chunks:
                    value = dot(g_buf[:, columns], e_buf[...], 0, 0)
                else:
                    value = dot(h_buf[...], eu_buf[:, columns], 0, 0)
                place = slice(i * width, (i + 1) * width)
                grad_buf[half, place, :] = value.astype(bf16)
                sem = sems.at[half * chunks + i]
                source = grad_buf.at[half, place]
                keep = pltpu.make_async_copy(source, keep_hbm.at[place], sem)
                send = pltpu.make_async_copy(source, send_hbm.at[place], sem)
                pl.when(digit_ref[0] == half)(keep.start)
                pl.when(digit_ref[0] != half)(send.start)
                outs.append(keep)
        wait(outs)


def back_heads(do_ref, out_w, e, inv_ref):
    value = dot(out_w[...], e, 1, 1)
    size = value.shape[0] // HEADS
    for i in range(HEADS):
        rows = slice(i * size, (i + 1) * size)
        do_ref[rows, :] = (value[rows] * inv_ref[i : i + 1]).astype(bf16)


def back_head(do_rows, o_rows):
    length = do_rows.shape[1]
    delta = jnp.sum(do_rows.astype(f32) * o_rows.astype(f32), axis=0, keepdims=True)
    high = delta.astype(bf16).astype(f32)
    row = lax.broadcasted_iota(jnp.int32, (PAD, length), 0)
    extra = jnp.where(row == 0, -high, jnp.where(row == 1, high - delta, 0.0))
    return jnp.concatenate((do_rows, extra.astype(bf16)), axis=0)


def cross_backward_kernel(
    holders, stage, digit_ref, e_ref, do_ref, o_ref, q_ref, k_ref, v_ref, par_ref, old_ref,
    z1_hbm, h1_hbm, x_hbm, qw_hbm, kw_hbm, dz2_hbm, *refs
):
    m_hbm, refs = refs[:holders], refs[holders:]
    mem_hbm, dz1_hbm, small_ref, *refs = refs
    keeps, sends, refs = refs[:2], refs[2:4], refs[4:]
    z1_ref, h1_ref, x_ref, q_w, kv_w, dz2_ref, m_ref, mem_ref, *refs = refs
    o_buf, dq_buf, dkv_buf, dz_buf, grad_buf, sems = refs
    step = pl.program_id(0)
    last = pl.num_programs(0) - 1
    length, width = x_ref.shape
    size = width // HEADS
    count = k_ref.shape[1]
    pair = PAIR * size
    part_rows = mem_ref.shape[1]
    copy = pltpu.make_async_copy
    pairs_of = [(z1_hbm, z1_ref), (h1_hbm, h1_ref), (x_hbm, x_ref), (qw_hbm, q_w), (kw_hbm, kv_w)]
    pairs_of += [(dz2_hbm, dz2_ref)]
    pairs_of += [(source.at[:part_rows], m_ref.at[b]) for b, source in enumerate(m_hbm)]
    loads = [copy(source, target, sems.at[i]) for i, (source, target) in enumerate(pairs_of)]

    @pl.when(step == 0)
    def _():
        start(loads)
        small_ref[...] = old_ref[...]

    base = pl.multiple_of(step * pair, pair)
    o_buf[pl.ds(base, pair), :] = o_ref[...]
    heads = []
    for one in range(PAIR):
        here = slice(one * size, (one + 1) * size)
        heads.append(
            (
                back_head(do_ref[here, :], o_ref[here, :]),
                q_ref[here, :],
                k_ref[here, :],
                with_ones(v_ref[here, :]),
            )
        )
    dq = [None] * PAIR
    for i in range(count // BLOCK):
        mine = slice(i * BLOCK, (i + 1) * BLOCK)
        for one, (do, q, k, v) in enumerate(heads):
            weights = e_ref[one, mine, :]
            ds = (weights.astype(f32) * dot(v[:, mine], do, 0, 0)).astype(bf16)
            begin = base + one * size
            dkv_buf[pl.ds(width + begin, size), mine] = dot(do[:size], weights, 1, 1).astype(bf16)
            dkv_buf[pl.ds(begin, size), mine] = (dot(q, ds, 1, 1) * LN2).astype(bf16)
            part = dot(k[:, mine], ds, 1, 0)
            dq[one] = part if i == 0 else dq[one] + part
    for one in range(PAIR):
        dq_buf[pl.ds(base + one * size, size), :] = (dq[one] * size**-0.5).astype(bf16)

    @pl.when(step == last)
    def _():
        wait(loads)
        after = len(loads)
        dq_all = dq_buf[...]
        dh1 = par_ref[OMEGA + 1 : OMEGA + 2] * dz2_ref[...] + dot(dq_all, q_w[...], 0, 1)
        normal, inverse = normalize(z1_ref[...])
        small_ref[GAIN : GAIN + 1] = row_sum(dh1 * normal)
        small_ref[SHIFT : SHIFT + 1] = row_sum(dh1)
        dz1 = normalize_back(dh1, par_ref[GAIN : GAIN + 1], normal, inverse)
        small_ref[OMEGA : OMEGA + 1] = row_sum(dz1 * x_ref[...].astype(f32))
        small_ref[SELF_OUT_BIAS : SELF_OUT_BIAS + 1] = row_sum(dz1.astype(bf16))
        dz_buf[...] = dz1
        outs = [copy(dz_buf, dz1_hbm, sems.at[after])]
        outs[0].start()
        small_ref[CROSS_BIAS : CROSS_BIAS + 1] = feature_sum(dq_all)
        small_ref[CROSS_BIAS + 1 : CROSS_BIAS + 2] = feature_sum(dkv_buf[width:, :])
        grad_buf[:, :width] = dot(h1_ref[...], dq_all, 0, 1).astype(bf16)
        grad_buf[:, width : 2 * width] = dot(
            o_buf[...], dz2_ref[...].astype(bf16), 1, 0
        ).astype(bf16)
        key_grad = value_grad = None
        for b in range(holders):
            columns = slice(b * part_rows, (b + 1) * part_rows)
            dkv = dkv_buf[:, columns]
            k_part = dot(m_ref[b], dkv[:width], 0, 1)
            v_part = dot(m_ref[b], dkv[width:], 0, 1)
            key_grad = k_part if b == 0 else key_grad + k_part
            value_grad = v_part if b == 0 else value_grad + v_part
        grad_buf[:, 2 * width : 3 * width] = key_grad.astype(bf16)
        grad_buf[:, 3 * width :] = value_grad.astype(bf16)
        outs += halves(digit_ref, grad_buf, keeps, sends, sems, after + 1 + holders)
        for b in range(holders):
            dkv = dkv_buf[:, b * part_rows : (b + 1) * part_rows]
            mem_ref[b] = dot(dkv, kv_w[...], 0, 1).astype(bf16)
            outs.append(copy(mem_ref.at[b], mem_hbm.at[digit_ref[stage] ^ b], sems.at[after + 1 + b]))
            outs[-1].start()
        wait(outs)


def halves(digit_ref, grad_buf, keeps, sends, sems, at):
    rows = grad_buf.shape[0] // 2
    result, begin = [], 0
    for keep, send in zip(keeps, sends):
        columns = slice(begin, begin + keep.shape[1])
        begin += keep.shape[1]
        for i, target in enumerate((keep, send)):
            mine = pl.ds(pl.multiple_of((digit_ref[0] ^ i) * rows, rows), rows)
            sem = sems.at[at + len(result)]
            result.append(pltpu.make_async_copy(grad_buf.at[mine, columns], target, sem))
            result[-1].start()
    return result


def back_start_kernel(digit_ref, dz_ref, inv_ref, out_w, do_ref):
    back_heads(do_ref, out_w, dz_ref[...].astype(bf16), inv_ref)


def self_backward_kernel(
    digit_ref, e_ref, inv_ref, o_ref, q_ref, k_ref, v_ref, dz1_ref, out_w,
    dq_ref, dk_ref, dv_ref, do_buf,
):
    step = pl.program_id(0)
    pair, length = q_ref.shape
    size = pair // PAIR
    blocks = length // BLOCK

    @pl.when(step == 0)
    def _():
        back_heads(do_buf, out_w, dz1_ref[...].astype(bf16), inv_ref)

    base = pl.multiple_of(step * pair, pair)
    for one in range(PAIR):
        here = slice(one * size, (one + 1) * size)
        do = back_head(do_buf[pl.ds(base + one * size, size), :], o_ref[here, :])
        q, k, v = q_ref[here, :], k_ref[here, :], with_ones(v_ref[here, :])
        dq = [None] * blocks
        for i in range(blocks):
            mine = slice(i * BLOCK, (i + 1) * BLOCK)
            several = min(blocks - i, REACH + 1)
            seen = slice(i * BLOCK, (i + several) * BLOCK)
            weights = e_ref[one, i, :, : several * BLOCK]
            ds = (weights.astype(f32) * dot(v[:, mine], do[:, seen], 0, 0)).astype(bf16)
            dv_ref[here, mine] = dot(do[:size, seen], weights, 1, 1).astype(bf16)
            dk_ref[here, mine] = (dot(q[:, seen], ds, 1, 1) * LN2).astype(bf16)
            part = dot(k[:, mine], ds, 1, 0)
            for b in range(several):
                piece = part[:, b * BLOCK : (b + 1) * BLOCK]
                dq[i + b] = piece if dq[i + b] is None else dq[i + b] + piece
        for j in range(blocks):
            dq_ref[here, j * BLOCK : (j + 1) * BLOCK] = (dq[j] * size**-0.5).astype(bf16)


def self_weights_kernel(
    digit_ref, old_ref, x_hbm, dq_hbm, dk_hbm, dv_hbm, dz1_hbm, o_hbm, *refs
):
    keeps, sends, refs = refs[:2], refs[2:4], refs[4:]
    (
        x_ref, dq_ref, dk_ref, dv_ref, dz1_ref, o_ref, grad_buf, sems,
    ) = refs
    width = x_ref.shape[1]
    refs = (x_ref, dq_ref, dk_ref, dv_ref, dz1_ref, o_ref)
    loads = [
        pltpu.make_async_copy(source, target, sems.at[i])
        for i, (source, target) in enumerate(
            zip((x_hbm, dq_hbm, dk_hbm, dv_hbm, dz1_hbm, o_hbm), refs)
        )
    ]
    start(loads)
    loads[0].wait()
    sums = []
    for part, ref in enumerate((dq_ref, dk_ref, dv_ref)):
        loads[1 + part].wait()
        d = ref[...]
        grad_buf[:, (part + 1) * width : (part + 2) * width] = dot(x_ref[...], d, 0, 1).astype(bf16)
        sums.append(feature_sum(d) if part != 1 else None)
    row = lax.broadcasted_iota(jnp.int32, old_ref.shape, 0)
    small = jnp.where(row == SELF_BIAS, sums[0], old_ref[...])
    small = jnp.where(row == SELF_BIAS + 1, sums[2], small)
    small = jnp.concatenate((small, jnp.zeros((LANES - SMALL, width), f32)), axis=0)
    grad_buf[:, 4 * width :] = jnp.transpose(small).astype(bf16)
    wait(loads[4:])
    grad_buf[:, :width] = dot(o_ref[...], dz1_ref[...].astype(bf16), 1, 0).astype(bf16)
    wait(halves(digit_ref, grad_buf, keeps, sends, sems, len(loads)))


def token_kernel(digit_ref, dq_ref, dk_ref, dv_ref, dz1_ref, par_ref, qkv_w, token_ref):
    width = dz1_ref.shape[1]
    total = par_ref[OMEGA : OMEGA + 1] * dz1_ref[...]
    for part, ref in enumerate((dq_ref, dk_ref, dv_ref)):
        total = total + dot(ref[...], qkv_w[:, part * width : (part + 1) * width], 0, 1)
    token_ref[...] = total.astype(bf16)


def tree_sum(values):
    while len(values) > 1:
        values = [a + b for a, b in zip(values[::2], values[1::2])]
    return values[0]


def combine_kernel(stage, outs, groups, *refs):
    sources, results = refs[1 : 1 + sum(groups)], refs[1 + sum(groups) :]
    rows = results[0].shape[0]
    for d in range(outs):
        begin = 0 if outs == 1 else pl.multiple_of((refs[0][stage] ^ d) * rows, rows)
        left, column = list(sources), 0
        for count in groups:
            group, left = left[:count], left[count:]
            total = tree_sum([ref[pl.ds(begin, rows), :].astype(f32) for ref in group])
            width = total.shape[1]
            results[d][:, column : column + width] = total.astype(bf16)
            column += width


def place_kernel(stage, ins, *refs):
    digit, sources, result = refs[0][stage], refs[1 : 1 + ins], refs[1 + ins]
    rows = sources[0].shape[0]
    for d in range(ins):
        result[pl.ds(pl.multiple_of((digit ^ d) * rows, rows), rows), :] = sources[d][...]


def finish_kernel(
    digit_ref, mine_hbm, other_hbm, cross_q, cross_out, cross_kv, self_out, self_qkv,
    self_bias, self_out_bias, cross_bias, cross_out_bias, in_bias, out_bias, omega, gain, shift,
    buf, *refs
):
    targets = (cross_q, cross_out, cross_kv, self_out, self_qkv)
    bufs, sems = refs[: len(targets)], refs[len(targets)]
    rows, width = mine_hbm.shape[0], cross_q.shape[1]
    loads = []
    for i, source in enumerate((mine_hbm, other_hbm)):
        here = pl.ds(pl.multiple_of((digit_ref[0] ^ i) * rows, rows), rows)
        loads.append(pltpu.make_async_copy(source, buf.at[here], sems.at[len(targets) + i]))
    start(loads)
    wait(loads)
    begin, outs = 0, []
    for i, (target, wide) in enumerate(zip(targets, bufs)):
        count = target.shape[1]
        wide[...] = buf[:, begin : begin + count].astype(f32)
        outs.append(pltpu.make_async_copy(wide, target, sems.at[i]))
        outs[-1].start()
        begin += count
    part = jnp.transpose(buf[:, begin:].astype(f32))
    begin = 0
    for target in (
        self_bias, self_out_bias, cross_bias, cross_out_bias, in_bias, out_bias, omega, gain, shift,
    ):
        count = target.shape[0]
        target[...] = part[begin : begin + count]
        begin += count
    wait(outs)


def copy_kernel(digit_ref, source, target):
    target[...] = source[...]


def ffn_finish_kernel(digit_ref, mine_hbm, other_hbm, out_hbm, in_hbm, buf, out_buf, in_buf, sems):
    rows, width = mine_hbm.shape
    chunks = out_hbm.shape[0] // width
    loads = [
        pltpu.make_async_copy(source, buf.at[digit_ref[0] ^ i], sems.at[2 * chunks + i])
        for i, source in enumerate((mine_hbm, other_hbm))
    ]
    start(loads)
    wait(loads)
    outs = []
    for c in range(chunks):
        half, place = c // (chunks // 2), c % (chunks // 2) * width
        out_buf[c] = buf[half, place : place + width, :].astype(f32)
        place += rows // 2
        in_buf[c] = buf[half, place : place + width, :].astype(f32)
        here = slice(c * width, (c + 1) * width)
        outs.append(pltpu.make_async_copy(out_buf.at[c], out_hbm.at[here], sems.at[2 * c]))
        outs.append(pltpu.make_async_copy(in_buf.at[c], in_hbm.at[:, here], sems.at[2 * c + 1]))
        start(outs[-2:])
    wait(outs)


class Order:
    def __init__(self, digits):
        self.digits = digits

    def after(self, value):
        return lax.optimization_barrier((value, self.digits))[0]

    def through(self, value):
        value, self.digits = lax.optimization_barrier((value, self.digits))
        return value

    def __call__(self, kernel, steps, ins, outs, scratch=(), vmem=VMEM, us=1):
        def whole(shape):
            return pl.BlockSpec(shape, lambda i: (0,) * len(shape), pipeline_mode=pl.Buffered(1))

        arrays, in_specs, shapes, out_specs = (
            [self.digits], [pl.BlockSpec(memory_space=pltpu.SMEM)], [], []
        )
        anywhere = pl.BlockSpec(memory_space=pl.ANY)
        for item in ins:
            if isinstance(item, tuple):
                arrays.append(item[0])
                in_specs.append(pl.BlockSpec(*item[1:]) if item[1:] else anywhere)
            else:
                arrays.append(item)
                in_specs.append(whole(item.shape))
        for shape, dtype, *block in outs:
            shapes.append(jax.ShapeDtypeStruct(shape, dtype))
            if block == [None]:
                out_specs.append(anywhere)
            elif block:
                out_specs.append(pl.BlockSpec(*block))
            else:
                out_specs.append(pl.BlockSpec(shape, lambda i, n=len(shape): (0,) * n))
        result = pl.pallas_call(
            kernel,
            grid=(steps,),
            in_specs=in_specs,
            out_specs=out_specs,
            out_shape=shapes,
            scratch_shapes=list(scratch),
            compiler_params=pltpu.CompilerParams(
                dimension_semantics=("arbitrary",), vmem_limit_bytes=vmem
            ),
            cost_estimate=pl.CostEstimate(flops=us * 10**9, bytes_accessed=0, transcendentals=0),
        )(*arrays)
        self.digits = lax.optimization_barrier((self.digits, result[0]))[0]
        return result


def stages_of(sizes):
    result = []
    for axis in ("dp", "ctx"):
        stride = 1
        while stride < sizes[axis]:
            left = sizes[axis] // stride
            count = 2 if (axis == "dp" and stride == 1) or left % 4 else 4
            result.append((axis, stride, count))
            stride *= count
    return result


class Sum:
    def __init__(self, order, stages, sizes, pieces):
        self.order, self.stages, self.sizes = order, stages, sizes
        self.stage, self.spread, self.pieces, self.others = 0, [], pieces, []
        self.send(0)

    def send(self, stage):
        axis, stride, count = self.stages[stage]
        pieces = self.pieces if len(self.pieces) > 1 else self.pieces * count
        self.got = [
            lax.ppermute(
                pieces[d], axis, [(i, i ^ (d * stride)) for i in range(self.sizes[axis])]
            )
            for d in range(1, count)
        ]

    def settle(self):
        self.spread.append(self.stage)
        self.stage += 1
        group = [self.pieces[0], *self.got]
        self.pieces, self.got = self.order(
            functools.partial(combine_kernel, self.stage, 1, [len(group)]), 1, group,
            [(group[0].shape, bf16)], vmem=SMALL_VMEM,
        ), []

    def join(self, other):
        self.others.append(other)

    def step(self):
        groups = [[one.pieces[0], *one.got] for one in (*self.others, self)]
        rows = groups[0][0].shape[0]
        width = sum(group[0].shape[1] for group in groups)
        outs = 1
        if self.stage < len(self.stages):
            if len(self.pieces) > 1:
                self.spread.append(self.stage)
            self.stage += 1
            if self.stage < len(self.stages):
                count = self.stages[self.stage][2]
                outs = count if rows % (PAD * count) == 0 else 1
            kernel = functools.partial(
                combine_kernel, self.stage, outs, [len(group) for group in groups]
            )
            rows //= outs
        else:
            stage = self.spread.pop()
            kernel = functools.partial(place_kernel, stage, len(groups[0]))
            rows *= len(groups[0])
        self.others = []
        self.pieces = self.order(
            kernel, 1, sum(groups, []), [((rows, width), bf16)] * outs, vmem=SMALL_VMEM
        )
        self.send(self.stage if self.stage < len(self.stages) else self.spread[-1])

    @property
    def last(self):
        return self.stage == len(self.stages) and len(self.spread) == 1


def local(sizes, *args):
    (
        tokens, memory, mem_mask, segment_ids, cotangent, self_qkv, self_bias, self_out,
        self_out_bias, cross_q, cross_kv, cross_bias, cross_out, cross_out_bias, ffn_in,
        ffn_in_bias, ffn_out, ffn_out_bias, omegas, ln_gains, ln_biases,
    ) = args
    length, width = tokens.shape[1:]
    hidden = ffn_in.shape[1]
    size = width // HEADS
    holders, part_rows = memory.shape[:2]
    count = holders * part_rows
    x = tokens.reshape(length, width)
    cot = cotangent.reshape(length, width)
    seg = segment_ids.reshape(1, length)
    stages = stages_of(sizes)
    digits = [(lax.axis_index(axis) // stride) % several for axis, stride, several in stages]
    first_ctx = [axis for axis, _, _ in stages].index("ctx")
    order = Order(jnp.stack(digits).astype(jnp.int32))

    blocks = length // BLOCK
    reach = (REACH + 1) * BLOCK

    pairs, pair = HEADS // PAIR, PAIR * size

    def scores_in(array):
        shape = (PAIR, *array.shape[1:])
        return (array, shape, lambda i: (i,) + (0,) * (len(shape) - 1))

    def scores_out(*shape):
        return ((HEADS, *shape), bf16, (PAIR, *shape), lambda i: (i,) + (0,) * len(shape))

    def pair_in(array, part=0):
        return (array, (pair, array.shape[1]), lambda i: (part * pairs + i, 0))

    def vmem(*shape, dtype=bf16):
        return pltpu.VMEM(shape, dtype)

    dma = pltpu.SemaphoreType.DMA
    tall, wide = (width, length), (length, width)
    small, *pieces = order(
        functools.partial(prepare_kernel, first_ctx),
        1,
        [
            memory, mem_mask, self_bias, self_out_bias, cross_bias, cross_out_bias, ffn_in_bias,
            ffn_out_bias, omegas, ln_gains, ln_biases,
        ],
        [((SMALL, width), f32)] + [((part_rows + PAD, width), bf16)] * holders,
    )

    def trade(pieces):
        return [pieces[0]] + [
            lax.ppermute(pieces[d], "ctx", [(i, i ^ d) for i in range(holders)])
            for d in range(1, holders)
        ]

    pieces = trade(pieces)
    qkv, e_self, inv_self, o, z1, h1, q2 = order(
        self_forward_kernel,
        pairs,
        [x, seg, small, self_qkv, (self_out,), (cross_q,)],
        [
            ((3 * width, length), bf16, None),
            scores_out(blocks, BLOCK, reach),
            ((HEADS, length), f32),
            (tall, bf16, None),
            (wide, f32, None),
            (wide, bf16, None),
            (tall, bf16, None),
        ],
        [
            vmem(3 * width, length), vmem(*tall), vmem(*wide, dtype=f32), vmem(*wide), vmem(*tall),
            vmem(width, width), vmem(width, width), vmem(PAD, length), vmem(PAD, length), dma((7,)),
        ],
        us=15,
    )
    kv, e_cross, inv_cross, o2, z2, h2 = order(
        functools.partial(cross_forward_kernel, holders),
        pairs,
        [pair_in(q2), small, cross_kv, (h1,), (cross_out,), *pieces],
        [
            ((2 * width, count), bf16, None),
            scores_out(count, length),
            ((HEADS, length), f32),
            (tall, bf16, None),
            (wide, f32, None),
            (wide, bf16, None),
        ],
        [
            vmem(2 * width, count), vmem(*tall), vmem(*wide, dtype=f32), vmem(*wide), vmem(*wide),
            vmem(width, width), vmem(PAD, count), dma((6,)),
        ],
        us=22,
    )
    rows = BLOCK
    chunks = hidden // width
    row_block = ((rows, width), lambda i: (i, 0))
    activations, dz2, keep, send, small_grad = order(
        ffn_kernel,
        length // rows,
        [
            (h2, *row_block), (h1, *row_block), (z2, *row_block), (cot, *row_block), small, ffn_in,
            (ffn_out,),
        ],
        [
            (wide, bf16, *row_block),
            (wide, f32, *row_block),
            ((hidden, width), bf16, None),
            ((hidden, width), bf16, None),
            ((SMALL, width), f32),
        ],
        [
            vmem(*wide), vmem(length, hidden), vmem(rows, hidden, dtype=f32), vmem(*wide),
            vmem(length, hidden), vmem(2, hidden, width), vmem(hidden, width),
            dma((2 * chunks + 1,)),
        ],
        us=26,
    )
    def open_sum(parts):
        several = len(parts) // 2
        *others, last = [
            Sum(order, stages, sizes, [keep, send])
            for keep, send in zip(parts[:several], parts[several:])
        ]
        for one in others:
            last.join(one)
        return last

    ffn_sum = open_sum([keep, send])
    (do2,) = order(back_start_kernel, 1, [dz2, inv_cross, cross_out], [(tall, bf16)], us=3)
    ffn_sum.step()
    parts = [((width // 2, 2 * width), bf16, None)] * 4
    mem_part, dz1, small_grad, *parts = order(
        functools.partial(cross_backward_kernel, holders, first_ctx),
        pairs,
        [
            scores_in(e_cross), pair_in(do2), pair_in(o2), pair_in(q2), pair_in(kv), pair_in(kv, 1),
            small, small_grad, (z1,), (h1,), (x,), (cross_q,), (cross_kv,), (dz2,),
            *[(piece,) for piece in pieces],
        ],
        [(memory.shape, bf16, None), (wide, f32, None), ((SMALL, width), f32)] + parts,
        [
            vmem(*wide, dtype=f32), vmem(*wide), vmem(*wide), vmem(width, width),
            vmem(width, 2 * width), vmem(*wide, dtype=f32), vmem(*memory.shape),
            vmem(*memory.shape), vmem(*tall), vmem(*tall), vmem(2 * width, count),
            vmem(*wide, dtype=f32), vmem(width, 4 * width), dma((6 + 2 * holders + 9,)),
        ],
        us=26,
    )
    cross_sum = open_sum(parts)
    ffn_sum.step()
    cross_sum.step()
    memory_grad = lax.all_to_all(mem_part, "ctx", split_axis=0, concat_axis=0, tiled=True)
    total = 4 * width + LANES
    pair_out = (tall, bf16, (pair, length), lambda i: (i, 0))
    dq, dk, dv = order(
        self_backward_kernel,
        pairs,
        [
            scores_in(e_self), inv_self, pair_in(o), pair_in(qkv), pair_in(qkv, 1), pair_in(qkv, 2),
            dz1, self_out,
        ],
        [pair_out] * 3,
        [vmem(*tall)],
        us=16,
    )
    for _ in range(first_ctx - 2):
        cross_sum.step()
    cross_sum.settle()
    parts = [((width // 2, some), bf16, None) for some in (2 * width, 2 * width + LANES)] * 2
    self_sum = open_sum(
        order(
            self_weights_kernel,
            1,
            [small_grad, (x,), (dq,), (dk,), (dv,), (dz1,), (o,)],
            parts,
            [
                vmem(*wide), vmem(*tall), vmem(*tall), vmem(*tall), vmem(*wide, dtype=f32),
                vmem(*tall), vmem(width, total), dma((6 + 10,)),
            ],
            us=7,
        )
    )
    (memory_grad,) = order(
        copy_kernel, 1, [memory_grad], [(memory.shape, bf16)], vmem=SMALL_VMEM
    )
    for _ in range(first_ctx - 1):
        self_sum.step()
    ffn_sum.step()
    self_sum.join(cross_sum)
    self_sum.step()
    ffn_sum.step()
    self_sum.step()
    turned = ((width, rows), lambda i: (0, i))
    (token_grad,) = order(
        token_kernel,
        length // rows,
        [(dq, *turned), (dk, *turned), (dv, *turned), (dz1, *row_block), small, self_qkv],
        [(wide, bf16, *row_block)],
        us=6,
    )
    while not ffn_sum.last:
        ffn_sum.step()
    while len(self_sum.spread) > 2 or self_sum.stage < len(stages):
        self_sum.step()
    self_sum.step()
    square = (width, width)
    grad_ffn_out, grad_ffn_in = order(
        ffn_finish_kernel,
        1,
        [(ffn_sum.pieces[0],), (ffn_sum.got[0],)],
        [((hidden, width), f32, None), ((width, hidden), f32, None)],
        [
            vmem(2, hidden, width), vmem(chunks, *square, dtype=f32),
            vmem(chunks, *square, dtype=f32), dma((2 * chunks + 2,)),
        ],
        vmem=SMALL_VMEM,
    )
    while not self_sum.last:
        self_sum.step()
    shapes = [(width, several * width) for several in (1, 1, 2, 1, 3)]
    shapes += [(several, width) for several in (2, 1, 2, 1, chunks, 1, 3, 3, 3)]
    large = [shape for shape in shapes if shape[0] == width]
    grad_cross_q, grad_cross_out, grad_cross_kv, grad_out, grad_qkv, *smalls = order(
        finish_kernel,
        1,
        [(self_sum.pieces[0],), (self_sum.got[0],)],
        [(shape, f32, None) if shape in large else (shape, f32) for shape in shapes],
        [vmem(width, 8 * width + LANES), *[vmem(*shape, dtype=f32) for shape in large], dma((7,))],
        vmem=SMALL_VMEM,
    )
    (
        self_bias, self_out_bias, cross_bias, cross_out_bias, in_bias, out_bias, omega, gain, shift
    ) = smalls
    return (
        activations.reshape(tokens.shape),
        token_grad.reshape(tokens.shape),
        memory_grad,
        grad_qkv,
        self_bias,
        grad_out,
        self_out_bias.reshape(-1),
        grad_cross_q,
        grad_cross_kv,
        cross_bias,
        grad_cross_out,
        cross_out_bias.reshape(-1),
        grad_ffn_in,
        in_bias.reshape(-1),
        grad_ffn_out,
        out_bias.reshape(-1),
        omega,
        gain,
        shift,
    )


def solution(mesh):
    sizes = dict(mesh.shape)
    both = P(("dp", "ctx"), None, None)
    return jax.shard_map(
        functools.partial(local, sizes),
        mesh=mesh,
        in_specs=(both, P("dp", "ctx", None), P("dp", "ctx"), P(("dp", "ctx"), None), both)
        + (P(),) * 16,
        out_specs=(both, both, P("dp", "ctx", None)) + (P(),) * 16,
        check_vma=False,
    )
```

```python
import functools

import jax
import jax.numpy as jnp
from jax import lax
from jax.experimental import pallas as pl
from jax.experimental.pallas import tpu as pltpu
from jax.sharding import PartitionSpec as P

HEADS = 8
PAIR = 2
LOG2E = 1.4426950408889634
LN2 = 0.6931471805599453
UNSEEN = -1e30
BLOCK = 256
REACH = 2
PAD = 16
VMEM = 60 * 2**20
SMALL_VMEM = 24 * 2**20
bf16, f32 = jnp.bfloat16, jnp.float32

SELF_BIAS, SELF_OUT_BIAS, CROSS_BIAS, CROSS_OUT_BIAS = 0, 2, 3, 5
FFN_IN_BIAS, FFN_OUT_BIAS, OMEGA, GAIN, SHIFT, SMALL = 6, 10, 11, 14, 17, 24
LANES = 128


def dot(left, right, left_dim, right_dim):
    return lax.dot_general(
        left, right, (((left_dim,), (right_dim,)), ((), ())), preferred_element_type=f32
    )


def column(row):
    return jnp.transpose(jnp.broadcast_to(row, (8, row.shape[1])))[:, :1]


def row_sum(value):
    return jnp.sum(value.astype(f32), axis=0, keepdims=True)


def feature_sum(value):
    ones = jnp.ones((PAD, value.shape[1]), bf16)
    return dot(ones, value, 1, 1)[:1]


def normalize(value):
    centered = value - jnp.mean(value, axis=-1, keepdims=True)
    spread = jnp.mean(centered * centered, axis=-1, keepdims=True)
    inverse = lax.rsqrt(spread + 1e-05)
    return centered * inverse, inverse


def normalize_back(grad, gain, normal, inverse):
    scaled = grad * gain
    mean = jnp.mean(scaled, axis=-1, keepdims=True)
    slope = jnp.mean(scaled * normal, axis=-1, keepdims=True)
    return (scaled - mean - normal * slope) * inverse


def with_ones(rows):
    return jnp.concatenate((rows, jnp.ones((PAD, rows.shape[1]), bf16)), axis=0)


def start(copies):
    for copy in copies:
        copy.start()


def wait(copies):
    for copy in copies:
        copy.wait()


def prepare_kernel(stage, digit_ref, memory_ref, mask_ref, *refs):
    _, part_rows, width = memory_ref.shape
    params, par_ref, pieces = refs[:9], refs[9], refs[10:]
    row = 0
    for ref in params:
        value = ref[...].astype(f32)
        if value.ndim == 2:
            par_ref[row : row + value.shape[0], :] = value
            row += value.shape[0]
        else:
            for begin in range(0, value.shape[0], width):
                par_ref[row : row + 1, :] = value[begin : begin + width].reshape(1, width)
                row += 1
    par_ref[row:, :] = jnp.zeros((par_ref.shape[0] - row, width), f32)
    for d, piece in enumerate(pieces):
        index = digit_ref[stage] ^ d
        piece[:part_rows, :] = memory_ref[index]
        mask = mask_ref[pl.ds(index, 1), :].astype(f32)
        mask = jnp.concatenate((mask, jnp.zeros((1, width - part_rows), f32)), axis=1)
        piece[part_rows:, :] = jnp.broadcast_to(mask, (PAD, width)).astype(bf16)


def self_forward_kernel(
    digit_ref, x_ref, seg_ref, par_ref, qkv_w, out_hbm, cross_hbm,
    qkv_hbm, e_ref, inv_ref, o_hbm, z_hbm, h_hbm, q_hbm,
    qkv_ref, o_ref, z_ref, h_ref, q_ref, out_w, cross_w, q_mask, k_mask, sems,
):
    step = pl.program_id(0)
    last = pl.num_programs(0) - 1
    length, width = x_ref.shape
    size = width // HEADS
    scale = size**-0.5 * LOG2E
    copy = pltpu.make_async_copy
    loads = [copy(out_hbm, out_w, sems.at[0]), copy(cross_hbm, cross_w, sems.at[1])]
    projected = copy(qkv_ref, qkv_hbm, sems.at[2])

    @pl.when(step == 0)
    def _():
        start(loads)
        x = x_ref[...]
        for part, row in ((0, 0), (1, None), (2, 1)):
            columns = slice(part * width, (part + 1) * width)
            value = dot(qkv_w[:, columns], x, 0, 1)
            if row is not None:
                value = value + column(par_ref[SELF_BIAS + row : SELF_BIAS + row + 1])
            if part == 0:
                value = value * scale
            qkv_ref[columns, :] = value.astype(bf16)
        projected.start()
        same = lax.broadcasted_iota(jnp.int32, (PAD, length), 0) == seg_ref[...]
        q_mask[...] = jnp.where(same, 1.0, 0.0).astype(bf16)
        k_mask[...] = jnp.where(same, 0.0, UNSEEN).astype(bf16)

    causal = lax.broadcasted_iota(jnp.int32, (BLOCK, BLOCK), 0) <= lax.broadcasted_iota(
        jnp.int32, (BLOCK, BLOCK), 1
    )
    blocks = length // BLOCK
    for one in range(PAIR):
        head = step * PAIR + one
        base = pl.multiple_of(head * size, size)
        q = jnp.concatenate((qkv_ref[pl.ds(base, size), :], q_mask[...]), axis=0)
        k = jnp.concatenate((qkv_ref[pl.ds(width + base, size), :], k_mask[...]), axis=0)
        v = with_ones(qkv_ref[pl.ds(2 * width + base, size), :])
        scores, tops, mixed = [], [None] * blocks, [None] * blocks
        for i in range(blocks):
            s = dot(k[:, i * BLOCK : (i + 1) * BLOCK], q[:, i * BLOCK : (i + REACH + 1) * BLOCK], 0, 0)
            diagonal = jnp.where(causal, s[:, :BLOCK], UNSEEN)
            if s.shape[1] > BLOCK:
                diagonal = jnp.concatenate((diagonal, s[:, BLOCK:]), axis=1)
            scores.append(diagonal)
            top = jnp.max(diagonal, axis=0, keepdims=True)
            for b in range(s.shape[1] // BLOCK):
                part = top[:, b * BLOCK : (b + 1) * BLOCK]
                old = tops[i + b]
                tops[i + b] = part if old is None else jnp.maximum(old, part)
        for i, s in enumerate(scores):
            several = s.shape[1] // BLOCK
            weights = jnp.exp2(s - jnp.concatenate(tops[i : i + several], axis=1)).astype(bf16)
            e_ref[one, i, :, : several * BLOCK] = weights
            part = dot(v[:, i * BLOCK : (i + 1) * BLOCK], weights, 1, 0)
            for b in range(several):
                piece = part[:, b * BLOCK : (b + 1) * BLOCK]
                mixed[i + b] = piece if mixed[i + b] is None else mixed[i + b] + piece
        for j, value in enumerate(mixed):
            mine = slice(j * BLOCK, (j + 1) * BLOCK)
            inverse = 1.0 / value[size : size + 1]
            o_ref[pl.ds(base, size), mine] = (value[:size] * inverse).astype(bf16)
            inv_ref[pl.ds(head, 1), mine] = inverse

    @pl.when(step == last)
    def _():
        outs = [
            copy(o_ref, o_hbm, sems.at[3]),
            copy(z_ref, z_hbm, sems.at[4]),
            copy(h_ref, h_hbm, sems.at[5]),
            copy(q_ref, q_hbm, sems.at[6]),
        ]
        outs[0].start()
        wait(loads)
        z = (
            par_ref[OMEGA : OMEGA + 1] * x_ref[...].astype(f32)
            + dot(o_ref[...], out_w[...], 0, 0)
            + par_ref[SELF_OUT_BIAS : SELF_OUT_BIAS + 1]
        )
        z_ref[...] = z
        outs[1].start()
        normal, _ = normalize(z)
        h = (normal * par_ref[GAIN : GAIN + 1] + par_ref[SHIFT : SHIFT + 1]).astype(bf16)
        h_ref[...] = h
        outs[2].start()
        value = dot(cross_w[...], h, 0, 1) + column(par_ref[CROSS_BIAS : CROSS_BIAS + 1])
        q_ref[...] = (value * scale).astype(bf16)
        outs[3].start()
        wait([projected, *outs])


def cross_forward_kernel(
    holders, digit_ref, q_ref, par_ref, kv_w, h1_hbm, out_hbm, *refs
):
    pieces, refs = refs[:holders], refs[holders:]
    kv_hbm, e_ref, inv_ref, o_hbm, z_hbm, h_hbm, *refs = refs
    kv_ref, o_ref, z_ref, h_ref, h1_ref, out_w, k_mask, sems = refs
    step = pl.program_id(0)
    last = pl.num_programs(0) - 1
    length, width = h1_ref.shape
    size = width // HEADS
    part_rows = pieces[0].shape[0] - PAD
    copy = pltpu.make_async_copy
    loads = [copy(h1_hbm, h1_ref, sems.at[0]), copy(out_hbm, out_w, sems.at[1])]
    projected = copy(kv_ref, kv_hbm, sems.at[2])

    @pl.when(step == 0)
    def _():
        start(loads)
        shift = column(par_ref[CROSS_BIAS + 1 : CROSS_BIAS + 2])
        first = lax.broadcasted_iota(jnp.int32, (PAD, part_rows), 0) == 0
        for b, piece in enumerate(pieces):
            columns = slice(b * part_rows, (b + 1) * part_rows)
            m = piece[:part_rows, :]
            kv_ref[:width, columns] = dot(kv_w[:, :width], m, 0, 1).astype(bf16)
            kv_ref[width:, columns] = (dot(kv_w[:, width:], m, 0, 1) + shift).astype(bf16)
            seen = piece[part_rows:, :part_rows].astype(f32) > 0.5
            k_mask[:, columns] = jnp.where(first & ~seen, UNSEEN, 0.0).astype(bf16)
        projected.start()

    for one in range(PAIR):
        head = step * PAIR + one
        base = pl.multiple_of(head * size, size)
        q = with_ones(q_ref[one * size : (one + 1) * size, :])
        k = jnp.concatenate((kv_ref[pl.ds(base, size), :], k_mask[...]), axis=0)
        v = with_ones(kv_ref[pl.ds(width + base, size), :])
        scores = dot(k, q, 0, 0)
        weights = jnp.exp2(scores - jnp.max(scores, axis=0, keepdims=True)).astype(bf16)
        e_ref[one] = weights
        mixed = dot(v, weights, 1, 0)
        inverse = 1.0 / mixed[size : size + 1]
        o_ref[pl.ds(base, size), :] = (mixed[:size] * inverse).astype(bf16)
        inv_ref[pl.ds(head, 1), :] = inverse

    @pl.when(step == last)
    def _():
        outs = [
            copy(o_ref, o_hbm, sems.at[3]),
            copy(z_ref, z_hbm, sems.at[4]),
            copy(h_ref, h_hbm, sems.at[5]),
        ]
        outs[0].start()
        wait(loads)
        z = (
            par_ref[OMEGA + 1 : OMEGA + 2] * h1_ref[...].astype(f32)
            + dot(o_ref[...], out_w[...], 0, 0)
            + par_ref[CROSS_OUT_BIAS : CROSS_OUT_BIAS + 1]
        )
        z_ref[...] = z
        outs[1].start()
        normal, _ = normalize(z)
        h_ref[...] = (
            normal * par_ref[GAIN + 1 : GAIN + 2] + par_ref[SHIFT + 1 : SHIFT + 2]
        ).astype(bf16)
        outs[2].start()
        wait([projected, *outs])


def ffn_kernel(
    digit_ref, h2_ref, h1_ref, z2_ref, cot_ref, par_ref, in_w, out_hbm,
    act_ref, dz_ref, keep_hbm, send_hbm, small_ref,
    h_buf, g_buf, slope_buf, e_buf, eu_buf, grad_buf, out_w, sems,
):
    step = pl.program_id(0)
    rows, width = cot_ref.shape
    hidden = in_w.shape[1]
    chunks = hidden // width
    begin = pl.multiple_of(step * rows, rows)
    mine = pl.ds(begin, rows)
    load = pltpu.make_async_copy(out_hbm, out_w, sems.at[2 * chunks])

    @pl.when(step == 0)
    def _():
        load.start()
        small_ref[...] = jnp.zeros_like(small_ref)

    def add(row, value):
        small_ref[row : row + 1] += row_sum(value)

    h2 = h2_ref[...]
    h_buf[mine, :] = h2
    h2_wide = h2.astype(f32)
    for c in range(chunks):
        columns = slice(c * width, (c + 1) * width)
        u = dot(h2, in_w[:, columns], 1, 0) + par_ref[FFN_IN_BIAS + c : FFN_IN_BIAS + c + 1]
        rate = 0.7978845608028654
        square = u * u
        t = jnp.tanh(u * (rate + (rate * 0.044715) * square))
        half = 0.5 + 0.5 * t
        g_buf[mine, columns] = (u * half).astype(bf16)
        slope_buf[:, columns] = half + (0.5 * u) * (1.0 - t * t) * (
            rate + (3 * rate * 0.044715) * square
        )

    @pl.when(step == 0)
    def _():
        load.wait()

    z3 = (
        par_ref[OMEGA + 2 : OMEGA + 3] * h2_wide
        + dot(g_buf[mine, :], out_w[...], 1, 0)
        + par_ref[FFN_OUT_BIAS : FFN_OUT_BIAS + 1]
    )
    normal, inverse = normalize(z3)
    gain = par_ref[GAIN + 2 : GAIN + 3]
    act_ref[...] = (normal * gain + par_ref[SHIFT + 2 : SHIFT + 3]).astype(bf16)
    dy = cot_ref[...].astype(f32)
    add(GAIN + 2, dy * normal)
    add(SHIFT + 2, dy)
    dz3 = normalize_back(dy, gain, normal, inverse)
    add(OMEGA + 2, dz3 * h2_wide)
    e3 = dz3.astype(bf16)
    e_buf[mine, :] = e3
    add(FFN_OUT_BIAS, e3)
    for c in range(chunks):
        columns = slice(c * width, (c + 1) * width)
        eu = (dot(e3, out_w[columns, :], 1, 1) * slope_buf[:, columns]).astype(bf16)
        eu_buf[mine, columns] = eu
        add(FFN_IN_BIAS + c, eu)
    dh2 = par_ref[OMEGA + 2 : OMEGA + 3] * dz3 + dot(eu_buf[mine, :], in_w[...], 1, 1)
    normal, inverse = normalize(z2_ref[...])
    add(GAIN + 1, dh2 * normal)
    add(SHIFT + 1, dh2)
    dz2 = normalize_back(dh2, par_ref[GAIN + 1 : GAIN + 2], normal, inverse)
    add(OMEGA + 1, dz2 * h1_ref[...].astype(f32))
    add(CROSS_OUT_BIAS, dz2.astype(bf16))
    dz_ref[...] = dz2

    @pl.when(step == pl.num_programs(0) - 1)
    def _():
        outs = []
        for half in range(2):
            mine = [c for c in range(chunks) if c // (chunks // 2) == half]
            for i, c in enumerate(mine + [chunks + c for c in mine]):
                columns = slice(c % chunks * width, (c % chunks + 1) * width)
                if c < chunks:
                    value = dot(g_buf[:, columns], e_buf[...], 0, 0)
                else:
                    value = dot(h_buf[...], eu_buf[:, columns], 0, 0)
                place = slice(i * width, (i + 1) * width)
                grad_buf[half, place, :] = value.astype(bf16)
                sem = sems.at[half * chunks + i]
                source = grad_buf.at[half, place]
                keep = pltpu.make_async_copy(source, keep_hbm.at[place], sem)
                send = pltpu.make_async_copy(source, send_hbm.at[place], sem)
                pl.when(digit_ref[0] == half)(keep.start)
                pl.when(digit_ref[0] != half)(send.start)
                outs.append(keep)
        wait(outs)


def back_heads(do_ref, out_w, e, inv_ref):
    value = dot(out_w[...], e, 1, 1)
    size = value.shape[0] // HEADS
    for i in range(HEADS):
        rows = slice(i * size, (i + 1) * size)
        do_ref[rows, :] = (value[rows] * inv_ref[i : i + 1]).astype(bf16)


def back_head(do_rows, o_rows):
    length = do_rows.shape[1]
    delta = jnp.sum(do_rows.astype(f32) * o_rows.astype(f32), axis=0, keepdims=True)
    high = delta.astype(bf16).astype(f32)
    row = lax.broadcasted_iota(jnp.int32, (PAD, length), 0)
    extra = jnp.where(row == 0, -high, jnp.where(row == 1, high - delta, 0.0))
    return jnp.concatenate((do_rows, extra.astype(bf16)), axis=0)


def cross_backward_kernel(
    holders, digit_ref, e_ref, do_ref, o_ref, q_ref, k_ref, v_ref, par_ref, old_ref,
    z1_hbm, h1_hbm, x_hbm, qw_hbm, kw_hbm, dz2_hbm, *refs
):
    m_hbm, refs = refs[:holders], refs[holders:]
    mem_hbm, refs = refs[:holders], refs[holders:]
    dz1_hbm, small_ref, *refs = refs
    keeps, sends, refs = refs[:2], refs[2:4], refs[4:]
    z1_ref, h1_ref, x_ref, q_w, kv_w, dz2_ref, m_ref, mem_ref, *refs = refs
    o_buf, dq_buf, dkv_buf, dz_buf, grad_buf, sems = refs
    step = pl.program_id(0)
    last = pl.num_programs(0) - 1
    length, width = x_ref.shape
    size = width // HEADS
    count = k_ref.shape[1]
    pair = PAIR * size
    part_rows = mem_ref.shape[1]
    copy = pltpu.make_async_copy
    pairs_of = [(z1_hbm, z1_ref), (h1_hbm, h1_ref), (x_hbm, x_ref), (qw_hbm, q_w), (kw_hbm, kv_w)]
    pairs_of += [(dz2_hbm, dz2_ref)]
    pairs_of += [(source.at[:part_rows], m_ref.at[b]) for b, source in enumerate(m_hbm)]
    loads = [copy(source, target, sems.at[i]) for i, (source, target) in enumerate(pairs_of)]

    @pl.when(step == 0)
    def _():
        start(loads)
        small_ref[...] = old_ref[...]

    base = pl.multiple_of(step * pair, pair)
    o_buf[pl.ds(base, pair), :] = o_ref[...]
    heads = []
    for one in range(PAIR):
        here = slice(one * size, (one + 1) * size)
        heads.append(
            (
                back_head(do_ref[here, :], o_ref[here, :]),
                q_ref[here, :],
                k_ref[here, :],
                with_ones(v_ref[here, :]),
            )
        )
    dq = [None] * PAIR
    for i in range(count // BLOCK):
        mine = slice(i * BLOCK, (i + 1) * BLOCK)
        for one, (do, q, k, v) in enumerate(heads):
            weights = e_ref[one, mine, :]
            ds = (weights.astype(f32) * dot(v[:, mine], do, 0, 0)).astype(bf16)
            begin = base + one * size
            dkv_buf[pl.ds(width + begin, size), mine] = dot(do[:size], weights, 1, 1).astype(bf16)
            dkv_buf[pl.ds(begin, size), mine] = (dot(q, ds, 1, 1) * LN2).astype(bf16)
            part = dot(k[:, mine], ds, 1, 0)
            dq[one] = part if i == 0 else dq[one] + part
    for one in range(PAIR):
        dq_buf[pl.ds(base + one * size, size), :] = (dq[one] * size**-0.5).astype(bf16)

    @pl.when(step == last)
    def _():
        wait(loads)
        after = len(loads)
        dq_all = dq_buf[...]
        dh1 = par_ref[OMEGA + 1 : OMEGA + 2] * dz2_ref[...] + dot(dq_all, q_w[...], 0, 1)
        normal, inverse = normalize(z1_ref[...])
        small_ref[GAIN : GAIN + 1] = row_sum(dh1 * normal)
        small_ref[SHIFT : SHIFT + 1] = row_sum(dh1)
        dz1 = normalize_back(dh1, par_ref[GAIN : GAIN + 1], normal, inverse)
        small_ref[OMEGA : OMEGA + 1] = row_sum(dz1 * x_ref[...].astype(f32))
        small_ref[SELF_OUT_BIAS : SELF_OUT_BIAS + 1] = row_sum(dz1.astype(bf16))
        dz_buf[...] = dz1
        outs = [copy(dz_buf, dz1_hbm, sems.at[after])]
        outs[0].start()
        small_ref[CROSS_BIAS : CROSS_BIAS + 1] = feature_sum(dq_all)
        small_ref[CROSS_BIAS + 1 : CROSS_BIAS + 2] = feature_sum(dkv_buf[width:, :])
        grad_buf[:, :width] = dot(h1_ref[...], dq_all, 0, 1).astype(bf16)
        grad_buf[:, width : 2 * width] = dot(
            o_buf[...], dz2_ref[...].astype(bf16), 1, 0
        ).astype(bf16)
        key_grad = value_grad = None
        for b in range(holders):
            columns = slice(b * part_rows, (b + 1) * part_rows)
            dkv = dkv_buf[:, columns]
            k_part = dot(m_ref[b], dkv[:width], 0, 1)
            v_part = dot(m_ref[b], dkv[width:], 0, 1)
            key_grad = k_part if b == 0 else key_grad + k_part
            value_grad = v_part if b == 0 else value_grad + v_part
        grad_buf[:, 2 * width : 3 * width] = key_grad.astype(bf16)
        grad_buf[:, 3 * width :] = value_grad.astype(bf16)
        outs += halves(digit_ref, grad_buf, keeps, sends, sems, after + 1 + holders)
        for b in range(holders):
            dkv = dkv_buf[:, b * part_rows : (b + 1) * part_rows]
            mem_ref[b] = dot(dkv, kv_w[...], 0, 1).astype(bf16)
            outs.append(copy(mem_ref.at[b], mem_hbm[b], sems.at[after + 1 + b]))
            outs[-1].start()
        wait(outs)


def halves(digit_ref, grad_buf, keeps, sends, sems, at):
    rows = grad_buf.shape[0] // 2
    result, begin = [], 0
    for keep, send in zip(keeps, sends):
        columns = slice(begin, begin + keep.shape[1])
        begin += keep.shape[1]
        for i, target in enumerate((keep, send)):
            mine = pl.ds(pl.multiple_of((digit_ref[0] ^ i) * rows, rows), rows)
            sem = sems.at[at + len(result)]
            result.append(pltpu.make_async_copy(grad_buf.at[mine, columns], target, sem))
            result[-1].start()
    return result


def back_start_kernel(digit_ref, dz_ref, inv_ref, out_w, do_ref):
    back_heads(do_ref, out_w, dz_ref[...].astype(bf16), inv_ref)


def self_backward_kernel(
    digit_ref, e_ref, inv_ref, o_ref, q_ref, k_ref, v_ref, dz1_ref, out_w,
    dq_ref, dk_ref, dv_ref, do_buf,
):
    step = pl.program_id(0)
    pair, length = q_ref.shape
    size = pair // PAIR
    blocks = length // BLOCK

    @pl.when(step == 0)
    def _():
        back_heads(do_buf, out_w, dz1_ref[...].astype(bf16), inv_ref)

    base = pl.multiple_of(step * pair, pair)
    for one in range(PAIR):
        here = slice(one * size, (one + 1) * size)
        do = back_head(do_buf[pl.ds(base + one * size, size), :], o_ref[here, :])
        q, k, v = q_ref[here, :], k_ref[here, :], with_ones(v_ref[here, :])
        dq = [None] * blocks
        for i in range(blocks):
            mine = slice(i * BLOCK, (i + 1) * BLOCK)
            several = min(blocks - i, REACH + 1)
            seen = slice(i * BLOCK, (i + several) * BLOCK)
            weights = e_ref[one, i, :, : several * BLOCK]
            ds = (weights.astype(f32) * dot(v[:, mine], do[:, seen], 0, 0)).astype(bf16)
            dv_ref[here, mine] = dot(do[:size, seen], weights, 1, 1).astype(bf16)
            dk_ref[here, mine] = (dot(q[:, seen], ds, 1, 1) * LN2).astype(bf16)
            part = dot(k[:, mine], ds, 1, 0)
            for b in range(several):
                piece = part[:, b * BLOCK : (b + 1) * BLOCK]
                dq[i + b] = piece if dq[i + b] is None else dq[i + b] + piece
        for j in range(blocks):
            dq_ref[here, j * BLOCK : (j + 1) * BLOCK] = (dq[j] * size**-0.5).astype(bf16)


def self_weights_kernel(
    digit_ref, old_ref, x_hbm, dq_hbm, dk_hbm, dv_hbm, dz1_hbm, o_hbm, *refs
):
    keeps, sends, refs = refs[:2], refs[2:4], refs[4:]
    (
        x_ref, dq_ref, dk_ref, dv_ref, dz1_ref, o_ref, grad_buf, sems,
    ) = refs
    width = x_ref.shape[1]
    refs = (x_ref, dq_ref, dk_ref, dv_ref, dz1_ref, o_ref)
    loads = [
        pltpu.make_async_copy(source, target, sems.at[i])
        for i, (source, target) in enumerate(
            zip((x_hbm, dq_hbm, dk_hbm, dv_hbm, dz1_hbm, o_hbm), refs)
        )
    ]
    start(loads)
    loads[0].wait()
    sums = []
    for part, ref in enumerate((dq_ref, dk_ref, dv_ref)):
        loads[1 + part].wait()
        d = ref[...]
        grad_buf[:, (part + 1) * width : (part + 2) * width] = dot(x_ref[...], d, 0, 1).astype(bf16)
        sums.append(feature_sum(d) if part != 1 else None)
    row = lax.broadcasted_iota(jnp.int32, old_ref.shape, 0)
    small = jnp.where(row == SELF_BIAS, sums[0], old_ref[...])
    small = jnp.where(row == SELF_BIAS + 1, sums[2], small)
    small = jnp.concatenate((small, jnp.zeros((LANES - SMALL, width), f32)), axis=0)
    grad_buf[:, 4 * width :] = jnp.transpose(small).astype(bf16)
    wait(loads[4:])
    grad_buf[:, :width] = dot(o_ref[...], dz1_ref[...].astype(bf16), 1, 0).astype(bf16)
    wait(halves(digit_ref, grad_buf, keeps, sends, sems, len(loads)))


def token_kernel(digit_ref, dq_ref, dk_ref, dv_ref, dz1_ref, par_ref, qkv_w, token_ref):
    width = dz1_ref.shape[1]
    total = par_ref[OMEGA : OMEGA + 1] * dz1_ref[...]
    for part, ref in enumerate((dq_ref, dk_ref, dv_ref)):
        total = total + dot(ref[...], qkv_w[:, part * width : (part + 1) * width], 0, 1)
    token_ref[...] = total.astype(bf16)


def tree_sum(values):
    while len(values) > 1:
        values = [a + b for a, b in zip(values[::2], values[1::2])]
    return values[0]


def combine_kernel(stage, outs, groups, *refs):
    sources, results = refs[1 : 1 + sum(groups)], refs[1 + sum(groups) :]
    rows = results[0].shape[0]
    for d in range(outs):
        begin = 0 if outs == 1 else pl.multiple_of((refs[0][stage] ^ d) * rows, rows)
        left, column = list(sources), 0
        for count in groups:
            group, left = left[:count], left[count:]
            total = tree_sum([ref[pl.ds(begin, rows), :].astype(f32) for ref in group])
            width = total.shape[1]
            results[d][:, column : column + width] = total.astype(bf16)
            column += width


def place_kernel(stage, ins, *refs):
    digit, sources, result = refs[0][stage], refs[1 : 1 + ins], refs[1 + ins]
    rows = sources[0].shape[0]
    for d in range(ins):
        result[pl.ds(pl.multiple_of((digit ^ d) * rows, rows), rows), :] = sources[d][...]


def finish_kernel(
    digit_ref, mine_hbm, other_hbm, cross_q, cross_out, cross_kv, self_out, self_qkv,
    self_bias, self_out_bias, cross_bias, cross_out_bias, in_bias, out_bias, omega, gain, shift,
    buf, *refs
):
    targets = (cross_q, cross_out, cross_kv, self_out, self_qkv)
    bufs, sems = refs[: len(targets)], refs[len(targets)]
    rows, width = mine_hbm.shape[0], cross_q.shape[1]
    loads = []
    for i, source in enumerate((mine_hbm, other_hbm)):
        here = pl.ds(pl.multiple_of((digit_ref[0] ^ i) * rows, rows), rows)
        loads.append(pltpu.make_async_copy(source, buf.at[here], sems.at[len(targets) + i]))
    start(loads)
    wait(loads)
    begin, outs = 0, []
    for i, (target, wide) in enumerate(zip(targets, bufs)):
        count = target.shape[1]
        wide[...] = buf[:, begin : begin + count].astype(f32)
        outs.append(pltpu.make_async_copy(wide, target, sems.at[i]))
        outs[-1].start()
        begin += count
    part = jnp.transpose(buf[:, begin:].astype(f32))
    begin = 0
    for target in (
        self_bias, self_out_bias, cross_bias, cross_out_bias, in_bias, out_bias, omega, gain, shift,
    ):
        count = target.shape[0]
        target[...] = part[begin : begin + count]
        begin += count
    wait(outs)


def spread_kernel(stage, digit_ref, *refs):
    *sources, target = refs
    for d, source in enumerate(sources):
        target[digit_ref[stage] ^ d] = source[...]


def ffn_finish_kernel(digit_ref, mine_hbm, other_hbm, out_hbm, in_hbm, buf, out_buf, in_buf, sems):
    rows, width = mine_hbm.shape
    chunks = out_hbm.shape[0] // width
    loads = [
        pltpu.make_async_copy(source, buf.at[digit_ref[0] ^ i], sems.at[2 * chunks + i])
        for i, source in enumerate((mine_hbm, other_hbm))
    ]
    start(loads)
    wait(loads)
    outs = []
    for c in range(chunks):
        half, place = c // (chunks // 2), c % (chunks // 2) * width
        out_buf[c] = buf[half, place : place + width, :].astype(f32)
        place += rows // 2
        in_buf[c] = buf[half, place : place + width, :].astype(f32)
        here = slice(c * width, (c + 1) * width)
        outs.append(pltpu.make_async_copy(out_buf.at[c], out_hbm.at[here], sems.at[2 * c]))
        outs.append(pltpu.make_async_copy(in_buf.at[c], in_hbm.at[:, here], sems.at[2 * c + 1]))
        start(outs[-2:])
    wait(outs)


class Order:
    def __init__(self, digits):
        self.digits = digits

    def after(self, value):
        return lax.optimization_barrier((value, self.digits))[0]

    def through(self, value):
        value, self.digits = lax.optimization_barrier((value, self.digits))
        return value

    def __call__(self, kernel, steps, ins, outs, scratch=(), vmem=VMEM, us=1):
        def whole(shape):
            return pl.BlockSpec(shape, lambda i: (0,) * len(shape), pipeline_mode=pl.Buffered(1))

        arrays, in_specs, shapes, out_specs = (
            [self.digits], [pl.BlockSpec(memory_space=pltpu.SMEM)], [], []
        )
        anywhere = pl.BlockSpec(memory_space=pl.ANY)
        for item in ins:
            if isinstance(item, tuple):
                arrays.append(item[0])
                in_specs.append(pl.BlockSpec(*item[1:]) if item[1:] else anywhere)
            else:
                arrays.append(item)
                in_specs.append(whole(item.shape))
        for shape, dtype, *block in outs:
            shapes.append(jax.ShapeDtypeStruct(shape, dtype))
            if block == [None]:
                out_specs.append(anywhere)
            elif block:
                out_specs.append(pl.BlockSpec(*block))
            else:
                out_specs.append(pl.BlockSpec(shape, lambda i, n=len(shape): (0,) * n))
        result = pl.pallas_call(
            kernel,
            grid=(steps,),
            in_specs=in_specs,
            out_specs=out_specs,
            out_shape=shapes,
            scratch_shapes=list(scratch),
            compiler_params=pltpu.CompilerParams(
                dimension_semantics=("arbitrary",), vmem_limit_bytes=vmem
            ),
            cost_estimate=pl.CostEstimate(flops=us * 10**9, bytes_accessed=0, transcendentals=0),
        )(*arrays)
        self.digits = lax.optimization_barrier((self.digits, result[0]))[0]
        return result


def stages_of(sizes):
    result = []
    for axis in ("dp", "ctx"):
        stride = 1
        while stride < sizes[axis]:
            left = sizes[axis] // stride
            count = 2 if (axis == "dp" and stride == 1) or left % 4 else 4
            result.append((axis, stride, count))
            stride *= count
    return result


class Sum:
    def __init__(self, order, stages, sizes, pieces):
        self.order, self.stages, self.sizes = order, stages, sizes
        self.stage, self.spread, self.pieces, self.others = 0, [], pieces, []
        self.send(0)

    def send(self, stage):
        axis, stride, count = self.stages[stage]
        pieces = self.pieces if len(self.pieces) > 1 else self.pieces * count
        self.got = [
            lax.ppermute(
                pieces[d], axis, [(i, i ^ (d * stride)) for i in range(self.sizes[axis])]
            )
            for d in range(1, count)
        ]

    def settle(self):
        self.spread.append(self.stage)
        self.stage += 1
        group = [self.pieces[0], *self.got]
        self.pieces, self.got = self.order(
            functools.partial(combine_kernel, self.stage, 1, [len(group)]), 1, group,
            [(group[0].shape, bf16)], vmem=SMALL_VMEM,
        ), []

    def join(self, other):
        self.others.append(other)

    def step(self):
        groups = [[one.pieces[0], *one.got] for one in (*self.others, self)]
        rows = groups[0][0].shape[0]
        width = sum(group[0].shape[1] for group in groups)
        outs = 1
        if self.stage < len(self.stages):
            if len(self.pieces) > 1:
                self.spread.append(self.stage)
            self.stage += 1
            if self.stage < len(self.stages):
                count = self.stages[self.stage][2]
                outs = count if rows % (PAD * count) == 0 else 1
            kernel = functools.partial(
                combine_kernel, self.stage, outs, [len(group) for group in groups]
            )
            rows //= outs
        else:
            stage = self.spread.pop()
            kernel = functools.partial(place_kernel, stage, len(groups[0]))
            rows *= len(groups[0])
        self.others = []
        self.pieces = self.order(
            kernel, 1, sum(groups, []), [((rows, width), bf16)] * outs, vmem=SMALL_VMEM
        )
        self.send(self.stage if self.stage < len(self.stages) else self.spread[-1])

    @property
    def last(self):
        return self.stage == len(self.stages) and len(self.spread) == 1


def local(sizes, *args):
    (
        tokens, memory, mem_mask, segment_ids, cotangent, self_qkv, self_bias, self_out,
        self_out_bias, cross_q, cross_kv, cross_bias, cross_out, cross_out_bias, ffn_in,
        ffn_in_bias, ffn_out, ffn_out_bias, omegas, ln_gains, ln_biases,
    ) = args
    length, width = tokens.shape[1:]
    hidden = ffn_in.shape[1]
    size = width // HEADS
    holders, part_rows = memory.shape[:2]
    count = holders * part_rows
    x = tokens.reshape(length, width)
    cot = cotangent.reshape(length, width)
    seg = segment_ids.reshape(1, length)
    stages = stages_of(sizes)
    digits = [(lax.axis_index(axis) // stride) % several for axis, stride, several in stages]
    first_ctx = [axis for axis, _, _ in stages].index("ctx")
    order = Order(jnp.stack(digits).astype(jnp.int32))

    blocks = length // BLOCK
    reach = (REACH + 1) * BLOCK

    pairs, pair = HEADS // PAIR, PAIR * size

    def scores_in(array):
        shape = (PAIR, *array.shape[1:])
        return (array, shape, lambda i: (i,) + (0,) * (len(shape) - 1))

    def scores_out(*shape):
        return ((HEADS, *shape), bf16, (PAIR, *shape), lambda i: (i,) + (0,) * len(shape))

    def pair_in(array, part=0):
        return (array, (pair, array.shape[1]), lambda i: (part * pairs + i, 0))

    def vmem(*shape, dtype=bf16):
        return pltpu.VMEM(shape, dtype)

    dma = pltpu.SemaphoreType.DMA
    tall, wide = (width, length), (length, width)
    small, *pieces = order(
        functools.partial(prepare_kernel, first_ctx),
        1,
        [
            memory, mem_mask, self_bias, self_out_bias, cross_bias, cross_out_bias, ffn_in_bias,
            ffn_out_bias, omegas, ln_gains, ln_biases,
        ],
        [((SMALL, width), f32)] + [((part_rows + PAD, width), bf16)] * holders,
    )

    def trade(pieces):
        return [pieces[0]] + [
            lax.ppermute(pieces[d], "ctx", [(i, i ^ d) for i in range(holders)])
            for d in range(1, holders)
        ]

    pieces = trade(pieces)
    qkv, e_self, inv_self, o, z1, h1, q2 = order(
        self_forward_kernel,
        pairs,
        [x, seg, small, self_qkv, (self_out,), (cross_q,)],
        [
            ((3 * width, length), bf16, None),
            scores_out(blocks, BLOCK, reach),
            ((HEADS, length), f32),
            (tall, bf16, None),
            (wide, f32, None),
            (wide, bf16, None),
            (tall, bf16, None),
        ],
        [
            vmem(3 * width, length), vmem(*tall), vmem(*wide, dtype=f32), vmem(*wide), vmem(*tall),
            vmem(width, width), vmem(width, width), vmem(PAD, length), vmem(PAD, length), dma((7,)),
        ],
        us=15,
    )
    kv, e_cross, inv_cross, o2, z2, h2 = order(
        functools.partial(cross_forward_kernel, holders),
        pairs,
        [pair_in(q2), small, cross_kv, (h1,), (cross_out,), *pieces],
        [
            ((2 * width, count), bf16, None),
            scores_out(count, length),
            ((HEADS, length), f32),
            (tall, bf16, None),
            (wide, f32, None),
            (wide, bf16, None),
        ],
        [
            vmem(2 * width, count), vmem(*tall), vmem(*wide, dtype=f32), vmem(*wide), vmem(*wide),
            vmem(width, width), vmem(PAD, count), dma((6,)),
        ],
        us=22,
    )
    rows = BLOCK
    chunks = hidden // width
    row_block = ((rows, width), lambda i: (i, 0))
    activations, dz2, keep, send, small_grad = order(
        ffn_kernel,
        length // rows,
        [
            (h2, *row_block), (h1, *row_block), (z2, *row_block), (cot, *row_block), small, ffn_in,
            (ffn_out,),
        ],
        [
            (wide, bf16, *row_block),
            (wide, f32, *row_block),
            ((hidden, width), bf16, None),
            ((hidden, width), bf16, None),
            ((SMALL, width), f32),
        ],
        [
            vmem(*wide), vmem(length, hidden), vmem(rows, hidden, dtype=f32), vmem(*wide),
            vmem(length, hidden), vmem(2, hidden, width), vmem(hidden, width),
            dma((2 * chunks + 1,)),
        ],
        us=26,
    )
    def open_sum(parts):
        several = len(parts) // 2
        *others, last = [
            Sum(order, stages, sizes, [keep, send])
            for keep, send in zip(parts[:several], parts[several:])
        ]
        for one in others:
            last.join(one)
        return last

    ffn_sum = open_sum([keep, send])
    (do2,) = order(back_start_kernel, 1, [dz2, inv_cross, cross_out], [(tall, bf16)], us=3)
    ffn_sum.step()
    parts = [((width // 2, 2 * width), bf16, None)] * 4
    *mem_parts, dz1, small_grad, p0, p1, p2, p3 = order(
        functools.partial(cross_backward_kernel, holders),
        pairs,
        [
            scores_in(e_cross), pair_in(do2), pair_in(o2), pair_in(q2), pair_in(kv), pair_in(kv, 1),
            small, small_grad, (z1,), (h1,), (x,), (cross_q,), (cross_kv,), (dz2,),
            *[(piece,) for piece in pieces],
        ],
        [((part_rows, width), bf16, None)] * holders
        + [(wide, f32, None), ((SMALL, width), f32)]
        + parts,
        [
            vmem(*wide, dtype=f32), vmem(*wide), vmem(*wide), vmem(width, width),
            vmem(width, 2 * width), vmem(*wide, dtype=f32), vmem(*memory.shape),
            vmem(*memory.shape), vmem(*tall), vmem(*tall), vmem(2 * width, count),
            vmem(*wide, dtype=f32), vmem(width, 4 * width), dma((6 + 2 * holders + 9,)),
        ],
        us=26,
    )
    cross_sum = open_sum([p0, p1, p2, p3])
    ffn_sum.step()
    cross_sum.step()
    total = 4 * width + LANES
    pair_out = (tall, bf16, (pair, length), lambda i: (i, 0))
    dq, dk, dv = order(
        self_backward_kernel,
        pairs,
        [
            scores_in(e_self), inv_self, pair_in(o), pair_in(qkv), pair_in(qkv, 1), pair_in(qkv, 2),
            dz1, self_out,
        ],
        [pair_out] * 3,
        [vmem(*tall)],
        us=16,
    )
    for _ in range(first_ctx - 2):
        cross_sum.step()
    cross_sum.settle()
    ffn_sum.step()
    parts = [((width // 2, some), bf16, None) for some in (2 * width, 2 * width + LANES)] * 2
    self_sum = open_sum(
        order(
            self_weights_kernel,
            1,
            [small_grad, (x,), (dq,), (dk,), (dv,), (dz1,), (o,)],
            parts,
            [
                vmem(*wide), vmem(*tall), vmem(*tall), vmem(*tall), vmem(*wide, dtype=f32),
                vmem(*tall), vmem(width, total), dma((6 + 10,)),
            ],
            us=7,
        )
    )
    for _ in range(first_ctx - 1):
        self_sum.step()
    self_sum.join(cross_sum)
    self_sum.step()
    ffn_sum.step()
    self_sum.step()
    turned = ((width, rows), lambda i: (0, i))
    (token_grad,) = order(
        token_kernel,
        length // rows,
        [(dq, *turned), (dk, *turned), (dv, *turned), (dz1, *row_block), small, self_qkv],
        [(wide, bf16, *row_block)],
        us=6,
    )
    while not ffn_sum.last:
        ffn_sum.step()
    while len(self_sum.spread) > 2 or self_sum.stage < len(stages):
        self_sum.step()
    mem_parts = trade(order.after(mem_parts))
    (memory_grad,) = order(
        functools.partial(spread_kernel, first_ctx), 1, mem_parts, [(memory.shape, bf16)],
        vmem=SMALL_VMEM,
    )
    self_sum.step()
    while not self_sum.last:
        self_sum.step()
    square = (width, width)
    grad_ffn_out, grad_ffn_in = order(
        ffn_finish_kernel,
        1,
        [(ffn_sum.pieces[0],), (ffn_sum.got[0],)],
        [((hidden, width), f32, None), ((width, hidden), f32, None)],
        [
            vmem(2, hidden, width), vmem(chunks, *square, dtype=f32),
            vmem(chunks, *square, dtype=f32), dma((2 * chunks + 2,)),
        ],
        vmem=SMALL_VMEM,
    )
    shapes = [(width, several * width) for several in (1, 1, 2, 1, 3)]
    shapes += [(several, width) for several in (2, 1, 2, 1, chunks, 1, 3, 3, 3)]
    large = [shape for shape in shapes if shape[0] == width]
    grad_cross_q, grad_cross_out, grad_cross_kv, grad_out, grad_qkv, *smalls = order(
        finish_kernel,
        1,
        [(self_sum.pieces[0],), (self_sum.got[0],)],
        [(shape, f32, None) if shape in large else (shape, f32) for shape in shapes],
        [vmem(width, 8 * width + LANES), *[vmem(*shape, dtype=f32) for shape in large], dma((7,))],
        vmem=SMALL_VMEM,
    )
    (
        self_bias, self_out_bias, cross_bias, cross_out_bias, in_bias, out_bias, omega, gain, shift
    ) = smalls
    return (
        activations.reshape(tokens.shape),
        token_grad.reshape(tokens.shape),
        memory_grad,
        grad_qkv,
        self_bias,
        grad_out,
        self_out_bias.reshape(-1),
        grad_cross_q,
        grad_cross_kv,
        cross_bias,
        grad_cross_out,
        cross_out_bias.reshape(-1),
        grad_ffn_in,
        in_bias.reshape(-1),
        grad_ffn_out,
        out_bias.reshape(-1),
        omega,
        gain,
        shift,
    )


def solution(mesh):
    sizes = dict(mesh.shape)
    both = P(("dp", "ctx"), None, None)
    return jax.shard_map(
        functools.partial(local, sizes),
        mesh=mesh,
        in_specs=(both, P("dp", "ctx", None), P("dp", "ctx"), P(("dp", "ctx"), None), both)
        + (P(),) * 16,
        out_specs=(both, both, P("dp", "ctx", None)) + (P(),) * 16,
        check_vma=False,
    )
```

```python
import functools

import jax
import jax.numpy as jnp
from jax import lax
from jax.experimental import pallas as pl
from jax.experimental.pallas import tpu as pltpu
from jax.sharding import PartitionSpec as P

HEADS = 8
PAIR = 2
LOG2E = 1.4426950408889634
LN2 = 0.6931471805599453
UNSEEN = -1e30
BLOCK = 256
REACH = 2
PAD = 16
VMEM = 60 * 2**20
SMALL_VMEM = 24 * 2**20
bf16, f32 = jnp.bfloat16, jnp.float32

SELF_BIAS, SELF_OUT_BIAS, CROSS_BIAS, CROSS_OUT_BIAS = 0, 2, 3, 5
FFN_IN_BIAS, FFN_OUT_BIAS, OMEGA, GAIN, SHIFT, SMALL = 6, 10, 11, 14, 17, 24
LANES = 128


def dot(left, right, left_dim, right_dim):
    return lax.dot_general(
        left, right, (((left_dim,), (right_dim,)), ((), ())), preferred_element_type=f32
    )


def column(row):
    return jnp.transpose(jnp.broadcast_to(row, (8, row.shape[1])))[:, :1]


def row_sum(value):
    return jnp.sum(value.astype(f32), axis=0, keepdims=True)


def feature_sum(value):
    ones = jnp.ones((PAD, value.shape[1]), bf16)
    return dot(ones, value, 1, 1)[:1]


def normalize(value):
    centered = value - jnp.mean(value, axis=-1, keepdims=True)
    spread = jnp.mean(centered * centered, axis=-1, keepdims=True)
    inverse = lax.rsqrt(spread + 1e-05)
    return centered * inverse, inverse


def normalize_back(grad, gain, normal, inverse):
    scaled = grad * gain
    mean = jnp.mean(scaled, axis=-1, keepdims=True)
    slope = jnp.mean(scaled * normal, axis=-1, keepdims=True)
    return (scaled - mean - normal * slope) * inverse


def with_ones(rows):
    return jnp.concatenate((rows, jnp.ones((PAD, rows.shape[1]), bf16)), axis=0)


def start(copies):
    for copy in copies:
        copy.start()


def wait(copies):
    for copy in copies:
        copy.wait()


def score_copies(step, buf, hbm, sems):
    slot = lax.rem(step, 2)
    return [
        pltpu.make_async_copy(buf.at[slot, one], hbm.at[step * PAIR + one], sems.at[slot, one])
        for one in range(PAIR)
    ]


def prepare_kernel(stage, digit_ref, memory_ref, mask_ref, *refs):
    _, part_rows, width = memory_ref.shape
    params, par_ref, pieces = refs[:9], refs[9], refs[10:]
    row = 0
    for ref in params:
        value = ref[...].astype(f32)
        if value.ndim == 2:
            par_ref[row : row + value.shape[0], :] = value
            row += value.shape[0]
        else:
            for begin in range(0, value.shape[0], width):
                par_ref[row : row + 1, :] = value[begin : begin + width].reshape(1, width)
                row += 1
    par_ref[row:, :] = jnp.zeros((par_ref.shape[0] - row, width), f32)
    for d, piece in enumerate(pieces):
        index = digit_ref[stage] ^ d
        piece[:part_rows, :] = memory_ref[index]
        mask = mask_ref[pl.ds(index, 1), :].astype(f32)
        mask = jnp.concatenate((mask, jnp.zeros((1, width - part_rows), f32)), axis=1)
        piece[part_rows:, :] = jnp.broadcast_to(mask, (PAD, width)).astype(bf16)


def self_forward_kernel(
    digit_ref, x_ref, seg_ref, par_ref, qkv_w, out_hbm, cross_hbm,
    qkv_hbm, e_hbm, inv_ref, o_hbm, z_hbm, h_hbm, q_hbm,
    qkv_ref, e_ref, o_ref, z_ref, h_ref, q_ref, out_w, cross_w, q_mask, k_mask, sems, e_sems,
):
    step = pl.program_id(0)
    last = pl.num_programs(0) - 1
    length, width = x_ref.shape
    size = width // HEADS
    scale = size**-0.5 * LOG2E
    copy = pltpu.make_async_copy
    loads = [copy(out_hbm, out_w, sems.at[0]), copy(cross_hbm, cross_w, sems.at[1])]
    projected = copy(qkv_ref, qkv_hbm, sems.at[2])

    @pl.when(step == 0)
    def _():
        start(loads)
        x = x_ref[...]
        for part, row in ((0, 0), (1, None), (2, 1)):
            columns = slice(part * width, (part + 1) * width)
            value = dot(qkv_w[:, columns], x, 0, 1)
            if row is not None:
                value = value + column(par_ref[SELF_BIAS + row : SELF_BIAS + row + 1])
            if part == 0:
                value = value * scale
            qkv_ref[columns, :] = value.astype(bf16)
        projected.start()
        same = lax.broadcasted_iota(jnp.int32, (PAD, length), 0) == seg_ref[...]
        q_mask[...] = jnp.where(same, 1.0, 0.0).astype(bf16)
        k_mask[...] = jnp.where(same, 0.0, UNSEEN).astype(bf16)

    causal = lax.broadcasted_iota(jnp.int32, (BLOCK, BLOCK), 0) <= lax.broadcasted_iota(
        jnp.int32, (BLOCK, BLOCK), 1
    )
    blocks = length // BLOCK
    slot = lax.rem(step, 2)

    @pl.when(step >= 2)
    def _():
        wait(score_copies(step - 2, e_ref, e_hbm, e_sems))

    for one in range(PAIR):
        head = step * PAIR + one
        base = pl.multiple_of(head * size, size)
        q = jnp.concatenate((qkv_ref[pl.ds(base, size), :], q_mask[...]), axis=0)
        k = jnp.concatenate((qkv_ref[pl.ds(width + base, size), :], k_mask[...]), axis=0)
        v = with_ones(qkv_ref[pl.ds(2 * width + base, size), :])
        scores, tops, mixed = [], [None] * blocks, [None] * blocks
        for i in range(blocks):
            s = dot(k[:, i * BLOCK : (i + 1) * BLOCK], q[:, i * BLOCK : (i + REACH + 1) * BLOCK], 0, 0)
            diagonal = jnp.where(causal, s[:, :BLOCK], UNSEEN)
            if s.shape[1] > BLOCK:
                diagonal = jnp.concatenate((diagonal, s[:, BLOCK:]), axis=1)
            scores.append(diagonal)
            top = jnp.max(diagonal, axis=0, keepdims=True)
            for b in range(s.shape[1] // BLOCK):
                part = top[:, b * BLOCK : (b + 1) * BLOCK]
                old = tops[i + b]
                tops[i + b] = part if old is None else jnp.maximum(old, part)
        for i, s in enumerate(scores):
            several = s.shape[1] // BLOCK
            weights = jnp.exp2(s - jnp.concatenate(tops[i : i + several], axis=1)).astype(bf16)
            e_ref[slot, one, i, :, : several * BLOCK] = weights
            part = dot(v[:, i * BLOCK : (i + 1) * BLOCK], weights, 1, 0)
            for b in range(several):
                piece = part[:, b * BLOCK : (b + 1) * BLOCK]
                mixed[i + b] = piece if mixed[i + b] is None else mixed[i + b] + piece
        for j, value in enumerate(mixed):
            mine = slice(j * BLOCK, (j + 1) * BLOCK)
            inverse = 1.0 / value[size : size + 1]
            o_ref[pl.ds(base, size), mine] = (value[:size] * inverse).astype(bf16)
            inv_ref[pl.ds(head, 1), mine] = inverse
    start(score_copies(step, e_ref, e_hbm, e_sems))

    @pl.when(step == last)
    def _():
        outs = [
            copy(o_ref, o_hbm, sems.at[3]),
            copy(z_ref, z_hbm, sems.at[4]),
            copy(h_ref, h_hbm, sems.at[5]),
            copy(q_ref, q_hbm, sems.at[6]),
        ]
        outs[0].start()
        wait(loads)
        z = (
            par_ref[OMEGA : OMEGA + 1] * x_ref[...].astype(f32)
            + dot(o_ref[...], out_w[...], 0, 0)
            + par_ref[SELF_OUT_BIAS : SELF_OUT_BIAS + 1]
        )
        z_ref[...] = z
        outs[1].start()
        normal, _ = normalize(z)
        h = (normal * par_ref[GAIN : GAIN + 1] + par_ref[SHIFT : SHIFT + 1]).astype(bf16)
        h_ref[...] = h
        outs[2].start()
        value = dot(cross_w[...], h, 0, 1) + column(par_ref[CROSS_BIAS : CROSS_BIAS + 1])
        q_ref[...] = (value * scale).astype(bf16)
        outs[3].start()
        wait([projected, *outs])
        wait(score_copies(step - 1, e_ref, e_hbm, e_sems))
        wait(score_copies(step, e_ref, e_hbm, e_sems))


def cross_forward_kernel(
    holders, digit_ref, q_ref, par_ref, kv_w, h1_hbm, out_hbm, *refs
):
    pieces, refs = refs[:holders], refs[holders:]
    kv_hbm, e_hbm, inv_ref, o_hbm, z_hbm, h_hbm, *refs = refs
    kv_ref, e_ref, o_ref, z_ref, h_ref, h1_ref, out_w, k_mask, sems, e_sems = refs
    step = pl.program_id(0)
    last = pl.num_programs(0) - 1
    length, width = h1_ref.shape
    size = width // HEADS
    part_rows = pieces[0].shape[0] - PAD
    copy = pltpu.make_async_copy
    loads = [copy(h1_hbm, h1_ref, sems.at[0]), copy(out_hbm, out_w, sems.at[1])]
    projected = copy(kv_ref, kv_hbm, sems.at[2])

    @pl.when(step == 0)
    def _():
        start(loads)
        shift = column(par_ref[CROSS_BIAS + 1 : CROSS_BIAS + 2])
        first = lax.broadcasted_iota(jnp.int32, (PAD, part_rows), 0) == 0
        for b, piece in enumerate(pieces):
            columns = slice(b * part_rows, (b + 1) * part_rows)
            m = piece[:part_rows, :]
            kv_ref[:width, columns] = dot(kv_w[:, :width], m, 0, 1).astype(bf16)
            kv_ref[width:, columns] = (dot(kv_w[:, width:], m, 0, 1) + shift).astype(bf16)
            seen = piece[part_rows:, :part_rows].astype(f32) > 0.5
            k_mask[:, columns] = jnp.where(first & ~seen, UNSEEN, 0.0).astype(bf16)
        projected.start()

    slot = lax.rem(step, 2)

    @pl.when(step >= 2)
    def _():
        wait(score_copies(step - 2, e_ref, e_hbm, e_sems))

    heads = []
    for one in range(PAIR):
        base = pl.multiple_of((step * PAIR + one) * size, size)
        heads.append(
            (
                with_ones(q_ref[one * size : (one + 1) * size, :]),
                jnp.concatenate((kv_ref[pl.ds(base, size), :], k_mask[...]), axis=0),
                with_ones(kv_ref[pl.ds(width + base, size), :]),
            )
        )
    blocks = [slice(i, i + BLOCK) for i in range(0, kv_ref.shape[1], BLOCK)]

    def block_scores(one, block):
        q, k, _ = heads[one]
        scores = dot(k[:, block], q, 0, 0)
        return scores, jnp.max(scores, axis=0, keepdims=True)

    now = [block_scores(0, block) for block in blocks]
    for one in range(PAIR):
        top = functools.reduce(jnp.maximum, [each for _, each in now])
        later, weights = [], []
        for (scores, _), block in zip(now, blocks):
            if one + 1 < PAIR:
                later.append(block_scores(one + 1, block))
            weights.append(jnp.exp2(scores - top).astype(bf16))
            e_ref[slot, one, block, :] = weights[-1]
        mixed = None
        for weight, block in zip(weights, blocks):
            part = dot(heads[one][2][:, block], weight, 1, 0)
            mixed = part if mixed is None else mixed + part
        inverse = 1.0 / mixed[size : size + 1]
        head = step * PAIR + one
        o_ref[pl.ds(pl.multiple_of(head * size, size), size), :] = (mixed[:size] * inverse).astype(
            bf16
        )
        inv_ref[pl.ds(head, 1), :] = inverse
        now = later
    start(score_copies(step, e_ref, e_hbm, e_sems))

    @pl.when(step == last)
    def _():
        outs = [
            copy(o_ref, o_hbm, sems.at[3]),
            copy(z_ref, z_hbm, sems.at[4]),
            copy(h_ref, h_hbm, sems.at[5]),
        ]
        outs[0].start()
        wait(loads)
        z = (
            par_ref[OMEGA + 1 : OMEGA + 2] * h1_ref[...].astype(f32)
            + dot(o_ref[...], out_w[...], 0, 0)
            + par_ref[CROSS_OUT_BIAS : CROSS_OUT_BIAS + 1]
        )
        z_ref[...] = z
        outs[1].start()
        normal, _ = normalize(z)
        h_ref[...] = (
            normal * par_ref[GAIN + 1 : GAIN + 2] + par_ref[SHIFT + 1 : SHIFT + 2]
        ).astype(bf16)
        outs[2].start()
        wait([projected, *outs])
        wait(score_copies(step - 1, e_ref, e_hbm, e_sems))
        wait(score_copies(step, e_ref, e_hbm, e_sems))


def ffn_kernel(
    digit_ref, h2_ref, h1_ref, z2_ref, cot_ref, par_ref, in_w, out_hbm,
    act_ref, dz_ref, keep_hbm, send_hbm, small_ref,
    h_buf, g_buf, slope_buf, e_buf, eu_buf, grad_buf, out_w, sems,
):
    step = pl.program_id(0)
    rows, width = cot_ref.shape
    hidden = in_w.shape[1]
    chunks = hidden // width
    begin = pl.multiple_of(step * rows, rows)
    mine = pl.ds(begin, rows)
    load = pltpu.make_async_copy(out_hbm, out_w, sems.at[2 * chunks])

    @pl.when(step == 0)
    def _():
        load.start()
        small_ref[...] = jnp.zeros_like(small_ref)

    def add(row, value):
        small_ref[row : row + 1] += row_sum(value)

    h2 = h2_ref[...]
    h_buf[mine, :] = h2
    h2_wide = h2.astype(f32)
    for c in range(chunks):
        columns = slice(c * width, (c + 1) * width)
        u = dot(h2, in_w[:, columns], 1, 0) + par_ref[FFN_IN_BIAS + c : FFN_IN_BIAS + c + 1]
        rate = 0.7978845608028654
        square = u * u
        t = jnp.tanh(u * (rate + (rate * 0.044715) * square))
        half = 0.5 + 0.5 * t
        g_buf[mine, columns] = (u * half).astype(bf16)
        slope_buf[:, columns] = half + (0.5 * u) * (1.0 - t * t) * (
            rate + (3 * rate * 0.044715) * square
        )

    @pl.when(step == 0)
    def _():
        load.wait()

    z3 = (
        par_ref[OMEGA + 2 : OMEGA + 3] * h2_wide
        + dot(g_buf[mine, :], out_w[...], 1, 0)
        + par_ref[FFN_OUT_BIAS : FFN_OUT_BIAS + 1]
    )
    normal, inverse = normalize(z3)
    gain = par_ref[GAIN + 2 : GAIN + 3]
    act_ref[...] = (normal * gain + par_ref[SHIFT + 2 : SHIFT + 3]).astype(bf16)
    dy = cot_ref[...].astype(f32)
    add(GAIN + 2, dy * normal)
    add(SHIFT + 2, dy)
    dz3 = normalize_back(dy, gain, normal, inverse)
    add(OMEGA + 2, dz3 * h2_wide)
    e3 = dz3.astype(bf16)
    e_buf[mine, :] = e3
    add(FFN_OUT_BIAS, e3)
    for c in range(chunks):
        columns = slice(c * width, (c + 1) * width)
        eu = (dot(e3, out_w[columns, :], 1, 1) * slope_buf[:, columns]).astype(bf16)
        eu_buf[mine, columns] = eu
        add(FFN_IN_BIAS + c, eu)
    dh2 = par_ref[OMEGA + 2 : OMEGA + 3] * dz3 + dot(eu_buf[mine, :], in_w[...], 1, 1)
    normal, inverse = normalize(z2_ref[...])
    add(GAIN + 1, dh2 * normal)
    add(SHIFT + 1, dh2)
    dz2 = normalize_back(dh2, par_ref[GAIN + 1 : GAIN + 2], normal, inverse)
    add(OMEGA + 1, dz2 * h1_ref[...].astype(f32))
    add(CROSS_OUT_BIAS, dz2.astype(bf16))
    dz_ref[...] = dz2

    @pl.when(step == pl.num_programs(0) - 1)
    def _():
        outs = []
        for half in range(2):
            mine = [c for c in range(chunks) if c // (chunks // 2) == half]
            for i, c in enumerate(mine + [chunks + c for c in mine]):
                columns = slice(c % chunks * width, (c % chunks + 1) * width)
                if c < chunks:
                    value = dot(g_buf[:, columns], e_buf[...], 0, 0)
                else:
                    value = dot(h_buf[...], eu_buf[:, columns], 0, 0)
                place = slice(i * width, (i + 1) * width)
                grad_buf[half, place, :] = value.astype(bf16)
                sem = sems.at[half * chunks + i]
                source = grad_buf.at[half, place]
                keep = pltpu.make_async_copy(source, keep_hbm.at[place], sem)
                send = pltpu.make_async_copy(source, send_hbm.at[place], sem)
                pl.when(digit_ref[0] == half)(keep.start)
                pl.when(digit_ref[0] != half)(send.start)
                outs.append(keep)
        wait(outs)


def back_heads(do_ref, out_w, e, inv_ref):
    value = dot(out_w[...], e, 1, 1)
    size = value.shape[0] // HEADS
    for i in range(HEADS):
        rows = slice(i * size, (i + 1) * size)
        do_ref[rows, :] = (value[rows] * inv_ref[i : i + 1]).astype(bf16)


def back_head(do_rows, o_rows):
    length = do_rows.shape[1]
    delta = jnp.sum(do_rows.astype(f32) * o_rows.astype(f32), axis=0, keepdims=True)
    high = delta.astype(bf16).astype(f32)
    row = lax.broadcasted_iota(jnp.int32, (PAD, length), 0)
    extra = jnp.where(row == 0, -high, jnp.where(row == 1, high - delta, 0.0))
    return jnp.concatenate((do_rows, extra.astype(bf16)), axis=0)


def cross_backward_kernel(
    holders, digit_ref, e_ref, do_ref, o_ref, q_ref, k_ref, v_ref, par_ref, old_ref,
    z1_hbm, h1_hbm, x_hbm, qw_hbm, kw_hbm, dz2_hbm, *refs
):
    m_hbm, refs = refs[:holders], refs[holders:]
    mem_hbm, refs = refs[:holders], refs[holders:]
    dz1_hbm, small_ref, *refs = refs
    keeps, sends, refs = refs[:2], refs[2:4], refs[4:]
    z1_ref, h1_ref, x_ref, q_w, kv_w, dz2_ref, m_ref, mem_ref, *refs = refs
    o_buf, dq_buf, dkv_buf, dz_buf, grad_buf, sems = refs
    step = pl.program_id(0)
    last = pl.num_programs(0) - 1
    length, width = x_ref.shape
    size = width // HEADS
    count = k_ref.shape[1]
    pair = PAIR * size
    part_rows = mem_ref.shape[1]
    copy = pltpu.make_async_copy
    pairs_of = [(z1_hbm, z1_ref), (h1_hbm, h1_ref), (x_hbm, x_ref), (qw_hbm, q_w), (kw_hbm, kv_w)]
    pairs_of += [(dz2_hbm, dz2_ref)]
    pairs_of += [(source.at[:part_rows], m_ref.at[b]) for b, source in enumerate(m_hbm)]
    loads = [copy(source, target, sems.at[i]) for i, (source, target) in enumerate(pairs_of)]

    @pl.when(step == 0)
    def _():
        start(loads)
        small_ref[...] = old_ref[...]

    base = pl.multiple_of(step * pair, pair)
    o_buf[pl.ds(base, pair), :] = o_ref[...]
    heads = []
    for one in range(PAIR):
        here = slice(one * size, (one + 1) * size)
        heads.append(
            (
                back_head(do_ref[here, :], o_ref[here, :]),
                q_ref[here, :],
                k_ref[here, :],
                with_ones(v_ref[here, :]),
            )
        )
    dq = [None] * PAIR
    for i in range(count // BLOCK):
        mine = slice(i * BLOCK, (i + 1) * BLOCK)
        for one, (do, q, k, v) in enumerate(heads):
            weights = e_ref[one, mine, :]
            ds = (weights.astype(f32) * dot(v[:, mine], do, 0, 0)).astype(bf16)
            begin = base + one * size
            dkv_buf[pl.ds(width + begin, size), mine] = dot(do[:size], weights, 1, 1).astype(bf16)
            dkv_buf[pl.ds(begin, size), mine] = (dot(q, ds, 1, 1) * LN2).astype(bf16)
            part = dot(k[:, mine], ds, 1, 0)
            dq[one] = part if i == 0 else dq[one] + part
    for one in range(PAIR):
        dq_buf[pl.ds(base + one * size, size), :] = (dq[one] * size**-0.5).astype(bf16)

    @pl.when(step == last)
    def _():
        wait(loads)
        after = len(loads)
        dq_all = dq_buf[...]
        dh1 = par_ref[OMEGA + 1 : OMEGA + 2] * dz2_ref[...] + dot(dq_all, q_w[...], 0, 1)
        normal, inverse = normalize(z1_ref[...])
        small_ref[GAIN : GAIN + 1] = row_sum(dh1 * normal)
        small_ref[SHIFT : SHIFT + 1] = row_sum(dh1)
        dz1 = normalize_back(dh1, par_ref[GAIN : GAIN + 1], normal, inverse)
        small_ref[OMEGA : OMEGA + 1] = row_sum(dz1 * x_ref[...].astype(f32))
        small_ref[SELF_OUT_BIAS : SELF_OUT_BIAS + 1] = row_sum(dz1.astype(bf16))
        dz_buf[...] = dz1
        outs = [copy(dz_buf, dz1_hbm, sems.at[after])]
        outs[0].start()
        small_ref[CROSS_BIAS : CROSS_BIAS + 1] = feature_sum(dq_all)
        small_ref[CROSS_BIAS + 1 : CROSS_BIAS + 2] = feature_sum(dkv_buf[width:, :])
        grad_buf[:, :width] = dot(h1_ref[...], dq_all, 0, 1).astype(bf16)
        grad_buf[:, width : 2 * width] = dot(
            o_buf[...], dz2_ref[...].astype(bf16), 1, 0
        ).astype(bf16)
        key_grad = value_grad = None
        for b in range(holders):
            columns = slice(b * part_rows, (b + 1) * part_rows)
            dkv = dkv_buf[:, columns]
            k_part = dot(m_ref[b], dkv[:width], 0, 1)
            v_part = dot(m_ref[b], dkv[width:], 0, 1)
            key_grad = k_part if b == 0 else key_grad + k_part
            value_grad = v_part if b == 0 else value_grad + v_part
        grad_buf[:, 2 * width : 3 * width] = key_grad.astype(bf16)
        grad_buf[:, 3 * width :] = value_grad.astype(bf16)
        outs += halves(digit_ref, grad_buf, keeps, sends, sems, after + 1 + holders)
        for b in range(holders):
            dkv = dkv_buf[:, b * part_rows : (b + 1) * part_rows]
            mem_ref[b] = dot(dkv, kv_w[...], 0, 1).astype(bf16)
            outs.append(copy(mem_ref.at[b], mem_hbm[b], sems.at[after + 1 + b]))
            outs[-1].start()
        wait(outs)


def halves(digit_ref, grad_buf, keeps, sends, sems, at):
    rows = grad_buf.shape[0] // 2
    result, begin = [], 0
    for keep, send in zip(keeps, sends):
        columns = slice(begin, begin + keep.shape[1])
        begin += keep.shape[1]
        for i, target in enumerate((keep, send)):
            mine = pl.ds(pl.multiple_of((digit_ref[0] ^ i) * rows, rows), rows)
            sem = sems.at[at + len(result)]
            result.append(pltpu.make_async_copy(grad_buf.at[mine, columns], target, sem))
            result[-1].start()
    return result


def back_start_kernel(digit_ref, dz_ref, inv_ref, out_w, do_ref):
    back_heads(do_ref, out_w, dz_ref[...].astype(bf16), inv_ref)


def self_backward_kernel(
    digit_ref, e_ref, inv_ref, o_ref, q_ref, k_ref, v_ref, dz1_ref, out_w,
    dq_ref, dk_ref, dv_ref, do_buf,
):
    step = pl.program_id(0)
    pair, length = q_ref.shape
    size = pair // PAIR
    blocks = length // BLOCK

    @pl.when(step == 0)
    def _():
        back_heads(do_buf, out_w, dz1_ref[...].astype(bf16), inv_ref)

    base = pl.multiple_of(step * pair, pair)
    for one in range(PAIR):
        here = slice(one * size, (one + 1) * size)
        do = back_head(do_buf[pl.ds(base + one * size, size), :], o_ref[here, :])
        q, k, v = q_ref[here, :], k_ref[here, :], with_ones(v_ref[here, :])
        dq = [None] * blocks
        for i in range(blocks):
            mine = slice(i * BLOCK, (i + 1) * BLOCK)
            several = min(blocks - i, REACH + 1)
            seen = slice(i * BLOCK, (i + several) * BLOCK)
            weights = e_ref[one, i, :, : several * BLOCK]
            ds = (weights.astype(f32) * dot(v[:, mine], do[:, seen], 0, 0)).astype(bf16)
            dv_ref[here, mine] = dot(do[:size, seen], weights, 1, 1).astype(bf16)
            dk_ref[here, mine] = (dot(q[:, seen], ds, 1, 1) * LN2).astype(bf16)
            part = dot(k[:, mine], ds, 1, 0)
            for b in range(several):
                piece = part[:, b * BLOCK : (b + 1) * BLOCK]
                dq[i + b] = piece if dq[i + b] is None else dq[i + b] + piece
        for j in range(blocks):
            dq_ref[here, j * BLOCK : (j + 1) * BLOCK] = (dq[j] * size**-0.5).astype(bf16)


def self_weights_kernel(
    digit_ref, old_ref, x_hbm, dq_hbm, dk_hbm, dv_hbm, dz1_hbm, o_hbm, *refs
):
    keeps, sends, refs = refs[:2], refs[2:4], refs[4:]
    (
        x_ref, dq_ref, dk_ref, dv_ref, dz1_ref, o_ref, grad_buf, sems,
    ) = refs
    width = x_ref.shape[1]
    refs = (x_ref, dq_ref, dk_ref, dv_ref, dz1_ref, o_ref)
    loads = [
        pltpu.make_async_copy(source, target, sems.at[i])
        for i, (source, target) in enumerate(
            zip((x_hbm, dq_hbm, dk_hbm, dv_hbm, dz1_hbm, o_hbm), refs)
        )
    ]
    start(loads)
    loads[0].wait()
    sums = []
    for part, ref in enumerate((dq_ref, dk_ref, dv_ref)):
        loads[1 + part].wait()
        d = ref[...]
        grad_buf[:, (part + 1) * width : (part + 2) * width] = dot(x_ref[...], d, 0, 1).astype(bf16)
        sums.append(feature_sum(d) if part != 1 else None)
    row = lax.broadcasted_iota(jnp.int32, old_ref.shape, 0)
    small = jnp.where(row == SELF_BIAS, sums[0], old_ref[...])
    small = jnp.where(row == SELF_BIAS + 1, sums[2], small)
    small = jnp.concatenate((small, jnp.zeros((LANES - SMALL, width), f32)), axis=0)
    grad_buf[:, 4 * width :] = jnp.transpose(small).astype(bf16)
    wait(loads[4:])
    grad_buf[:, :width] = dot(o_ref[...], dz1_ref[...].astype(bf16), 1, 0).astype(bf16)
    wait(halves(digit_ref, grad_buf, keeps, sends, sems, len(loads)))


def token_kernel(digit_ref, dq_ref, dk_ref, dv_ref, dz1_ref, par_ref, qkv_w, token_ref):
    width = dz1_ref.shape[1]
    total = par_ref[OMEGA : OMEGA + 1] * dz1_ref[...]
    for part, ref in enumerate((dq_ref, dk_ref, dv_ref)):
        total = total + dot(ref[...], qkv_w[:, part * width : (part + 1) * width], 0, 1)
    token_ref[...] = total.astype(bf16)


def tree_sum(values):
    while len(values) > 1:
        values = [a + b for a, b in zip(values[::2], values[1::2])]
    return values[0]


def combine_kernel(stage, outs, groups, *refs):
    sources, results = refs[1 : 1 + sum(groups)], refs[1 + sum(groups) :]
    rows = results[0].shape[0]
    for d in range(outs):
        begin = 0 if outs == 1 else pl.multiple_of((refs[0][stage] ^ d) * rows, rows)
        left, column = list(sources), 0
        for count in groups:
            group, left = left[:count], left[count:]
            total = tree_sum([ref[pl.ds(begin, rows), :].astype(f32) for ref in group])
            width = total.shape[1]
            results[d][:, column : column + width] = total.astype(bf16)
            column += width


def place_kernel(stage, ins, *refs):
    digit, sources, result = refs[0][stage], refs[1 : 1 + ins], refs[1 + ins]
    rows = sources[0].shape[0]
    for d in range(ins):
        result[pl.ds(pl.multiple_of((digit ^ d) * rows, rows), rows), :] = sources[d][...]


def finish_kernel(
    digit_ref, mine_hbm, other_hbm, cross_q, cross_out, cross_kv, self_out, self_qkv,
    self_bias, self_out_bias, cross_bias, cross_out_bias, in_bias, out_bias, omega, gain, shift,
    buf, *refs
):
    targets = (cross_q, cross_out, cross_kv, self_out, self_qkv)
    bufs, sems = refs[: len(targets)], refs[len(targets)]
    rows, width = mine_hbm.shape[0], cross_q.shape[1]
    loads = []
    for i, source in enumerate((mine_hbm, other_hbm)):
        here = pl.ds(pl.multiple_of((digit_ref[0] ^ i) * rows, rows), rows)
        loads.append(pltpu.make_async_copy(source, buf.at[here], sems.at[len(targets) + i]))
    start(loads)
    wait(loads)
    begin, outs = 0, []
    for i, (target, wide) in enumerate(zip(targets, bufs)):
        count = target.shape[1]
        wide[...] = buf[:, begin : begin + count].astype(f32)
        outs.append(pltpu.make_async_copy(wide, target, sems.at[i]))
        outs[-1].start()
        begin += count
    part = jnp.transpose(buf[:, begin:].astype(f32))
    begin = 0
    for target in (
        self_bias, self_out_bias, cross_bias, cross_out_bias, in_bias, out_bias, omega, gain, shift,
    ):
        count = target.shape[0]
        target[...] = part[begin : begin + count]
        begin += count
    wait(outs)


def spread_kernel(stage, digit_ref, *refs):
    *sources, target = refs
    for d, source in enumerate(sources):
        target[digit_ref[stage] ^ d] = source[...]


def ffn_finish_kernel(digit_ref, mine_hbm, other_hbm, out_hbm, in_hbm, buf, out_buf, in_buf, sems):
    rows, width = mine_hbm.shape
    chunks = out_hbm.shape[0] // width
    loads = [
        pltpu.make_async_copy(source, buf.at[digit_ref[0] ^ i], sems.at[2 * chunks + i])
        for i, source in enumerate((mine_hbm, other_hbm))
    ]
    start(loads)
    wait(loads)
    outs = []
    for c in range(chunks):
        half, place = c // (chunks // 2), c % (chunks // 2) * width
        out_buf[c] = buf[half, place : place + width, :].astype(f32)
        place += rows // 2
        in_buf[c] = buf[half, place : place + width, :].astype(f32)
        here = slice(c * width, (c + 1) * width)
        outs.append(pltpu.make_async_copy(out_buf.at[c], out_hbm.at[here], sems.at[2 * c]))
        outs.append(pltpu.make_async_copy(in_buf.at[c], in_hbm.at[:, here], sems.at[2 * c + 1]))
        start(outs[-2:])
    wait(outs)


class Order:
    def __init__(self, digits):
        self.digits = digits

    def after(self, value):
        return lax.optimization_barrier((value, self.digits))[0]

    def through(self, value):
        value, self.digits = lax.optimization_barrier((value, self.digits))
        return value

    def __call__(self, kernel, steps, ins, outs, scratch=(), vmem=VMEM, us=1):
        def whole(shape):
            return pl.BlockSpec(shape, lambda i: (0,) * len(shape), pipeline_mode=pl.Buffered(1))

        arrays, in_specs, shapes, out_specs = (
            [self.digits], [pl.BlockSpec(memory_space=pltpu.SMEM)], [], []
        )
        anywhere = pl.BlockSpec(memory_space=pl.ANY)
        for item in ins:
            if isinstance(item, tuple):
                arrays.append(item[0])
                in_specs.append(pl.BlockSpec(*item[1:]) if item[1:] else anywhere)
            else:
                arrays.append(item)
                in_specs.append(whole(item.shape))
        for shape, dtype, *block in outs:
            shapes.append(jax.ShapeDtypeStruct(shape, dtype))
            if block == [None]:
                out_specs.append(anywhere)
            elif block:
                out_specs.append(pl.BlockSpec(*block))
            else:
                out_specs.append(pl.BlockSpec(shape, lambda i, n=len(shape): (0,) * n))
        result = pl.pallas_call(
            kernel,
            grid=(steps,),
            in_specs=in_specs,
            out_specs=out_specs,
            out_shape=shapes,
            scratch_shapes=list(scratch),
            compiler_params=pltpu.CompilerParams(
                dimension_semantics=("arbitrary",), vmem_limit_bytes=vmem
            ),
            cost_estimate=pl.CostEstimate(flops=us * 10**9, bytes_accessed=0, transcendentals=0),
        )(*arrays)
        self.digits = lax.optimization_barrier((self.digits, result[0]))[0]
        return result


def stages_of(sizes):
    result = []
    for axis in ("dp", "ctx"):
        stride = 1
        while stride < sizes[axis]:
            left = sizes[axis] // stride
            count = 2 if (axis == "dp" and stride == 1) or left % 4 else 4
            result.append((axis, stride, count))
            stride *= count
    return result


class Sum:
    def __init__(self, order, stages, sizes, pieces):
        self.order, self.stages, self.sizes = order, stages, sizes
        self.stage, self.spread, self.pieces, self.others = 0, [], pieces, []
        self.send(0)

    def send(self, stage):
        axis, stride, count = self.stages[stage]
        pieces = self.pieces if len(self.pieces) > 1 else self.pieces * count
        self.got = [
            lax.ppermute(
                pieces[d], axis, [(i, i ^ (d * stride)) for i in range(self.sizes[axis])]
            )
            for d in range(1, count)
        ]

    def settle(self):
        self.spread.append(self.stage)
        self.stage += 1
        group = [self.pieces[0], *self.got]
        self.pieces, self.got = self.order(
            functools.partial(combine_kernel, self.stage, 1, [len(group)]), 1, group,
            [(group[0].shape, bf16)], vmem=SMALL_VMEM,
        ), []

    def join(self, other):
        self.others.append(other)

    def step(self):
        groups = [[one.pieces[0], *one.got] for one in (*self.others, self)]
        rows = groups[0][0].shape[0]
        width = sum(group[0].shape[1] for group in groups)
        outs = 1
        if self.stage < len(self.stages):
            if len(self.pieces) > 1:
                self.spread.append(self.stage)
            self.stage += 1
            if self.stage < len(self.stages):
                count = self.stages[self.stage][2]
                outs = count if rows % (PAD * count) == 0 else 1
            kernel = functools.partial(
                combine_kernel, self.stage, outs, [len(group) for group in groups]
            )
            rows //= outs
        else:
            stage = self.spread.pop()
            kernel = functools.partial(place_kernel, stage, len(groups[0]))
            rows *= len(groups[0])
        self.others = []
        self.pieces = self.order(
            kernel, 1, sum(groups, []), [((rows, width), bf16)] * outs, vmem=SMALL_VMEM
        )
        self.send(self.stage if self.stage < len(self.stages) else self.spread[-1])

    @property
    def last(self):
        return self.stage == len(self.stages) and len(self.spread) == 1


def local(sizes, *args):
    (
        tokens, memory, mem_mask, segment_ids, cotangent, self_qkv, self_bias, self_out,
        self_out_bias, cross_q, cross_kv, cross_bias, cross_out, cross_out_bias, ffn_in,
        ffn_in_bias, ffn_out, ffn_out_bias, omegas, ln_gains, ln_biases,
    ) = args
    length, width = tokens.shape[1:]
    hidden = ffn_in.shape[1]
    size = width // HEADS
    holders, part_rows = memory.shape[:2]
    count = holders * part_rows
    x = tokens.reshape(length, width)
    cot = cotangent.reshape(length, width)
    seg = segment_ids.reshape(1, length)
    stages = stages_of(sizes)
    digits = [(lax.axis_index(axis) // stride) % several for axis, stride, several in stages]
    first_ctx = [axis for axis, _, _ in stages].index("ctx")
    order = Order(jnp.stack(digits).astype(jnp.int32))

    blocks = length // BLOCK
    reach = (REACH + 1) * BLOCK

    pairs, pair = HEADS // PAIR, PAIR * size

    def scores_in(array):
        shape = (PAIR, *array.shape[1:])
        return (array, shape, lambda i: (i,) + (0,) * (len(shape) - 1))

    def scores_out(*shape):
        return ((HEADS, *shape), bf16, None)

    def pair_in(array, part=0):
        return (array, (pair, array.shape[1]), lambda i: (part * pairs + i, 0))

    def vmem(*shape, dtype=bf16):
        return pltpu.VMEM(shape, dtype)

    dma = pltpu.SemaphoreType.DMA
    tall, wide = (width, length), (length, width)
    small, *pieces = order(
        functools.partial(prepare_kernel, first_ctx),
        1,
        [
            memory, mem_mask, self_bias, self_out_bias, cross_bias, cross_out_bias, ffn_in_bias,
            ffn_out_bias, omegas, ln_gains, ln_biases,
        ],
        [((SMALL, width), f32)] + [((part_rows + PAD, width), bf16)] * holders,
    )

    def trade(pieces):
        return [pieces[0]] + [
            lax.ppermute(pieces[d], "ctx", [(i, i ^ d) for i in range(holders)])
            for d in range(1, holders)
        ]

    pieces = trade(pieces)
    qkv, e_self, inv_self, o, z1, h1, q2 = order(
        self_forward_kernel,
        pairs,
        [x, seg, small, self_qkv, (self_out,), (cross_q,)],
        [
            ((3 * width, length), bf16, None),
            scores_out(blocks, BLOCK, reach),
            ((HEADS, length), f32),
            (tall, bf16, None),
            (wide, f32, None),
            (wide, bf16, None),
            (tall, bf16, None),
        ],
        [
            vmem(3 * width, length), vmem(2, PAIR, blocks, BLOCK, reach), vmem(*tall),
            vmem(*wide, dtype=f32), vmem(*wide), vmem(*tall),
            vmem(width, width), vmem(width, width), vmem(PAD, length), vmem(PAD, length), dma((7,)),
            dma((2, PAIR)),
        ],
        us=15,
    )
    kv, e_cross, inv_cross, o2, z2, h2 = order(
        functools.partial(cross_forward_kernel, holders),
        pairs,
        [pair_in(q2), small, cross_kv, (h1,), (cross_out,), *pieces],
        [
            ((2 * width, count), bf16, None),
            scores_out(count, length),
            ((HEADS, length), f32),
            (tall, bf16, None),
            (wide, f32, None),
            (wide, bf16, None),
        ],
        [
            vmem(2 * width, count), vmem(2, PAIR, count, length), vmem(*tall),
            vmem(*wide, dtype=f32), vmem(*wide), vmem(*wide), vmem(width, width), vmem(PAD, count),
            dma((6,)), dma((2, PAIR)),
        ],
        us=22,
    )
    rows = BLOCK
    chunks = hidden // width
    row_block = ((rows, width), lambda i: (i, 0))
    activations, dz2, keep, send, small_grad = order(
        ffn_kernel,
        length // rows,
        [
            (h2, *row_block), (h1, *row_block), (z2, *row_block), (cot, *row_block), small, ffn_in,
            (ffn_out,),
        ],
        [
            (wide, bf16, *row_block),
            (wide, f32, *row_block),
            ((hidden, width), bf16, None),
            ((hidden, width), bf16, None),
            ((SMALL, width), f32),
        ],
        [
            vmem(*wide), vmem(length, hidden), vmem(rows, hidden, dtype=f32), vmem(*wide),
            vmem(length, hidden), vmem(2, hidden, width), vmem(hidden, width),
            dma((2 * chunks + 1,)),
        ],
        us=26,
    )
    def open_sum(parts):
        several = len(parts) // 2
        *others, last = [
            Sum(order, stages, sizes, [keep, send])
            for keep, send in zip(parts[:several], parts[several:])
        ]
        for one in others:
            last.join(one)
        return last

    ffn_sum = open_sum([keep, send])
    (do2,) = order(back_start_kernel, 1, [dz2, inv_cross, cross_out], [(tall, bf16)], us=3)
    ffn_sum.step()
    parts = [((width // 2, 2 * width), bf16, None)] * 4
    *mem_parts, dz1, small_grad, p0, p1, p2, p3 = order(
        functools.partial(cross_backward_kernel, holders),
        pairs,
        [
            scores_in(e_cross), pair_in(do2), pair_in(o2), pair_in(q2), pair_in(kv), pair_in(kv, 1),
            small, small_grad, (z1,), (h1,), (x,), (cross_q,), (cross_kv,), (dz2,),
            *[(piece,) for piece in pieces],
        ],
        [((part_rows, width), bf16, None)] * holders
        + [(wide, f32, None), ((SMALL, width), f32)]
        + parts,
        [
            vmem(*wide, dtype=f32), vmem(*wide), vmem(*wide), vmem(width, width),
            vmem(width, 2 * width), vmem(*wide, dtype=f32), vmem(*memory.shape),
            vmem(*memory.shape), vmem(*tall), vmem(*tall), vmem(2 * width, count),
            vmem(*wide, dtype=f32), vmem(width, 4 * width), dma((6 + 2 * holders + 9,)),
        ],
        us=26,
    )
    cross_sum = open_sum([p0, p1, p2, p3])
    ffn_sum.step()
    cross_sum.step()
    total = 4 * width + LANES
    pair_out = (tall, bf16, (pair, length), lambda i: (i, 0))
    dq, dk, dv = order(
        self_backward_kernel,
        pairs,
        [
            scores_in(e_self), inv_self, pair_in(o), pair_in(qkv), pair_in(qkv, 1), pair_in(qkv, 2),
            dz1, self_out,
        ],
        [pair_out] * 3,
        [vmem(*tall)],
        us=16,
    )
    for _ in range(first_ctx - 2):
        cross_sum.step()
    cross_sum.settle()
    ffn_sum.step()
    parts = [((width // 2, some), bf16, None) for some in (2 * width, 2 * width + LANES)] * 2
    self_sum = open_sum(
        order(
            self_weights_kernel,
            1,
            [small_grad, (x,), (dq,), (dk,), (dv,), (dz1,), (o,)],
            parts,
            [
                vmem(*wide), vmem(*tall), vmem(*tall), vmem(*tall), vmem(*wide, dtype=f32),
                vmem(*tall), vmem(width, total), dma((6 + 10,)),
            ],
            us=7,
        )
    )
    for _ in range(first_ctx - 1):
        self_sum.step()
    self_sum.join(cross_sum)
    self_sum.step()
    ffn_sum.step()
    self_sum.step()
    turned = ((width, rows), lambda i: (0, i))
    (token_grad,) = order(
        token_kernel,
        length // rows,
        [(dq, *turned), (dk, *turned), (dv, *turned), (dz1, *row_block), small, self_qkv],
        [(wide, bf16, *row_block)],
        us=6,
    )
    while not ffn_sum.last:
        ffn_sum.step()
    while len(self_sum.spread) > 2 or self_sum.stage < len(stages):
        self_sum.step()
    mem_parts = trade(order.after(mem_parts))
    (memory_grad,) = order(
        functools.partial(spread_kernel, first_ctx), 1, mem_parts, [(memory.shape, bf16)],
        vmem=SMALL_VMEM,
    )
    self_sum.step()
    while not self_sum.last:
        self_sum.step()
    square = (width, width)
    grad_ffn_out, grad_ffn_in = order(
        ffn_finish_kernel,
        1,
        [(ffn_sum.pieces[0],), (ffn_sum.got[0],)],
        [((hidden, width), f32, None), ((width, hidden), f32, None)],
        [
            vmem(2, hidden, width), vmem(chunks, *square, dtype=f32),
            vmem(chunks, *square, dtype=f32), dma((2 * chunks + 2,)),
        ],
        vmem=SMALL_VMEM,
    )
    shapes = [(width, several * width) for several in (1, 1, 2, 1, 3)]
    shapes += [(several, width) for several in (2, 1, 2, 1, chunks, 1, 3, 3, 3)]
    large = [shape for shape in shapes if shape[0] == width]
    grad_cross_q, grad_cross_out, grad_cross_kv, grad_out, grad_qkv, *smalls = order(
        finish_kernel,
        1,
        [(self_sum.pieces[0],), (self_sum.got[0],)],
        [(shape, f32, None) if shape in large else (shape, f32) for shape in shapes],
        [vmem(width, 8 * width + LANES), *[vmem(*shape, dtype=f32) for shape in large], dma((7,))],
        vmem=SMALL_VMEM,
    )
    (
        self_bias, self_out_bias, cross_bias, cross_out_bias, in_bias, out_bias, omega, gain, shift
    ) = smalls
    return (
        activations.reshape(tokens.shape),
        token_grad.reshape(tokens.shape),
        memory_grad,
        grad_qkv,
        self_bias,
        grad_out,
        self_out_bias.reshape(-1),
        grad_cross_q,
        grad_cross_kv,
        cross_bias,
        grad_cross_out,
        cross_out_bias.reshape(-1),
        grad_ffn_in,
        in_bias.reshape(-1),
        grad_ffn_out,
        out_bias.reshape(-1),
        omega,
        gain,
        shift,
    )


def solution(mesh):
    sizes = dict(mesh.shape)
    both = P(("dp", "ctx"), None, None)
    return jax.shard_map(
        functools.partial(local, sizes),
        mesh=mesh,
        in_specs=(both, P("dp", "ctx", None), P("dp", "ctx"), P(("dp", "ctx"), None), both)
        + (P(),) * 16,
        out_specs=(both, both, P("dp", "ctx", None)) + (P(),) * 16,
        check_vma=False,
    )
```

```python
import functools

import jax
import jax.numpy as jnp
from jax import lax
from jax.experimental import pallas as pl
from jax.experimental.pallas import tpu as pltpu
from jax.sharding import PartitionSpec as P

HEADS = 8
PAIR = 2
LOG2E = 1.4426950408889634
LN2 = 0.6931471805599453
UNSEEN = -1e30
BLOCK = 256
REACH = 2
PAD = 16
VMEM = 60 * 2**20
SMALL_VMEM = 24 * 2**20
bf16, f32 = jnp.bfloat16, jnp.float32

SELF_BIAS, SELF_OUT_BIAS, CROSS_BIAS, CROSS_OUT_BIAS = 0, 2, 3, 5
FFN_IN_BIAS, FFN_OUT_BIAS, OMEGA, GAIN, SHIFT, SMALL = 6, 10, 11, 14, 17, 24
LANES = 128


def dot(left, right, left_dim, right_dim):
    return lax.dot_general(
        left, right, (((left_dim,), (right_dim,)), ((), ())), preferred_element_type=f32
    )


def column(row):
    return jnp.transpose(jnp.broadcast_to(row, (8, row.shape[1])))[:, :1]


def row_sum(value):
    return jnp.sum(value.astype(f32), axis=0, keepdims=True)


def feature_sum(value):
    ones = jnp.ones((PAD, value.shape[1]), bf16)
    return dot(ones, value, 1, 1)[:1]


def normalize(value):
    centered = value - jnp.mean(value, axis=-1, keepdims=True)
    spread = jnp.mean(centered * centered, axis=-1, keepdims=True)
    inverse = lax.rsqrt(spread + 1e-05)
    return centered * inverse, inverse


def normalize_back(grad, gain, normal, inverse):
    scaled = grad * gain
    mean = jnp.mean(scaled, axis=-1, keepdims=True)
    slope = jnp.mean(scaled * normal, axis=-1, keepdims=True)
    return (scaled - mean - normal * slope) * inverse


def with_ones(rows):
    return jnp.concatenate((rows, jnp.ones((PAD, rows.shape[1]), bf16)), axis=0)


def start(copies):
    for copy in copies:
        copy.start()


def wait(copies):
    for copy in copies:
        copy.wait()


def score_copies(step, buf, hbm, sems):
    slot = lax.rem(step, 2)
    return [
        pltpu.make_async_copy(buf.at[slot, one], hbm.at[step * PAIR + one], sems.at[slot, one])
        for one in range(PAIR)
    ]


def prepare_kernel(stage, digit_ref, memory_ref, mask_ref, *refs):
    _, part_rows, width = memory_ref.shape
    params, par_ref, pieces = refs[:9], refs[9], refs[10:]
    row = 0
    for ref in params:
        value = ref[...].astype(f32)
        if value.ndim == 2:
            par_ref[row : row + value.shape[0], :] = value
            row += value.shape[0]
        else:
            for begin in range(0, value.shape[0], width):
                par_ref[row : row + 1, :] = value[begin : begin + width].reshape(1, width)
                row += 1
    par_ref[row:, :] = jnp.zeros((par_ref.shape[0] - row, width), f32)
    for d, piece in enumerate(pieces):
        index = digit_ref[stage] ^ d
        piece[:part_rows, :] = memory_ref[index]
        mask = mask_ref[pl.ds(index, 1), :].astype(f32)
        mask = jnp.concatenate((mask, jnp.zeros((1, width - part_rows), f32)), axis=1)
        piece[part_rows:, :] = jnp.broadcast_to(mask, (PAD, width)).astype(bf16)


def self_forward_kernel(
    digit_ref, x_ref, seg_ref, par_ref, qkv_w, out_hbm, cross_hbm,
    qkv_hbm, e_hbm, inv_ref, o_hbm, z_hbm, h_hbm, q_hbm,
    qkv_ref, e_ref, o_ref, z_ref, h_ref, q_ref, out_w, cross_w, q_mask, k_mask, sems, e_sems,
):
    step = pl.program_id(0)
    last = pl.num_programs(0) - 1
    length, width = x_ref.shape
    size = width // HEADS
    scale = size**-0.5 * LOG2E
    copy = pltpu.make_async_copy
    loads = [copy(out_hbm, out_w, sems.at[0]), copy(cross_hbm, cross_w, sems.at[1])]
    projected = copy(qkv_ref, qkv_hbm, sems.at[2])

    @pl.when(step == 0)
    def _():
        start(loads)
        x = x_ref[...]
        for part, row in ((0, 0), (1, None), (2, 1)):
            columns = slice(part * width, (part + 1) * width)
            value = dot(qkv_w[:, columns], x, 0, 1)
            if row is not None:
                value = value + column(par_ref[SELF_BIAS + row : SELF_BIAS + row + 1])
            if part == 0:
                value = value * scale
            qkv_ref[columns, :] = value.astype(bf16)
        projected.start()
        same = lax.broadcasted_iota(jnp.int32, (PAD, length), 0) == seg_ref[...]
        q_mask[...] = jnp.where(same, 1.0, 0.0).astype(bf16)
        k_mask[...] = jnp.where(same, 0.0, UNSEEN).astype(bf16)

    causal = lax.broadcasted_iota(jnp.int32, (BLOCK, BLOCK), 0) <= lax.broadcasted_iota(
        jnp.int32, (BLOCK, BLOCK), 1
    )
    blocks = length // BLOCK
    slot = lax.rem(step, 2)

    @pl.when(step >= 2)
    def _():
        wait(score_copies(step - 2, e_ref, e_hbm, e_sems))

    for one in range(PAIR):
        head = step * PAIR + one
        base = pl.multiple_of(head * size, size)
        q = jnp.concatenate((qkv_ref[pl.ds(base, size), :], q_mask[...]), axis=0)
        k = jnp.concatenate((qkv_ref[pl.ds(width + base, size), :], k_mask[...]), axis=0)
        v = with_ones(qkv_ref[pl.ds(2 * width + base, size), :])
        scores, tops, mixed = [], [None] * blocks, [None] * blocks
        for i in range(blocks):
            s = dot(k[:, i * BLOCK : (i + 1) * BLOCK], q[:, i * BLOCK : (i + REACH + 1) * BLOCK], 0, 0)
            diagonal = jnp.where(causal, s[:, :BLOCK], UNSEEN)
            if s.shape[1] > BLOCK:
                diagonal = jnp.concatenate((diagonal, s[:, BLOCK:]), axis=1)
            scores.append(diagonal)
            top = jnp.max(diagonal, axis=0, keepdims=True)
            for b in range(s.shape[1] // BLOCK):
                part = top[:, b * BLOCK : (b + 1) * BLOCK]
                old = tops[i + b]
                tops[i + b] = part if old is None else jnp.maximum(old, part)
        for i, s in enumerate(scores):
            several = s.shape[1] // BLOCK
            weights = jnp.exp2(s - jnp.concatenate(tops[i : i + several], axis=1)).astype(bf16)
            e_ref[slot, one, i, :, : several * BLOCK] = weights
            part = dot(v[:, i * BLOCK : (i + 1) * BLOCK], weights, 1, 0)
            for b in range(several):
                piece = part[:, b * BLOCK : (b + 1) * BLOCK]
                mixed[i + b] = piece if mixed[i + b] is None else mixed[i + b] + piece
        for j, value in enumerate(mixed):
            mine = slice(j * BLOCK, (j + 1) * BLOCK)
            inverse = 1.0 / value[size : size + 1]
            o_ref[pl.ds(base, size), mine] = (value[:size] * inverse).astype(bf16)
            inv_ref[pl.ds(head, 1), mine] = inverse
    start(score_copies(step, e_ref, e_hbm, e_sems))

    @pl.when(step == last)
    def _():
        outs = [
            copy(o_ref, o_hbm, sems.at[3]),
            copy(z_ref, z_hbm, sems.at[4]),
            copy(h_ref, h_hbm, sems.at[5]),
            copy(q_ref, q_hbm, sems.at[6]),
        ]
        outs[0].start()
        wait(loads)
        z = (
            par_ref[OMEGA : OMEGA + 1] * x_ref[...].astype(f32)
            + dot(o_ref[...], out_w[...], 0, 0)
            + par_ref[SELF_OUT_BIAS : SELF_OUT_BIAS + 1]
        )
        z_ref[...] = z
        outs[1].start()
        normal, _ = normalize(z)
        h = (normal * par_ref[GAIN : GAIN + 1] + par_ref[SHIFT : SHIFT + 1]).astype(bf16)
        h_ref[...] = h
        outs[2].start()
        value = dot(cross_w[...], h, 0, 1) + column(par_ref[CROSS_BIAS : CROSS_BIAS + 1])
        q_ref[...] = (value * scale).astype(bf16)
        outs[3].start()
        wait([projected, *outs])
        wait(score_copies(step - 1, e_ref, e_hbm, e_sems))
        wait(score_copies(step, e_ref, e_hbm, e_sems))


def cross_forward_kernel(
    holders, digit_ref, q_ref, par_ref, kv_w, h1_hbm, out_hbm, *refs
):
    pieces, refs = refs[:holders], refs[holders:]
    kv_hbm, e_hbm, inv_ref, o_hbm, z_hbm, h_hbm, *refs = refs
    kv_ref, e_ref, o_ref, z_ref, h_ref, h1_ref, out_w, k_mask, sems, e_sems = refs
    step = pl.program_id(0)
    last = pl.num_programs(0) - 1
    length, width = h1_ref.shape
    size = width // HEADS
    part_rows = pieces[0].shape[0] - PAD
    copy = pltpu.make_async_copy
    loads = [copy(h1_hbm, h1_ref, sems.at[0]), copy(out_hbm, out_w, sems.at[1])]
    projected = copy(kv_ref, kv_hbm, sems.at[2])

    @pl.when(step == 0)
    def _():
        start(loads)
        shift = column(par_ref[CROSS_BIAS + 1 : CROSS_BIAS + 2])
        first = lax.broadcasted_iota(jnp.int32, (PAD, part_rows), 0) == 0
        for b, piece in enumerate(pieces):
            columns = slice(b * part_rows, (b + 1) * part_rows)
            m = piece[:part_rows, :]
            kv_ref[:width, columns] = dot(kv_w[:, :width], m, 0, 1).astype(bf16)
            kv_ref[width:, columns] = (dot(kv_w[:, width:], m, 0, 1) + shift).astype(bf16)
            seen = piece[part_rows:, :part_rows].astype(f32) > 0.5
            k_mask[:, columns] = jnp.where(first & ~seen, UNSEEN, 0.0).astype(bf16)
        projected.start()

    slot = lax.rem(step, 2)

    @pl.when(step >= 2)
    def _():
        wait(score_copies(step - 2, e_ref, e_hbm, e_sems))

    heads = []
    for one in range(PAIR):
        base = pl.multiple_of((step * PAIR + one) * size, size)
        heads.append(
            (
                with_ones(q_ref[one * size : (one + 1) * size, :]),
                jnp.concatenate((kv_ref[pl.ds(base, size), :], k_mask[...]), axis=0),
                with_ones(kv_ref[pl.ds(width + base, size), :]),
            )
        )
    blocks = [slice(i, i + BLOCK) for i in range(0, kv_ref.shape[1], BLOCK)]

    def block_scores(one, block):
        q, k, _ = heads[one]
        scores = dot(k[:, block], q, 0, 0)
        return scores, jnp.max(scores, axis=0, keepdims=True)

    now = [block_scores(0, block) for block in blocks]
    for one in range(PAIR):
        top = functools.reduce(jnp.maximum, [each for _, each in now])
        later, weights = [], []
        for (scores, _), block in zip(now, blocks):
            if one + 1 < PAIR:
                later.append(block_scores(one + 1, block))
            weights.append(jnp.exp2(scores - top).astype(bf16))
            e_ref[slot, one, block, :] = weights[-1]
        mixed = None
        for weight, block in zip(weights, blocks):
            part = dot(heads[one][2][:, block], weight, 1, 0)
            mixed = part if mixed is None else mixed + part
        inverse = 1.0 / mixed[size : size + 1]
        head = step * PAIR + one
        o_ref[pl.ds(pl.multiple_of(head * size, size), size), :] = (mixed[:size] * inverse).astype(
            bf16
        )
        inv_ref[pl.ds(head, 1), :] = inverse
        now = later
    start(score_copies(step, e_ref, e_hbm, e_sems))

    @pl.when(step == last)
    def _():
        outs = [
            copy(o_ref, o_hbm, sems.at[3]),
            copy(z_ref, z_hbm, sems.at[4]),
            copy(h_ref, h_hbm, sems.at[5]),
        ]
        outs[0].start()
        wait(loads)
        z = (
            par_ref[OMEGA + 1 : OMEGA + 2] * h1_ref[...].astype(f32)
            + dot(o_ref[...], out_w[...], 0, 0)
            + par_ref[CROSS_OUT_BIAS : CROSS_OUT_BIAS + 1]
        )
        z_ref[...] = z
        outs[1].start()
        normal, _ = normalize(z)
        h_ref[...] = (
            normal * par_ref[GAIN + 1 : GAIN + 2] + par_ref[SHIFT + 1 : SHIFT + 2]
        ).astype(bf16)
        outs[2].start()
        wait([projected, *outs])
        wait(score_copies(step - 1, e_ref, e_hbm, e_sems))
        wait(score_copies(step, e_ref, e_hbm, e_sems))


def ffn_kernel(
    digit_ref, h2_ref, h1_ref, z2_ref, cot_ref, par_ref, in_w, out_hbm,
    act_ref, dz_ref, keep_hbm, send_hbm, small_ref,
    h_buf, g_buf, slope_buf, e_buf, eu_buf, grad_buf, out_w, sems,
):
    step = pl.program_id(0)
    rows, width = cot_ref.shape
    hidden = in_w.shape[1]
    chunks = hidden // width
    begin = pl.multiple_of(step * rows, rows)
    mine = pl.ds(begin, rows)
    load = pltpu.make_async_copy(out_hbm, out_w, sems.at[2 * chunks])

    @pl.when(step == 0)
    def _():
        load.start()
        small_ref[...] = jnp.zeros_like(small_ref)

    def add(row, value):
        small_ref[row : row + 1] += row_sum(value)

    h2 = h2_ref[...]
    h_buf[mine, :] = h2
    h2_wide = h2.astype(f32)
    for c in range(chunks):
        columns = slice(c * width, (c + 1) * width)
        u = dot(h2, in_w[:, columns], 1, 0) + par_ref[FFN_IN_BIAS + c : FFN_IN_BIAS + c + 1]
        rate = 0.7978845608028654
        square = u * u
        t = jnp.tanh(u * (rate + (rate * 0.044715) * square))
        half = 0.5 + 0.5 * t
        g_buf[mine, columns] = (u * half).astype(bf16)
        slope_buf[:, columns] = half + (0.5 * u) * (1.0 - t * t) * (
            rate + (3 * rate * 0.044715) * square
        )

    @pl.when(step == 0)
    def _():
        load.wait()

    z3 = (
        par_ref[OMEGA + 2 : OMEGA + 3] * h2_wide
        + dot(g_buf[mine, :], out_w[...], 1, 0)
        + par_ref[FFN_OUT_BIAS : FFN_OUT_BIAS + 1]
    )
    normal, inverse = normalize(z3)
    gain = par_ref[GAIN + 2 : GAIN + 3]
    act_ref[...] = (normal * gain + par_ref[SHIFT + 2 : SHIFT + 3]).astype(bf16)
    dy = cot_ref[...].astype(f32)
    add(GAIN + 2, dy * normal)
    add(SHIFT + 2, dy)
    dz3 = normalize_back(dy, gain, normal, inverse)
    add(OMEGA + 2, dz3 * h2_wide)
    e3 = dz3.astype(bf16)
    e_buf[mine, :] = e3
    add(FFN_OUT_BIAS, e3)
    for c in range(chunks):
        columns = slice(c * width, (c + 1) * width)
        eu = (dot(e3, out_w[columns, :], 1, 1) * slope_buf[:, columns]).astype(bf16)
        eu_buf[mine, columns] = eu
        add(FFN_IN_BIAS + c, eu)
    dh2 = par_ref[OMEGA + 2 : OMEGA + 3] * dz3 + dot(eu_buf[mine, :], in_w[...], 1, 1)
    normal, inverse = normalize(z2_ref[...])
    add(GAIN + 1, dh2 * normal)
    add(SHIFT + 1, dh2)
    dz2 = normalize_back(dh2, par_ref[GAIN + 1 : GAIN + 2], normal, inverse)
    add(OMEGA + 1, dz2 * h1_ref[...].astype(f32))
    add(CROSS_OUT_BIAS, dz2.astype(bf16))
    dz_ref[...] = dz2

    @pl.when(step == pl.num_programs(0) - 1)
    def _():
        outs = []
        for half in range(2):
            mine = [c for c in range(chunks) if c // (chunks // 2) == half]
            for i, c in enumerate(mine + [chunks + c for c in mine]):
                columns = slice(c % chunks * width, (c % chunks + 1) * width)
                if c < chunks:
                    value = dot(g_buf[:, columns], e_buf[...], 0, 0)
                else:
                    value = dot(h_buf[...], eu_buf[:, columns], 0, 0)
                place = slice(i * width, (i + 1) * width)
                grad_buf[half, place, :] = value.astype(bf16)
                sem = sems.at[half * chunks + i]
                source = grad_buf.at[half, place]
                keep = pltpu.make_async_copy(source, keep_hbm.at[place], sem)
                send = pltpu.make_async_copy(source, send_hbm.at[place], sem)
                pl.when(digit_ref[0] == half)(keep.start)
                pl.when(digit_ref[0] != half)(send.start)
                outs.append(keep)
        wait(outs)


def back_heads(do_ref, out_w, e, inv_ref):
    value = dot(out_w[...], e, 1, 1)
    size = value.shape[0] // HEADS
    for i in range(HEADS):
        rows = slice(i * size, (i + 1) * size)
        do_ref[rows, :] = (value[rows] * inv_ref[i : i + 1]).astype(bf16)


def back_head(do_rows, o_rows):
    length = do_rows.shape[1]
    delta = jnp.sum(do_rows.astype(f32) * o_rows.astype(f32), axis=0, keepdims=True)
    high = delta.astype(bf16).astype(f32)
    row = lax.broadcasted_iota(jnp.int32, (PAD, length), 0)
    extra = jnp.where(row == 0, -high, jnp.where(row == 1, high - delta, 0.0))
    return jnp.concatenate((do_rows, extra.astype(bf16)), axis=0)


def cross_backward_kernel(
    holders, digit_ref, e_ref, do_ref, o_ref, q_ref, k_ref, v_ref, par_ref, old_ref,
    z1_hbm, h1_hbm, x_hbm, qw_hbm, dz2_hbm, *refs
):
    m_hbm, refs = refs[:holders], refs[holders:]
    dkv_hbm, dz1_hbm, small_ref, *refs = refs
    keeps, sends, refs = refs[:2], refs[2:4], refs[4:]
    z1_ref, h1_ref, x_ref, q_w, dz2_ref, m_ref, *refs = refs
    o_buf, dq_buf, dkv_buf, dz_buf, grad_buf, sems = refs
    step = pl.program_id(0)
    last = pl.num_programs(0) - 1
    length, width = x_ref.shape
    size = width // HEADS
    count = k_ref.shape[1]
    pair = PAIR * size
    part_rows = m_ref.shape[1]
    copy = pltpu.make_async_copy
    pairs_of = [(z1_hbm, z1_ref), (h1_hbm, h1_ref), (x_hbm, x_ref), (qw_hbm, q_w)]
    pairs_of += [(dz2_hbm, dz2_ref)]
    pairs_of += [(source.at[:part_rows], m_ref.at[b]) for b, source in enumerate(m_hbm)]
    loads = [copy(source, target, sems.at[i]) for i, (source, target) in enumerate(pairs_of)]

    def part_out(at, which):
        rows = pl.ds(pl.multiple_of(which * width + at * pair, pair), pair)
        return copy(dkv_buf.at[rows], dkv_hbm.at[rows], sems.at[len(loads) + 5 + 2 * at + which])

    @pl.when(step == 0)
    def _():
        start(loads)
        small_ref[...] = old_ref[...]

    base = pl.multiple_of(step * pair, pair)
    o_buf[pl.ds(base, pair), :] = o_ref[...]
    heads = []
    for one in range(PAIR):
        here = slice(one * size, (one + 1) * size)
        heads.append(
            (
                back_head(do_ref[here, :], o_ref[here, :]),
                q_ref[here, :],
                k_ref[here, :],
                with_ones(v_ref[here, :]),
            )
        )
    dq = [None] * PAIR
    for i in range(count // BLOCK):
        mine = slice(i * BLOCK, (i + 1) * BLOCK)
        for one, (do, q, k, v) in enumerate(heads):
            weights = e_ref[one, mine, :]
            ds = (weights.astype(f32) * dot(v[:, mine], do, 0, 0)).astype(bf16)
            begin = base + one * size
            dkv_buf[pl.ds(width + begin, size), mine] = dot(do[:size], weights, 1, 1).astype(bf16)
            dkv_buf[pl.ds(begin, size), mine] = (dot(q, ds, 1, 1) * LN2).astype(bf16)
            part = dot(k[:, mine], ds, 1, 0)
            dq[one] = part if i == 0 else dq[one] + part
    for one in range(PAIR):
        dq_buf[pl.ds(base + one * size, size), :] = (dq[one] * size**-0.5).astype(bf16)
    start([part_out(step, 0), part_out(step, 1)])

    @pl.when(step == last)
    def _():
        wait(loads)
        after = len(loads)
        dq_all = dq_buf[...]
        dh1 = par_ref[OMEGA + 1 : OMEGA + 2] * dz2_ref[...] + dot(dq_all, q_w[...], 0, 1)
        normal, inverse = normalize(z1_ref[...])
        small_ref[GAIN : GAIN + 1] = row_sum(dh1 * normal)
        small_ref[SHIFT : SHIFT + 1] = row_sum(dh1)
        dz1 = normalize_back(dh1, par_ref[GAIN : GAIN + 1], normal, inverse)
        small_ref[OMEGA : OMEGA + 1] = row_sum(dz1 * x_ref[...].astype(f32))
        small_ref[SELF_OUT_BIAS : SELF_OUT_BIAS + 1] = row_sum(dz1.astype(bf16))
        dz_buf[...] = dz1
        outs = [copy(dz_buf, dz1_hbm, sems.at[after])]
        outs[0].start()
        small_ref[CROSS_BIAS : CROSS_BIAS + 1] = feature_sum(dq_all)
        small_ref[CROSS_BIAS + 1 : CROSS_BIAS + 2] = feature_sum(dkv_buf[width:, :])
        grad_buf[:, :width] = dot(h1_ref[...], dq_all, 0, 1).astype(bf16)
        grad_buf[:, width : 2 * width] = dot(
            o_buf[...], dz2_ref[...].astype(bf16), 1, 0
        ).astype(bf16)
        key_grad = value_grad = None
        for b in range(holders):
            columns = slice(b * part_rows, (b + 1) * part_rows)
            dkv = dkv_buf[:, columns]
            k_part = dot(m_ref[b], dkv[:width], 0, 1)
            v_part = dot(m_ref[b], dkv[width:], 0, 1)
            key_grad = k_part if b == 0 else key_grad + k_part
            value_grad = v_part if b == 0 else value_grad + v_part
        grad_buf[:, 2 * width : 3 * width] = key_grad.astype(bf16)
        grad_buf[:, 3 * width :] = value_grad.astype(bf16)
        outs += halves(digit_ref, grad_buf, keeps, sends, sems, after + 1)
        outs += [part_out(at, which) for at in range(HEADS // PAIR) for which in range(2)]
        wait(outs)


def halves(digit_ref, grad_buf, keeps, sends, sems, at):
    rows = grad_buf.shape[0] // 2
    result, begin = [], 0
    for keep, send in zip(keeps, sends):
        columns = slice(begin, begin + keep.shape[1])
        begin += keep.shape[1]
        for i, target in enumerate((keep, send)):
            mine = pl.ds(pl.multiple_of((digit_ref[0] ^ i) * rows, rows), rows)
            sem = sems.at[at + len(result)]
            result.append(pltpu.make_async_copy(grad_buf.at[mine, columns], target, sem))
            result[-1].start()
    return result


def back_start_kernel(digit_ref, dz_ref, inv_ref, out_w, do_ref):
    back_heads(do_ref, out_w, dz_ref[...].astype(bf16), inv_ref)


def self_backward_kernel(
    digit_ref, e_ref, inv_ref, o_ref, q_ref, k_ref, v_ref, dz1_ref, out_w,
    dq_ref, dk_ref, dv_ref, do_buf,
):
    step = pl.program_id(0)
    pair, length = q_ref.shape
    size = pair // PAIR
    blocks = length // BLOCK

    @pl.when(step == 0)
    def _():
        back_heads(do_buf, out_w, dz1_ref[...].astype(bf16), inv_ref)

    base = pl.multiple_of(step * pair, pair)
    for one in range(PAIR):
        here = slice(one * size, (one + 1) * size)
        do = back_head(do_buf[pl.ds(base + one * size, size), :], o_ref[here, :])
        q, k, v = q_ref[here, :], k_ref[here, :], with_ones(v_ref[here, :])
        dq = [None] * blocks
        for i in range(blocks):
            mine = slice(i * BLOCK, (i + 1) * BLOCK)
            several = min(blocks - i, REACH + 1)
            seen = slice(i * BLOCK, (i + several) * BLOCK)
            weights = e_ref[one, i, :, : several * BLOCK]
            ds = (weights.astype(f32) * dot(v[:, mine], do[:, seen], 0, 0)).astype(bf16)
            dv_ref[here, mine] = dot(do[:size, seen], weights, 1, 1).astype(bf16)
            dk_ref[here, mine] = (dot(q[:, seen], ds, 1, 1) * LN2).astype(bf16)
            part = dot(k[:, mine], ds, 1, 0)
            for b in range(several):
                piece = part[:, b * BLOCK : (b + 1) * BLOCK]
                dq[i + b] = piece if dq[i + b] is None else dq[i + b] + piece
        for j in range(blocks):
            dq_ref[here, j * BLOCK : (j + 1) * BLOCK] = (dq[j] * size**-0.5).astype(bf16)


def self_weights_kernel(
    digit_ref, old_ref, x_hbm, dq_hbm, dk_hbm, dv_hbm, dz1_hbm, o_hbm, *refs
):
    keeps, sends, refs = refs[:2], refs[2:4], refs[4:]
    (
        x_ref, dq_ref, dk_ref, dv_ref, dz1_ref, o_ref, grad_buf, sems,
    ) = refs
    width = x_ref.shape[1]
    refs = (x_ref, dq_ref, dk_ref, dv_ref, dz1_ref, o_ref)
    loads = [
        pltpu.make_async_copy(source, target, sems.at[i])
        for i, (source, target) in enumerate(
            zip((x_hbm, dq_hbm, dk_hbm, dv_hbm, dz1_hbm, o_hbm), refs)
        )
    ]
    start(loads)
    loads[0].wait()
    sums = []
    for part, ref in enumerate((dq_ref, dk_ref, dv_ref)):
        loads[1 + part].wait()
        d = ref[...]
        grad_buf[:, (part + 1) * width : (part + 2) * width] = dot(x_ref[...], d, 0, 1).astype(bf16)
        sums.append(feature_sum(d) if part != 1 else None)
    row = lax.broadcasted_iota(jnp.int32, old_ref.shape, 0)
    small = jnp.where(row == SELF_BIAS, sums[0], old_ref[...])
    small = jnp.where(row == SELF_BIAS + 1, sums[2], small)
    small = jnp.concatenate((small, jnp.zeros((LANES - SMALL, width), f32)), axis=0)
    grad_buf[:, 4 * width :] = jnp.transpose(small).astype(bf16)
    wait(loads[4:])
    grad_buf[:, :width] = dot(o_ref[...], dz1_ref[...].astype(bf16), 1, 0).astype(bf16)
    wait(halves(digit_ref, grad_buf, keeps, sends, sems, len(loads)))


def memory_kernel(digit_ref, dkv_ref, kv_w, *mem_refs):
    rows = mem_refs[0].shape[0]
    for b, mem_ref in enumerate(mem_refs):
        part = dkv_ref[:, b * rows : (b + 1) * rows]
        mem_ref[...] = dot(part, kv_w[...], 0, 1).astype(bf16)


def token_kernel(digit_ref, dq_ref, dk_ref, dv_ref, dz1_ref, par_ref, qkv_w, token_ref):
    width = dz1_ref.shape[1]
    total = par_ref[OMEGA : OMEGA + 1] * dz1_ref[...]
    for part, ref in enumerate((dq_ref, dk_ref, dv_ref)):
        total = total + dot(ref[...], qkv_w[:, part * width : (part + 1) * width], 0, 1)
    token_ref[...] = total.astype(bf16)


def tree_sum(values):
    while len(values) > 1:
        values = [a + b for a, b in zip(values[::2], values[1::2])]
    return values[0]


def combine_kernel(stage, outs, groups, *refs):
    sources, results = refs[1 : 1 + sum(groups)], refs[1 + sum(groups) :]
    rows = results[0].shape[0]
    for d in range(outs):
        begin = 0 if outs == 1 else pl.multiple_of((refs[0][stage] ^ d) * rows, rows)
        left, column = list(sources), 0
        for count in groups:
            group, left = left[:count], left[count:]
            total = tree_sum([ref[pl.ds(begin, rows), :].astype(f32) for ref in group])
            width = total.shape[1]
            results[d][:, column : column + width] = total.astype(bf16)
            column += width


def place_kernel(stage, ins, *refs):
    digit, sources, result = refs[0][stage], refs[1 : 1 + ins], refs[1 + ins]
    rows = sources[0].shape[0]
    for d in range(ins):
        result[pl.ds(pl.multiple_of((digit ^ d) * rows, rows), rows), :] = sources[d][...]


def finish_kernel(
    digit_ref, mine_hbm, other_hbm, cross_q, cross_out, cross_kv, self_out, self_qkv,
    self_bias, self_out_bias, cross_bias, cross_out_bias, in_bias, out_bias, omega, gain, shift,
    buf, last, *refs
):
    targets = (cross_q, cross_out, cross_kv, self_out, self_qkv)
    bufs, sems = refs[: len(targets)], refs[len(targets)]
    rows = mine_hbm.shape[0]
    loads = [
        pltpu.make_async_copy(source, buf.at[i], sems.at[2 * len(targets) + i])
        for i, source in enumerate((mine_hbm, other_hbm))
    ]
    start(loads)
    outs = []
    for half, load in enumerate(loads):
        load.wait()
        here = pl.ds(pl.multiple_of((digit_ref[0] ^ half) * rows, rows), rows)
        begin = 0
        for i, (target, wide) in enumerate(zip(targets, bufs)):
            count = target.shape[1]
            wide[half] = buf[half, :, begin : begin + count].astype(f32)
            sem = sems.at[2 * i + half]
            outs.append(pltpu.make_async_copy(wide.at[half], target.at[here], sem))
            outs[-1].start()
            begin += count
        last[here, :] = buf[half, :, begin:]
    part = jnp.transpose(last[...].astype(f32))
    begin = 0
    for target in (
        self_bias, self_out_bias, cross_bias, cross_out_bias, in_bias, out_bias, omega, gain, shift,
    ):
        count = target.shape[0]
        target[...] = part[begin : begin + count]
        begin += count
    wait(outs)


def spread_kernel(stage, digit_ref, *refs):
    *sources, target = refs
    for d, source in enumerate(sources):
        target[digit_ref[stage] ^ d] = source[...]


def ffn_finish_kernel(digit_ref, mine_hbm, other_hbm, out_hbm, in_hbm, buf, out_buf, in_buf, sems):
    rows, width = mine_hbm.shape
    chunks = out_hbm.shape[0] // width
    loads = [
        pltpu.make_async_copy(source, buf.at[digit_ref[0] ^ i], sems.at[2 * chunks + i])
        for i, source in enumerate((mine_hbm, other_hbm))
    ]
    start(loads)
    wait(loads)
    outs = []
    for c in range(chunks):
        half, place = c // (chunks // 2), c % (chunks // 2) * width
        out_buf[c] = buf[half, place : place + width, :].astype(f32)
        place += rows // 2
        in_buf[c] = buf[half, place : place + width, :].astype(f32)
        here = slice(c * width, (c + 1) * width)
        outs.append(pltpu.make_async_copy(out_buf.at[c], out_hbm.at[here], sems.at[2 * c]))
        outs.append(pltpu.make_async_copy(in_buf.at[c], in_hbm.at[:, here], sems.at[2 * c + 1]))
        start(outs[-2:])
    wait(outs)


class Order:
    def __init__(self, digits):
        self.digits = digits

    def after(self, value):
        return lax.optimization_barrier((value, self.digits))[0]

    def through(self, value):
        value, self.digits = lax.optimization_barrier((value, self.digits))
        return value

    def __call__(self, kernel, steps, ins, outs, scratch=(), vmem=VMEM, us=1):
        def whole(shape):
            return pl.BlockSpec(shape, lambda i: (0,) * len(shape), pipeline_mode=pl.Buffered(1))

        arrays, in_specs, shapes, out_specs = (
            [self.digits], [pl.BlockSpec(memory_space=pltpu.SMEM)], [], []
        )
        anywhere = pl.BlockSpec(memory_space=pl.ANY)
        for item in ins:
            if isinstance(item, tuple):
                arrays.append(item[0])
                in_specs.append(pl.BlockSpec(*item[1:]) if item[1:] else anywhere)
            else:
                arrays.append(item)
                in_specs.append(whole(item.shape))
        for shape, dtype, *block in outs:
            shapes.append(jax.ShapeDtypeStruct(shape, dtype))
            if block == [None]:
                out_specs.append(anywhere)
            elif block:
                out_specs.append(pl.BlockSpec(*block))
            else:
                out_specs.append(pl.BlockSpec(shape, lambda i, n=len(shape): (0,) * n))
        result = pl.pallas_call(
            kernel,
            grid=(steps,),
            in_specs=in_specs,
            out_specs=out_specs,
            out_shape=shapes,
            scratch_shapes=list(scratch),
            compiler_params=pltpu.CompilerParams(
                dimension_semantics=("arbitrary",), vmem_limit_bytes=vmem
            ),
            cost_estimate=pl.CostEstimate(flops=us * 10**9, bytes_accessed=0, transcendentals=0),
        )(*arrays)
        self.digits = lax.optimization_barrier((self.digits, result[0]))[0]
        return result


def stages_of(sizes):
    result = []
    for axis in ("dp", "ctx"):
        stride = 1
        while stride < sizes[axis]:
            left = sizes[axis] // stride
            count = 2 if (axis == "dp" and stride == 1) or left % 4 else 4
            result.append((axis, stride, count))
            stride *= count
    return result


class Sum:
    def __init__(self, order, stages, sizes, pieces):
        self.order, self.stages, self.sizes = order, stages, sizes
        self.stage, self.spread, self.pieces, self.others = 0, [], pieces, []
        self.send(0)

    def send(self, stage):
        axis, stride, count = self.stages[stage]
        pieces = self.pieces if len(self.pieces) > 1 else self.pieces * count
        self.got = [
            lax.ppermute(
                pieces[d], axis, [(i, i ^ (d * stride)) for i in range(self.sizes[axis])]
            )
            for d in range(1, count)
        ]

    def settle(self):
        self.spread.append(self.stage)
        self.stage += 1
        group = [self.pieces[0], *self.got]
        self.pieces, self.got = self.order(
            functools.partial(combine_kernel, self.stage, 1, [len(group)]), 1, group,
            [(group[0].shape, bf16)], vmem=SMALL_VMEM,
        ), []

    def join(self, other):
        self.others.append(other)

    def step(self):
        groups = [[one.pieces[0], *one.got] for one in (*self.others, self)]
        rows = groups[0][0].shape[0]
        width = sum(group[0].shape[1] for group in groups)
        outs = 1
        if self.stage < len(self.stages):
            if len(self.pieces) > 1:
                self.spread.append(self.stage)
            self.stage += 1
            if self.stage < len(self.stages):
                count = self.stages[self.stage][2]
                outs = count if rows % (PAD * count) == 0 else 1
            kernel = functools.partial(
                combine_kernel, self.stage, outs, [len(group) for group in groups]
            )
            rows //= outs
        else:
            stage = self.spread.pop()
            kernel = functools.partial(place_kernel, stage, len(groups[0]))
            rows *= len(groups[0])
        self.others = []
        self.pieces = self.order(
            kernel, 1, sum(groups, []), [((rows, width), bf16)] * outs, vmem=SMALL_VMEM
        )
        self.send(self.stage if self.stage < len(self.stages) else self.spread[-1])

    @property
    def last(self):
        return self.stage == len(self.stages) and len(self.spread) == 1


def local(sizes, *args):
    (
        tokens, memory, mem_mask, segment_ids, cotangent, self_qkv, self_bias, self_out,
        self_out_bias, cross_q, cross_kv, cross_bias, cross_out, cross_out_bias, ffn_in,
        ffn_in_bias, ffn_out, ffn_out_bias, omegas, ln_gains, ln_biases,
    ) = args
    length, width = tokens.shape[1:]
    hidden = ffn_in.shape[1]
    size = width // HEADS
    holders, part_rows = memory.shape[:2]
    count = holders * part_rows
    x = tokens.reshape(length, width)
    cot = cotangent.reshape(length, width)
    seg = segment_ids.reshape(1, length)
    stages = stages_of(sizes)
    digits = [(lax.axis_index(axis) // stride) % several for axis, stride, several in stages]
    first_ctx = [axis for axis, _, _ in stages].index("ctx")
    order = Order(jnp.stack(digits).astype(jnp.int32))

    blocks = length // BLOCK
    reach = (REACH + 1) * BLOCK

    pairs, pair = HEADS // PAIR, PAIR * size

    def scores_in(array):
        shape = (PAIR, *array.shape[1:])
        return (array, shape, lambda i: (i,) + (0,) * (len(shape) - 1))

    def scores_out(*shape):
        return ((HEADS, *shape), bf16, None)

    def pair_in(array, part=0):
        return (array, (pair, array.shape[1]), lambda i: (part * pairs + i, 0))

    def vmem(*shape, dtype=bf16):
        return pltpu.VMEM(shape, dtype)

    dma = pltpu.SemaphoreType.DMA
    tall, wide = (width, length), (length, width)
    small, *pieces = order(
        functools.partial(prepare_kernel, first_ctx),
        1,
        [
            memory, mem_mask, self_bias, self_out_bias, cross_bias, cross_out_bias, ffn_in_bias,
            ffn_out_bias, omegas, ln_gains, ln_biases,
        ],
        [((SMALL, width), f32)] + [((part_rows + PAD, width), bf16)] * holders,
    )

    def trade(pieces):
        return [pieces[0]] + [
            lax.ppermute(pieces[d], "ctx", [(i, i ^ d) for i in range(holders)])
            for d in range(1, holders)
        ]

    pieces = trade(pieces)
    qkv, e_self, inv_self, o, z1, h1, q2 = order(
        self_forward_kernel,
        pairs,
        [x, seg, small, self_qkv, (self_out,), (cross_q,)],
        [
            ((3 * width, length), bf16, None),
            scores_out(blocks, BLOCK, reach),
            ((HEADS, length), f32),
            (tall, bf16, None),
            (wide, f32, None),
            (wide, bf16, None),
            (tall, bf16, None),
        ],
        [
            vmem(3 * width, length), vmem(2, PAIR, blocks, BLOCK, reach), vmem(*tall),
            vmem(*wide, dtype=f32), vmem(*wide), vmem(*tall),
            vmem(width, width), vmem(width, width), vmem(PAD, length), vmem(PAD, length), dma((7,)),
            dma((2, PAIR)),
        ],
        us=15,
    )
    kv, e_cross, inv_cross, o2, z2, h2 = order(
        functools.partial(cross_forward_kernel, holders),
        pairs,
        [pair_in(q2), small, cross_kv, (h1,), (cross_out,), *pieces],
        [
            ((2 * width, count), bf16, None),
            scores_out(count, length),
            ((HEADS, length), f32),
            (tall, bf16, None),
            (wide, f32, None),
            (wide, bf16, None),
        ],
        [
            vmem(2 * width, count), vmem(2, PAIR, count, length), vmem(*tall),
            vmem(*wide, dtype=f32), vmem(*wide), vmem(*wide), vmem(width, width), vmem(PAD, count),
            dma((6,)), dma((2, PAIR)),
        ],
        us=22,
    )
    rows = BLOCK
    chunks = hidden // width
    row_block = ((rows, width), lambda i: (i, 0))
    activations, dz2, keep, send, small_grad = order(
        ffn_kernel,
        length // rows,
        [
            (h2, *row_block), (h1, *row_block), (z2, *row_block), (cot, *row_block), small, ffn_in,
            (ffn_out,),
        ],
        [
            (wide, bf16, *row_block),
            (wide, f32, *row_block),
            ((hidden, width), bf16, None),
            ((hidden, width), bf16, None),
            ((SMALL, width), f32),
        ],
        [
            vmem(*wide), vmem(length, hidden), vmem(rows, hidden, dtype=f32), vmem(*wide),
            vmem(length, hidden), vmem(2, hidden, width), vmem(hidden, width),
            dma((2 * chunks + 1,)),
        ],
        us=26,
    )
    def open_sum(parts):
        several = len(parts) // 2
        *others, last = [
            Sum(order, stages, sizes, [keep, send])
            for keep, send in zip(parts[:several], parts[several:])
        ]
        for one in others:
            last.join(one)
        return last

    ffn_sum = open_sum([keep, send])
    (do2,) = order(back_start_kernel, 1, [dz2, inv_cross, cross_out], [(tall, bf16)], us=3)
    ffn_sum.step()
    parts = [((width // 2, 2 * width), bf16, None)] * 4
    dkv, dz1, small_grad, p0, p1, p2, p3 = order(
        functools.partial(cross_backward_kernel, holders),
        pairs,
        [
            scores_in(e_cross), pair_in(do2), pair_in(o2), pair_in(q2), pair_in(kv), pair_in(kv, 1),
            small, small_grad, (z1,), (h1,), (x,), (cross_q,), (dz2,),
            *[(piece,) for piece in pieces],
        ],
        [((2 * width, count), bf16, None), (wide, f32, None), ((SMALL, width), f32)] + parts,
        [
            vmem(*wide, dtype=f32), vmem(*wide), vmem(*wide), vmem(width, width),
            vmem(*wide, dtype=f32), vmem(*memory.shape), vmem(*tall), vmem(*tall),
            vmem(2 * width, count), vmem(*wide, dtype=f32), vmem(width, 4 * width),
            dma((5 + holders + 5 + 2 * pairs,)),
        ],
        us=26,
    )
    cross_sum = open_sum([p0, p1, p2, p3])
    ffn_sum.step()
    cross_sum.step()
    total = 4 * width + LANES
    pair_out = (tall, bf16, (pair, length), lambda i: (i, 0))
    dq, dk, dv = order(
        self_backward_kernel,
        pairs,
        [
            scores_in(e_self), inv_self, pair_in(o), pair_in(qkv), pair_in(qkv, 1), pair_in(qkv, 2),
            dz1, self_out,
        ],
        [pair_out] * 3,
        [vmem(*tall)],
        us=16,
    )
    for _ in range(first_ctx - 2):
        cross_sum.step()
    cross_sum.settle()
    ffn_sum.step()
    parts = [((width // 2, some), bf16, None) for some in (2 * width, 2 * width + LANES)] * 2
    self_sum = open_sum(
        order(
            self_weights_kernel,
            1,
            [small_grad, (x,), (dq,), (dk,), (dv,), (dz1,), (o,)],
            parts,
            [
                vmem(*wide), vmem(*tall), vmem(*tall), vmem(*tall), vmem(*wide, dtype=f32),
                vmem(*tall), vmem(width, total), dma((6 + 10,)),
            ],
            us=7,
        )
    )
    mem_parts = order(
        memory_kernel, 1, [dkv, cross_kv], [((part_rows, width), bf16)] * holders, us=3
    )
    for _ in range(first_ctx - 1):
        self_sum.step()
    self_sum.join(cross_sum)
    self_sum.step()
    ffn_sum.step()
    self_sum.step()
    turned = ((width, rows), lambda i: (0, i))
    (token_grad,) = order(
        token_kernel,
        length // rows,
        [(dq, *turned), (dk, *turned), (dv, *turned), (dz1, *row_block), small, self_qkv],
        [(wide, bf16, *row_block)],
        us=6,
    )
    while not ffn_sum.last:
        ffn_sum.step()
    while len(self_sum.spread) > 2 or self_sum.stage < len(stages):
        self_sum.step()
    mem_parts = trade(order.after(mem_parts))
    (memory_grad,) = order(
        functools.partial(spread_kernel, first_ctx), 1, mem_parts, [(memory.shape, bf16)],
        vmem=SMALL_VMEM,
    )
    self_sum.step()
    while not self_sum.last:
        self_sum.step()
    square = (width, width)
    grad_ffn_out, grad_ffn_in = order(
        ffn_finish_kernel,
        1,
        [(ffn_sum.pieces[0],), (ffn_sum.got[0],)],
        [((hidden, width), f32, None), ((width, hidden), f32, None)],
        [
            vmem(2, hidden, width), vmem(chunks, *square, dtype=f32),
            vmem(chunks, *square, dtype=f32), dma((2 * chunks + 2,)),
        ],
        vmem=SMALL_VMEM,
    )
    shapes = [(width, several * width) for several in (1, 1, 2, 1, 3)]
    shapes += [(several, width) for several in (2, 1, 2, 1, chunks, 1, 3, 3, 3)]
    large = [shape for shape in shapes if shape[0] == width]
    grad_cross_q, grad_cross_out, grad_cross_kv, grad_out, grad_qkv, *smalls = order(
        finish_kernel,
        1,
        [(self_sum.pieces[0],), (self_sum.got[0],)],
        [(shape, f32, None) if shape in large else (shape, f32) for shape in shapes],
        [
            vmem(2, width // 2, 8 * width + LANES), vmem(width, LANES),
            *[vmem(2, width // 2, shape[1], dtype=f32) for shape in large], dma((12,)),
        ],
        vmem=SMALL_VMEM,
    )
    (
        self_bias, self_out_bias, cross_bias, cross_out_bias, in_bias, out_bias, omega, gain, shift
    ) = smalls
    return (
        activations.reshape(tokens.shape),
        token_grad.reshape(tokens.shape),
        memory_grad,
        grad_qkv,
        self_bias,
        grad_out,
        self_out_bias.reshape(-1),
        grad_cross_q,
        grad_cross_kv,
        cross_bias,
        grad_cross_out,
        cross_out_bias.reshape(-1),
        grad_ffn_in,
        in_bias.reshape(-1),
        grad_ffn_out,
        out_bias.reshape(-1),
        omega,
        gain,
        shift,
    )


def solution(mesh):
    sizes = dict(mesh.shape)
    both = P(("dp", "ctx"), None, None)
    return jax.shard_map(
        functools.partial(local, sizes),
        mesh=mesh,
        in_specs=(both, P("dp", "ctx", None), P("dp", "ctx"), P(("dp", "ctx"), None), both)
        + (P(),) * 16,
        out_specs=(both, both, P("dp", "ctx", None)) + (P(),) * 16,
        check_vma=False,
    )
```

```python
import functools

import jax
import jax.numpy as jnp
from jax import lax
from jax.experimental import pallas as pl
from jax.experimental.pallas import tpu as pltpu
from jax.sharding import PartitionSpec as P

HEADS = 8
PAIR = 2
LOG2E = 1.4426950408889634
LN2 = 0.6931471805599453
UNSEEN = -1e30
BLOCK = 256
REACH = 2
PAD = 16
VMEM = 60 * 2**20
SMALL_VMEM = 24 * 2**20
bf16, f32 = jnp.bfloat16, jnp.float32

SELF_BIAS, SELF_OUT_BIAS, CROSS_BIAS, CROSS_OUT_BIAS = 0, 2, 3, 5
FFN_IN_BIAS, FFN_OUT_BIAS, OMEGA, GAIN, SHIFT, SMALL = 6, 10, 11, 14, 17, 24
LANES = 128


def dot(left, right, left_dim, right_dim):
    return lax.dot_general(
        left, right, (((left_dim,), (right_dim,)), ((), ())), preferred_element_type=f32
    )


def column(row):
    return jnp.transpose(jnp.broadcast_to(row, (8, row.shape[1])))[:, :1]


def row_sum(value):
    return jnp.sum(value.astype(f32), axis=0, keepdims=True)


def feature_sum(value):
    ones = jnp.ones((PAD, value.shape[1]), bf16)
    return dot(ones, value, 1, 1)[:1]


def normalize(value):
    centered = value - jnp.mean(value, axis=-1, keepdims=True)
    spread = jnp.mean(centered * centered, axis=-1, keepdims=True)
    inverse = lax.rsqrt(spread + 1e-05)
    return centered * inverse, inverse


def normalize_back(grad, gain, normal, inverse):
    scaled = grad * gain
    mean = jnp.mean(scaled, axis=-1, keepdims=True)
    slope = jnp.mean(scaled * normal, axis=-1, keepdims=True)
    return (scaled - mean - normal * slope) * inverse


def with_ones(rows):
    return jnp.concatenate((rows, jnp.ones((PAD, rows.shape[1]), bf16)), axis=0)


def start(copies):
    for copy in copies:
        copy.start()


def wait(copies):
    for copy in copies:
        copy.wait()


def score_copies(step, buf, hbm, sems):
    slot = lax.rem(step, 2)
    return [
        pltpu.make_async_copy(buf.at[slot, one], hbm.at[step * PAIR + one], sems.at[slot, one])
        for one in range(PAIR)
    ]


def far_first(place, count):
    return (count - place) % count


def prepare_kernel(stage, digit_ref, memory_ref, mask_ref, *refs):
    _, part_rows, width = memory_ref.shape
    params, par_ref, pieces = refs[:9], refs[9], refs[10:]
    row = 0
    for ref in params:
        value = ref[...].astype(f32)
        if value.ndim == 2:
            par_ref[row : row + value.shape[0], :] = value
            row += value.shape[0]
        else:
            for begin in range(0, value.shape[0], width):
                par_ref[row : row + 1, :] = value[begin : begin + width].reshape(1, width)
                row += 1
    par_ref[row:, :] = jnp.zeros((par_ref.shape[0] - row, width), f32)
    for d, piece in enumerate(pieces):
        index = digit_ref[stage] ^ far_first(d, len(pieces))
        piece[:part_rows, :] = memory_ref[index]
        mask = mask_ref[pl.ds(index, 1), :].astype(f32)
        mask = jnp.concatenate((mask, jnp.zeros((1, width - part_rows), f32)), axis=1)
        piece[part_rows:, :] = jnp.broadcast_to(mask, (PAD, width)).astype(bf16)


def self_forward_kernel(
    digit_ref, x_ref, seg_ref, par_ref, qkv_w, out_hbm, cross_hbm,
    qkv_hbm, e_hbm, inv_ref, o_hbm, z_hbm, h_hbm, q_hbm,
    qkv_ref, e_ref, o_ref, z_ref, h_ref, q_ref, out_w, cross_w, q_mask, k_mask, sems, e_sems,
):
    step = pl.program_id(0)
    last = pl.num_programs(0) - 1
    length, width = x_ref.shape
    size = width // HEADS
    scale = size**-0.5 * LOG2E
    copy = pltpu.make_async_copy
    loads = [copy(out_hbm, out_w, sems.at[0]), copy(cross_hbm, cross_w, sems.at[1])]
    projected = copy(qkv_ref, qkv_hbm, sems.at[2])

    @pl.when(step == 0)
    def _():
        start(loads)
        x = x_ref[...]
        for part, row in ((0, 0), (1, None), (2, 1)):
            columns = slice(part * width, (part + 1) * width)
            value = dot(qkv_w[:, columns], x, 0, 1)
            if row is not None:
                value = value + column(par_ref[SELF_BIAS + row : SELF_BIAS + row + 1])
            if part == 0:
                value = value * scale
            qkv_ref[columns, :] = value.astype(bf16)
        projected.start()
        same = lax.broadcasted_iota(jnp.int32, (PAD, length), 0) == seg_ref[...]
        q_mask[...] = jnp.where(same, 1.0, 0.0).astype(bf16)
        k_mask[...] = jnp.where(same, 0.0, UNSEEN).astype(bf16)

    causal = lax.broadcasted_iota(jnp.int32, (BLOCK, BLOCK), 0) <= lax.broadcasted_iota(
        jnp.int32, (BLOCK, BLOCK), 1
    )
    blocks = length // BLOCK
    slot = lax.rem(step, 2)

    @pl.when(step >= 2)
    def _():
        wait(score_copies(step - 2, e_ref, e_hbm, e_sems))

    for one in range(PAIR):
        head = step * PAIR + one
        base = pl.multiple_of(head * size, size)
        q = jnp.concatenate((qkv_ref[pl.ds(base, size), :], q_mask[...]), axis=0)
        k = jnp.concatenate((qkv_ref[pl.ds(width + base, size), :], k_mask[...]), axis=0)
        v = with_ones(qkv_ref[pl.ds(2 * width + base, size), :])
        scores, tops, mixed = [], [None] * blocks, [None] * blocks
        for i in range(blocks):
            s = dot(k[:, i * BLOCK : (i + 1) * BLOCK], q[:, i * BLOCK : (i + REACH + 1) * BLOCK], 0, 0)
            diagonal = jnp.where(causal, s[:, :BLOCK], UNSEEN)
            if s.shape[1] > BLOCK:
                diagonal = jnp.concatenate((diagonal, s[:, BLOCK:]), axis=1)
            scores.append(diagonal)
            top = jnp.max(diagonal, axis=0, keepdims=True)
            for b in range(s.shape[1] // BLOCK):
                part = top[:, b * BLOCK : (b + 1) * BLOCK]
                old = tops[i + b]
                tops[i + b] = part if old is None else jnp.maximum(old, part)
        for i, s in enumerate(scores):
            several = s.shape[1] // BLOCK
            weights = jnp.exp2(s - jnp.concatenate(tops[i : i + several], axis=1)).astype(bf16)
            e_ref[slot, one, i, :, : several * BLOCK] = weights
            part = dot(v[:, i * BLOCK : (i + 1) * BLOCK], weights, 1, 0)
            for b in range(several):
                piece = part[:, b * BLOCK : (b + 1) * BLOCK]
                mixed[i + b] = piece if mixed[i + b] is None else mixed[i + b] + piece
        for j, value in enumerate(mixed):
            mine = slice(j * BLOCK, (j + 1) * BLOCK)
            inverse = 1.0 / value[size : size + 1]
            o_ref[pl.ds(base, size), mine] = (value[:size] * inverse).astype(bf16)
            inv_ref[pl.ds(head, 1), mine] = inverse
    start(score_copies(step, e_ref, e_hbm, e_sems))

    @pl.when(step == last)
    def _():
        outs = [
            copy(o_ref, o_hbm, sems.at[3]),
            copy(z_ref, z_hbm, sems.at[4]),
            copy(h_ref, h_hbm, sems.at[5]),
            copy(q_ref, q_hbm, sems.at[6]),
        ]
        outs[0].start()
        wait(loads)
        z = (
            par_ref[OMEGA : OMEGA + 1] * x_ref[...].astype(f32)
            + dot(o_ref[...], out_w[...], 0, 0)
            + par_ref[SELF_OUT_BIAS : SELF_OUT_BIAS + 1]
        )
        z_ref[...] = z
        outs[1].start()
        normal, _ = normalize(z)
        h = (normal * par_ref[GAIN : GAIN + 1] + par_ref[SHIFT : SHIFT + 1]).astype(bf16)
        h_ref[...] = h
        outs[2].start()
        value = dot(cross_w[...], h, 0, 1) + column(par_ref[CROSS_BIAS : CROSS_BIAS + 1])
        q_ref[...] = (value * scale).astype(bf16)
        outs[3].start()
        wait([projected, *outs])
        wait(score_copies(step - 1, e_ref, e_hbm, e_sems))
        wait(score_copies(step, e_ref, e_hbm, e_sems))


def cross_forward_kernel(
    holders, digit_ref, q_ref, par_ref, kv_w, h1_hbm, out_hbm, *refs
):
    pieces, refs = refs[:holders], refs[holders:]
    kv_hbm, e_hbm, inv_ref, o_hbm, z_hbm, h_hbm, *refs = refs
    kv_ref, e_ref, o_ref, z_ref, h_ref, h1_ref, out_w, k_mask, sems, e_sems = refs
    step = pl.program_id(0)
    last = pl.num_programs(0) - 1
    length, width = h1_ref.shape
    size = width // HEADS
    part_rows = pieces[0].shape[0] - PAD
    copy = pltpu.make_async_copy
    loads = [copy(h1_hbm, h1_ref, sems.at[0]), copy(out_hbm, out_w, sems.at[1])]
    projected = copy(kv_ref, kv_hbm, sems.at[2])

    @pl.when(step == 0)
    def _():
        start(loads)
        shift = column(par_ref[CROSS_BIAS + 1 : CROSS_BIAS + 2])
        first = lax.broadcasted_iota(jnp.int32, (PAD, part_rows), 0) == 0
        for b, piece in enumerate(pieces):
            columns = slice(b * part_rows, (b + 1) * part_rows)
            m = piece[:part_rows, :]
            kv_ref[:width, columns] = dot(kv_w[:, :width], m, 0, 1).astype(bf16)
            kv_ref[width:, columns] = (dot(kv_w[:, width:], m, 0, 1) + shift).astype(bf16)
            seen = piece[part_rows:, :part_rows].astype(f32) > 0.5
            k_mask[:, columns] = jnp.where(first & ~seen, UNSEEN, 0.0).astype(bf16)
        projected.start()

    slot = lax.rem(step, 2)

    @pl.when(step >= 2)
    def _():
        wait(score_copies(step - 2, e_ref, e_hbm, e_sems))

    heads = []
    for one in range(PAIR):
        base = pl.multiple_of((step * PAIR + one) * size, size)
        heads.append(
            (
                with_ones(q_ref[one * size : (one + 1) * size, :]),
                jnp.concatenate((kv_ref[pl.ds(base, size), :], k_mask[...]), axis=0),
                with_ones(kv_ref[pl.ds(width + base, size), :]),
            )
        )
    blocks = [slice(i, i + BLOCK) for i in range(0, kv_ref.shape[1], BLOCK)]

    def block_scores(one, block):
        q, k, _ = heads[one]
        scores = dot(k[:, block], q, 0, 0)
        return scores, jnp.max(scores, axis=0, keepdims=True)

    now = [block_scores(0, block) for block in blocks]
    for one in range(PAIR):
        top = functools.reduce(jnp.maximum, [each for _, each in now])
        later, weights = [], []
        for (scores, _), block in zip(now, blocks):
            if one + 1 < PAIR:
                later.append(block_scores(one + 1, block))
            weights.append(jnp.exp2(scores - top).astype(bf16))
            e_ref[slot, one, block, :] = weights[-1]
        mixed = None
        for weight, block in zip(weights, blocks):
            part = dot(heads[one][2][:, block], weight, 1, 0)
            mixed = part if mixed is None else mixed + part
        inverse = 1.0 / mixed[size : size + 1]
        head = step * PAIR + one
        o_ref[pl.ds(pl.multiple_of(head * size, size), size), :] = (mixed[:size] * inverse).astype(
            bf16
        )
        inv_ref[pl.ds(head, 1), :] = inverse
        now = later
    start(score_copies(step, e_ref, e_hbm, e_sems))

    @pl.when(step == last)
    def _():
        outs = [
            copy(o_ref, o_hbm, sems.at[3]),
            copy(z_ref, z_hbm, sems.at[4]),
            copy(h_ref, h_hbm, sems.at[5]),
        ]
        outs[0].start()
        wait(loads)
        z = (
            par_ref[OMEGA + 1 : OMEGA + 2] * h1_ref[...].astype(f32)
            + dot(o_ref[...], out_w[...], 0, 0)
            + par_ref[CROSS_OUT_BIAS : CROSS_OUT_BIAS + 1]
        )
        z_ref[...] = z
        outs[1].start()
        normal, _ = normalize(z)
        h_ref[...] = (
            normal * par_ref[GAIN + 1 : GAIN + 2] + par_ref[SHIFT + 1 : SHIFT + 2]
        ).astype(bf16)
        outs[2].start()
        wait([projected, *outs])
        wait(score_copies(step - 1, e_ref, e_hbm, e_sems))
        wait(score_copies(step, e_ref, e_hbm, e_sems))


def ffn_kernel(
    digit_ref, h2_ref, h1_ref, z2_ref, cot_ref, par_ref, in_w, out_hbm,
    act_ref, dz_ref, keep_hbm, send_hbm, small_ref,
    h_buf, g_buf, slope_buf, e_buf, eu_buf, grad_buf, out_w, sems,
):
    step = pl.program_id(0)
    rows, width = cot_ref.shape
    hidden = in_w.shape[1]
    chunks = hidden // width
    begin = pl.multiple_of(step * rows, rows)
    mine = pl.ds(begin, rows)
    load = pltpu.make_async_copy(out_hbm, out_w, sems.at[2 * chunks])

    @pl.when(step == 0)
    def _():
        load.start()
        small_ref[...] = jnp.zeros_like(small_ref)

    def add(row, value):
        small_ref[row : row + 1] += row_sum(value)

    h2 = h2_ref[...]
    h_buf[mine, :] = h2
    h2_wide = h2.astype(f32)
    for c in range(chunks):
        columns = slice(c * width, (c + 1) * width)
        u = dot(h2, in_w[:, columns], 1, 0) + par_ref[FFN_IN_BIAS + c : FFN_IN_BIAS + c + 1]
        rate = 0.7978845608028654
        square = u * u
        t = jnp.tanh(u * (rate + (rate * 0.044715) * square))
        half = 0.5 + 0.5 * t
        g_buf[mine, columns] = (u * half).astype(bf16)
        slope_buf[:, columns] = half + (0.5 * u) * (1.0 - t * t) * (
            rate + (3 * rate * 0.044715) * square
        )

    @pl.when(step == 0)
    def _():
        load.wait()

    z3 = (
        par_ref[OMEGA + 2 : OMEGA + 3] * h2_wide
        + dot(g_buf[mine, :], out_w[...], 1, 0)
        + par_ref[FFN_OUT_BIAS : FFN_OUT_BIAS + 1]
    )
    normal, inverse = normalize(z3)
    gain = par_ref[GAIN + 2 : GAIN + 3]
    act_ref[...] = (normal * gain + par_ref[SHIFT + 2 : SHIFT + 3]).astype(bf16)
    dy = cot_ref[...].astype(f32)
    add(GAIN + 2, dy * normal)
    add(SHIFT + 2, dy)
    dz3 = normalize_back(dy, gain, normal, inverse)
    add(OMEGA + 2, dz3 * h2_wide)
    e3 = dz3.astype(bf16)
    e_buf[mine, :] = e3
    add(FFN_OUT_BIAS, e3)
    for c in range(chunks):
        columns = slice(c * width, (c + 1) * width)
        eu = (dot(e3, out_w[columns, :], 1, 1) * slope_buf[:, columns]).astype(bf16)
        eu_buf[mine, columns] = eu
        add(FFN_IN_BIAS + c, eu)
    dh2 = par_ref[OMEGA + 2 : OMEGA + 3] * dz3 + dot(eu_buf[mine, :], in_w[...], 1, 1)
    normal, inverse = normalize(z2_ref[...])
    add(GAIN + 1, dh2 * normal)
    add(SHIFT + 1, dh2)
    dz2 = normalize_back(dh2, par_ref[GAIN + 1 : GAIN + 2], normal, inverse)
    add(OMEGA + 1, dz2 * h1_ref[...].astype(f32))
    add(CROSS_OUT_BIAS, dz2.astype(bf16))
    dz_ref[...] = dz2

    @pl.when(step == pl.num_programs(0) - 1)
    def _():
        outs = []
        for half in range(2):
            mine = [c for c in range(chunks) if c // (chunks // 2) == half]
            for i, c in enumerate(mine + [chunks + c for c in mine]):
                columns = slice(c % chunks * width, (c % chunks + 1) * width)
                if c < chunks:
                    value = dot(g_buf[:, columns], e_buf[...], 0, 0)
                else:
                    value = dot(h_buf[...], eu_buf[:, columns], 0, 0)
                place = slice(i * width, (i + 1) * width)
                grad_buf[half, place, :] = value.astype(bf16)
                sem = sems.at[half * chunks + i]
                source = grad_buf.at[half, place]
                keep = pltpu.make_async_copy(source, keep_hbm.at[place], sem)
                send = pltpu.make_async_copy(source, send_hbm.at[place], sem)
                pl.when(digit_ref[0] == half)(keep.start)
                pl.when(digit_ref[0] != half)(send.start)
                outs.append(keep)
        wait(outs)


def back_heads(do_ref, out_w, e, inv_ref):
    value = dot(out_w[...], e, 1, 1)
    size = value.shape[0] // HEADS
    for i in range(HEADS):
        rows = slice(i * size, (i + 1) * size)
        do_ref[rows, :] = (value[rows] * inv_ref[i : i + 1]).astype(bf16)


def back_head(do_rows, o_rows):
    length = do_rows.shape[1]
    delta = jnp.sum(do_rows.astype(f32) * o_rows.astype(f32), axis=0, keepdims=True)
    high = delta.astype(bf16).astype(f32)
    row = lax.broadcasted_iota(jnp.int32, (PAD, length), 0)
    extra = jnp.where(row == 0, -high, jnp.where(row == 1, high - delta, 0.0))
    return jnp.concatenate((do_rows, extra.astype(bf16)), axis=0)


def cross_backward_kernel(
    holders, digit_ref, e_ref, do_ref, o_ref, q_ref, k_ref, v_ref, par_ref, old_ref,
    z1_hbm, h1_hbm, x_hbm, qw_hbm, dz2_hbm, *refs
):
    m_hbm, refs = refs[:holders], refs[holders:]
    dkv_hbm, dz1_hbm, small_ref, *refs = refs
    keeps, sends, refs = refs[:2], refs[2:4], refs[4:]
    z1_ref, h1_ref, x_ref, q_w, dz2_ref, m_ref, *refs = refs
    o_buf, dq_buf, dkv_buf, dz_buf, grad_buf, sems = refs
    step = pl.program_id(0)
    last = pl.num_programs(0) - 1
    length, width = x_ref.shape
    size = width // HEADS
    count = k_ref.shape[1]
    pair = PAIR * size
    part_rows = m_ref.shape[1]
    copy = pltpu.make_async_copy
    pairs_of = [(z1_hbm, z1_ref), (h1_hbm, h1_ref), (x_hbm, x_ref), (qw_hbm, q_w)]
    pairs_of += [(dz2_hbm, dz2_ref)]
    pairs_of += [(source.at[:part_rows], m_ref.at[b]) for b, source in enumerate(m_hbm)]
    loads = [copy(source, target, sems.at[i]) for i, (source, target) in enumerate(pairs_of)]

    def part_out(at, which):
        rows = pl.ds(pl.multiple_of(which * width + at * pair, pair), pair)
        return copy(dkv_buf.at[rows], dkv_hbm.at[rows], sems.at[len(loads) + 5 + 2 * at + which])

    @pl.when(step == 0)
    def _():
        start(loads)
        small_ref[...] = old_ref[...]

    base = pl.multiple_of(step * pair, pair)
    o_buf[pl.ds(base, pair), :] = o_ref[...]
    heads = []
    for one in range(PAIR):
        here = slice(one * size, (one + 1) * size)
        heads.append(
            (
                back_head(do_ref[here, :], o_ref[here, :]),
                q_ref[here, :],
                k_ref[here, :],
                with_ones(v_ref[here, :]),
            )
        )
    dq = [None] * PAIR
    for i in range(count // BLOCK):
        mine = slice(i * BLOCK, (i + 1) * BLOCK)
        for one, (do, q, k, v) in enumerate(heads):
            weights = e_ref[one, mine, :]
            ds = (weights.astype(f32) * dot(v[:, mine], do, 0, 0)).astype(bf16)
            begin = base + one * size
            dkv_buf[pl.ds(width + begin, size), mine] = dot(do[:size], weights, 1, 1).astype(bf16)
            dkv_buf[pl.ds(begin, size), mine] = (dot(q, ds, 1, 1) * LN2).astype(bf16)
            part = dot(k[:, mine], ds, 1, 0)
            dq[one] = part if i == 0 else dq[one] + part
    for one in range(PAIR):
        dq_buf[pl.ds(base + one * size, size), :] = (dq[one] * size**-0.5).astype(bf16)
    start([part_out(step, 0), part_out(step, 1)])

    @pl.when(step == last)
    def _():
        wait(loads)
        after = len(loads)
        dq_all = dq_buf[...]
        dh1 = par_ref[OMEGA + 1 : OMEGA + 2] * dz2_ref[...] + dot(dq_all, q_w[...], 0, 1)
        normal, inverse = normalize(z1_ref[...])
        small_ref[GAIN : GAIN + 1] = row_sum(dh1 * normal)
        small_ref[SHIFT : SHIFT + 1] = row_sum(dh1)
        dz1 = normalize_back(dh1, par_ref[GAIN : GAIN + 1], normal, inverse)
        small_ref[OMEGA : OMEGA + 1] = row_sum(dz1 * x_ref[...].astype(f32))
        small_ref[SELF_OUT_BIAS : SELF_OUT_BIAS + 1] = row_sum(dz1.astype(bf16))
        dz_buf[...] = dz1
        outs = [copy(dz_buf, dz1_hbm, sems.at[after])]
        outs[0].start()
        small_ref[CROSS_BIAS : CROSS_BIAS + 1] = feature_sum(dq_all)
        small_ref[CROSS_BIAS + 1 : CROSS_BIAS + 2] = feature_sum(dkv_buf[width:, :])
        grad_buf[:, :width] = dot(h1_ref[...], dq_all, 0, 1).astype(bf16)
        grad_buf[:, width : 2 * width] = dot(
            o_buf[...], dz2_ref[...].astype(bf16), 1, 0
        ).astype(bf16)
        key_grad = value_grad = None
        for b in range(holders):
            columns = slice(b * part_rows, (b + 1) * part_rows)
            dkv = dkv_buf[:, columns]
            k_part = dot(m_ref[b], dkv[:width], 0, 1)
            v_part = dot(m_ref[b], dkv[width:], 0, 1)
            key_grad = k_part if b == 0 else key_grad + k_part
            value_grad = v_part if b == 0 else value_grad + v_part
        grad_buf[:, 2 * width : 3 * width] = key_grad.astype(bf16)
        grad_buf[:, 3 * width :] = value_grad.astype(bf16)
        outs += halves(digit_ref, grad_buf, keeps, sends, sems, after + 1)
        outs += [part_out(at, which) for at in range(HEADS // PAIR) for which in range(2)]
        wait(outs)


def halves(digit_ref, grad_buf, keeps, sends, sems, at):
    rows = grad_buf.shape[0] // 2
    result, begin = [], 0
    for keep, send in zip(keeps, sends):
        columns = slice(begin, begin + keep.shape[1])
        begin += keep.shape[1]
        for i, target in enumerate((keep, send)):
            mine = pl.ds(pl.multiple_of((digit_ref[0] ^ i) * rows, rows), rows)
            sem = sems.at[at + len(result)]
            result.append(pltpu.make_async_copy(grad_buf.at[mine, columns], target, sem))
            result[-1].start()
    return result


def back_start_kernel(digit_ref, dz_ref, inv_ref, out_w, do_ref):
    back_heads(do_ref, out_w, dz_ref[...].astype(bf16), inv_ref)


def self_backward_kernel(
    digit_ref, e_ref, inv_ref, o_ref, q_ref, k_ref, v_ref, dz1_ref, out_w,
    dq_ref, dk_ref, dv_ref, do_buf,
):
    step = pl.program_id(0)
    pair, length = q_ref.shape
    size = pair // PAIR
    blocks = length // BLOCK

    @pl.when(step == 0)
    def _():
        back_heads(do_buf, out_w, dz1_ref[...].astype(bf16), inv_ref)

    base = pl.multiple_of(step * pair, pair)
    for one in range(PAIR):
        here = slice(one * size, (one + 1) * size)
        do = back_head(do_buf[pl.ds(base + one * size, size), :], o_ref[here, :])
        q, k, v = q_ref[here, :], k_ref[here, :], with_ones(v_ref[here, :])
        dq = [None] * blocks
        for i in range(blocks):
            mine = slice(i * BLOCK, (i + 1) * BLOCK)
            several = min(blocks - i, REACH + 1)
            seen = slice(i * BLOCK, (i + several) * BLOCK)
            weights = e_ref[one, i, :, : several * BLOCK]
            ds = (weights.astype(f32) * dot(v[:, mine], do[:, seen], 0, 0)).astype(bf16)
            dv_ref[here, mine] = dot(do[:size, seen], weights, 1, 1).astype(bf16)
            dk_ref[here, mine] = (dot(q[:, seen], ds, 1, 1) * LN2).astype(bf16)
            part = dot(k[:, mine], ds, 1, 0)
            for b in range(several):
                piece = part[:, b * BLOCK : (b + 1) * BLOCK]
                dq[i + b] = piece if dq[i + b] is None else dq[i + b] + piece
        for j in range(blocks):
            dq_ref[here, j * BLOCK : (j + 1) * BLOCK] = (dq[j] * size**-0.5).astype(bf16)


def self_weights_kernel(
    digit_ref, old_ref, x_hbm, dq_hbm, dk_hbm, dv_hbm, dz1_hbm, o_hbm, *refs
):
    keeps, sends, refs = refs[:2], refs[2:4], refs[4:]
    (
        x_ref, dq_ref, dk_ref, dv_ref, dz1_ref, o_ref, grad_buf, sems,
    ) = refs
    width = x_ref.shape[1]
    refs = (x_ref, dq_ref, dk_ref, dv_ref, dz1_ref, o_ref)
    loads = [
        pltpu.make_async_copy(source, target, sems.at[i])
        for i, (source, target) in enumerate(
            zip((x_hbm, dq_hbm, dk_hbm, dv_hbm, dz1_hbm, o_hbm), refs)
        )
    ]
    start(loads)
    loads[0].wait()
    sums = []
    for part, ref in enumerate((dq_ref, dk_ref, dv_ref)):
        loads[1 + part].wait()
        d = ref[...]
        grad_buf[:, (part + 1) * width : (part + 2) * width] = dot(x_ref[...], d, 0, 1).astype(bf16)
        sums.append(feature_sum(d) if part != 1 else None)
    row = lax.broadcasted_iota(jnp.int32, old_ref.shape, 0)
    small = jnp.where(row == SELF_BIAS, sums[0], old_ref[...])
    small = jnp.where(row == SELF_BIAS + 1, sums[2], small)
    small = jnp.concatenate((small, jnp.zeros((LANES - SMALL, width), f32)), axis=0)
    grad_buf[:, 4 * width :] = jnp.transpose(small).astype(bf16)
    wait(loads[4:])
    grad_buf[:, :width] = dot(o_ref[...], dz1_ref[...].astype(bf16), 1, 0).astype(bf16)
    wait(halves(digit_ref, grad_buf, keeps, sends, sems, len(loads)))


def memory_kernel(digit_ref, dkv_ref, kv_w, *mem_refs):
    rows = mem_refs[0].shape[0]
    for b, mem_ref in enumerate(mem_refs):
        part = dkv_ref[:, b * rows : (b + 1) * rows]
        mem_ref[...] = dot(part, kv_w[...], 0, 1).astype(bf16)


def token_kernel(digit_ref, dq_ref, dk_ref, dv_ref, dz1_ref, par_ref, qkv_w, token_ref):
    width = dz1_ref.shape[1]
    total = par_ref[OMEGA : OMEGA + 1] * dz1_ref[...]
    for part, ref in enumerate((dq_ref, dk_ref, dv_ref)):
        total = total + dot(ref[...], qkv_w[:, part * width : (part + 1) * width], 0, 1)
    token_ref[...] = total.astype(bf16)


def tree_sum(values):
    while len(values) > 1:
        values = [a + b for a, b in zip(values[::2], values[1::2])]
    return values[0]


def combine_kernel(stage, outs, groups, *refs):
    sources, results = refs[1 : 1 + sum(groups)], refs[1 + sum(groups) :]
    rows = results[0].shape[0]
    for d in range(outs):
        begin = 0 if outs == 1 else pl.multiple_of((refs[0][stage] ^ d) * rows, rows)
        left, column = list(sources), 0
        for count in groups:
            group, left = left[:count], left[count:]
            total = tree_sum([ref[pl.ds(begin, rows), :].astype(f32) for ref in group])
            width = total.shape[1]
            results[d][:, column : column + width] = total.astype(bf16)
            column += width


def place_kernel(stage, ins, *refs):
    digit, sources, result = refs[0][stage], refs[1 : 1 + ins], refs[1 + ins]
    rows = sources[0].shape[0]
    for d in range(ins):
        result[pl.ds(pl.multiple_of((digit ^ d) * rows, rows), rows), :] = sources[d][...]


def finish_kernel(
    digit_ref, mine_hbm, other_hbm, cross_q, cross_out, cross_kv, self_out, self_qkv,
    self_bias, self_out_bias, cross_bias, cross_out_bias, in_bias, out_bias, omega, gain, shift,
    buf, last, *refs
):
    targets = (cross_q, cross_out, cross_kv, self_out, self_qkv)
    bufs, sems = refs[: len(targets)], refs[len(targets)]
    rows = mine_hbm.shape[0]
    loads = [
        pltpu.make_async_copy(source, buf.at[i], sems.at[2 * len(targets) + i])
        for i, source in enumerate((mine_hbm, other_hbm))
    ]
    start(loads)
    outs = []
    for half, load in enumerate(loads):
        load.wait()
        here = pl.ds(pl.multiple_of((digit_ref[0] ^ half) * rows, rows), rows)
        begin = 0
        for i, (target, wide) in enumerate(zip(targets, bufs)):
            count = target.shape[1]
            wide[half] = buf[half, :, begin : begin + count].astype(f32)
            sem = sems.at[2 * i + half]
            outs.append(pltpu.make_async_copy(wide.at[half], target.at[here], sem))
            outs[-1].start()
            begin += count
        last[here, :] = buf[half, :, begin:]
    part = jnp.transpose(last[...].astype(f32))
    begin = 0
    for target in (
        self_bias, self_out_bias, cross_bias, cross_out_bias, in_bias, out_bias, omega, gain, shift,
    ):
        count = target.shape[0]
        target[...] = part[begin : begin + count]
        begin += count
    wait(outs)


def spread_kernel(stage, digit_ref, *refs):
    *sources, target = refs
    for d, source in enumerate(sources):
        target[digit_ref[stage] ^ far_first(d, len(sources))] = source[...]


def ffn_finish_kernel(digit_ref, mine_hbm, other_hbm, out_hbm, in_hbm, buf, out_buf, in_buf, sems):
    rows, width = mine_hbm.shape
    chunks = out_hbm.shape[0] // width
    loads = [
        pltpu.make_async_copy(source, buf.at[digit_ref[0] ^ i], sems.at[2 * chunks + i])
        for i, source in enumerate((mine_hbm, other_hbm))
    ]
    start(loads)
    wait(loads)
    outs = []
    for c in range(chunks):
        half, place = c // (chunks // 2), c % (chunks // 2) * width
        out_buf[c] = buf[half, place : place + width, :].astype(f32)
        place += rows // 2
        in_buf[c] = buf[half, place : place + width, :].astype(f32)
        here = slice(c * width, (c + 1) * width)
        outs.append(pltpu.make_async_copy(out_buf.at[c], out_hbm.at[here], sems.at[2 * c]))
        outs.append(pltpu.make_async_copy(in_buf.at[c], in_hbm.at[:, here], sems.at[2 * c + 1]))
        start(outs[-2:])
    wait(outs)


class Order:
    def __init__(self, digits):
        self.digits = digits

    def after(self, value):
        return lax.optimization_barrier((value, self.digits))[0]

    def through(self, value):
        value, self.digits = lax.optimization_barrier((value, self.digits))
        return value

    def __call__(self, kernel, steps, ins, outs, scratch=(), vmem=VMEM, us=1):
        def whole(shape):
            return pl.BlockSpec(shape, lambda i: (0,) * len(shape), pipeline_mode=pl.Buffered(1))

        arrays, in_specs, shapes, out_specs = (
            [self.digits], [pl.BlockSpec(memory_space=pltpu.SMEM)], [], []
        )
        anywhere = pl.BlockSpec(memory_space=pl.ANY)
        for item in ins:
            if isinstance(item, tuple):
                arrays.append(item[0])
                in_specs.append(pl.BlockSpec(*item[1:]) if item[1:] else anywhere)
            else:
                arrays.append(item)
                in_specs.append(whole(item.shape))
        for shape, dtype, *block in outs:
            shapes.append(jax.ShapeDtypeStruct(shape, dtype))
            if block == [None]:
                out_specs.append(anywhere)
            elif block:
                out_specs.append(pl.BlockSpec(*block))
            else:
                out_specs.append(pl.BlockSpec(shape, lambda i, n=len(shape): (0,) * n))
        result = pl.pallas_call(
            kernel,
            grid=(steps,),
            in_specs=in_specs,
            out_specs=out_specs,
            out_shape=shapes,
            scratch_shapes=list(scratch),
            compiler_params=pltpu.CompilerParams(
                dimension_semantics=("arbitrary",), vmem_limit_bytes=vmem
            ),
            cost_estimate=pl.CostEstimate(flops=us * 10**9, bytes_accessed=0, transcendentals=0),
        )(*arrays)
        self.digits = lax.optimization_barrier((self.digits, result[0]))[0]
        return result


def stages_of(sizes):
    result = []
    for axis in ("dp", "ctx"):
        stride = 1
        while stride < sizes[axis]:
            left = sizes[axis] // stride
            count = 2 if (axis == "dp" and stride == 1) or left % 4 else 4
            result.append((axis, stride, count))
            stride *= count
    return result


class Sum:
    def __init__(self, order, stages, sizes, pieces):
        self.order, self.stages, self.sizes = order, stages, sizes
        self.stage, self.spread, self.pieces, self.others = 0, [], pieces, []
        self.send(0)

    def send(self, stage):
        axis, stride, count = self.stages[stage]
        pieces = self.pieces if len(self.pieces) > 1 else self.pieces * count
        self.got = [
            lax.ppermute(
                pieces[d], axis, [(i, i ^ (d * stride)) for i in range(self.sizes[axis])]
            )
            for d in range(1, count)
        ]

    def settle(self):
        self.spread.append(self.stage)
        self.stage += 1
        group = [self.pieces[0], *self.got]
        self.pieces, self.got = self.order(
            functools.partial(combine_kernel, self.stage, 1, [len(group)]), 1, group,
            [(group[0].shape, bf16)], vmem=SMALL_VMEM,
        ), []

    def join(self, other):
        self.others.append(other)

    def step(self):
        groups = [[one.pieces[0], *one.got] for one in (*self.others, self)]
        rows = groups[0][0].shape[0]
        width = sum(group[0].shape[1] for group in groups)
        outs = 1
        if self.stage < len(self.stages):
            if len(self.pieces) > 1:
                self.spread.append(self.stage)
            self.stage += 1
            if self.stage < len(self.stages):
                count = self.stages[self.stage][2]
                outs = count if rows % (PAD * count) == 0 else 1
            kernel = functools.partial(
                combine_kernel, self.stage, outs, [len(group) for group in groups]
            )
            rows //= outs
        else:
            stage = self.spread.pop()
            kernel = functools.partial(place_kernel, stage, len(groups[0]))
            rows *= len(groups[0])
        self.others = []
        self.pieces = self.order(
            kernel, 1, sum(groups, []), [((rows, width), bf16)] * outs, vmem=SMALL_VMEM
        )
        self.send(self.stage if self.stage < len(self.stages) else self.spread[-1])

    @property
    def last(self):
        return self.stage == len(self.stages) and len(self.spread) == 1


def local(sizes, *args):
    (
        tokens, memory, mem_mask, segment_ids, cotangent, self_qkv, self_bias, self_out,
        self_out_bias, cross_q, cross_kv, cross_bias, cross_out, cross_out_bias, ffn_in,
        ffn_in_bias, ffn_out, ffn_out_bias, omegas, ln_gains, ln_biases,
    ) = args
    length, width = tokens.shape[1:]
    hidden = ffn_in.shape[1]
    size = width // HEADS
    holders, part_rows = memory.shape[:2]
    count = holders * part_rows
    x = tokens.reshape(length, width)
    cot = cotangent.reshape(length, width)
    seg = segment_ids.reshape(1, length)
    stages = stages_of(sizes)
    digits = [(lax.axis_index(axis) // stride) % several for axis, stride, several in stages]
    first_ctx = [axis for axis, _, _ in stages].index("ctx")
    order = Order(jnp.stack(digits).astype(jnp.int32))

    blocks = length // BLOCK
    reach = (REACH + 1) * BLOCK

    pairs, pair = HEADS // PAIR, PAIR * size

    def scores_in(array):
        shape = (PAIR, *array.shape[1:])
        return (array, shape, lambda i: (i,) + (0,) * (len(shape) - 1))

    def scores_out(*shape):
        return ((HEADS, *shape), bf16, None)

    def pair_in(array, part=0):
        return (array, (pair, array.shape[1]), lambda i: (part * pairs + i, 0))

    def vmem(*shape, dtype=bf16):
        return pltpu.VMEM(shape, dtype)

    dma = pltpu.SemaphoreType.DMA
    tall, wide = (width, length), (length, width)
    small, *pieces = order(
        functools.partial(prepare_kernel, first_ctx),
        1,
        [
            memory, mem_mask, self_bias, self_out_bias, cross_bias, cross_out_bias, ffn_in_bias,
            ffn_out_bias, omegas, ln_gains, ln_biases,
        ],
        [((SMALL, width), f32)] + [((part_rows + PAD, width), bf16)] * holders,
    )

    def trade(pieces):
        return [pieces[0]] + [
            lax.ppermute(
                pieces[j], "ctx", [(i, i ^ far_first(j, holders)) for i in range(holders)]
            )
            for j in range(1, holders)
        ]

    pieces = trade(pieces)
    qkv, e_self, inv_self, o, z1, h1, q2 = order(
        self_forward_kernel,
        pairs,
        [x, seg, small, self_qkv, (self_out,), (cross_q,)],
        [
            ((3 * width, length), bf16, None),
            scores_out(blocks, BLOCK, reach),
            ((HEADS, length), f32),
            (tall, bf16, None),
            (wide, f32, None),
            (wide, bf16, None),
            (tall, bf16, None),
        ],
        [
            vmem(3 * width, length), vmem(2, PAIR, blocks, BLOCK, reach), vmem(*tall),
            vmem(*wide, dtype=f32), vmem(*wide), vmem(*tall),
            vmem(width, width), vmem(width, width), vmem(PAD, length), vmem(PAD, length), dma((7,)),
            dma((2, PAIR)),
        ],
        us=15,
    )
    kv, e_cross, inv_cross, o2, z2, h2 = order(
        functools.partial(cross_forward_kernel, holders),
        pairs,
        [pair_in(q2), small, cross_kv, (h1,), (cross_out,), *pieces],
        [
            ((2 * width, count), bf16, None),
            scores_out(count, length),
            ((HEADS, length), f32),
            (tall, bf16, None),
            (wide, f32, None),
            (wide, bf16, None),
        ],
        [
            vmem(2 * width, count), vmem(2, PAIR, count, length), vmem(*tall),
            vmem(*wide, dtype=f32), vmem(*wide), vmem(*wide), vmem(width, width), vmem(PAD, count),
            dma((6,)), dma((2, PAIR)),
        ],
        us=22,
    )
    rows = BLOCK
    chunks = hidden // width
    row_block = ((rows, width), lambda i: (i, 0))
    activations, dz2, keep, send, small_grad = order(
        ffn_kernel,
        length // rows,
        [
            (h2, *row_block), (h1, *row_block), (z2, *row_block), (cot, *row_block), small, ffn_in,
            (ffn_out,),
        ],
        [
            (wide, bf16, *row_block),
            (wide, f32, *row_block),
            ((hidden, width), bf16, None),
            ((hidden, width), bf16, None),
            ((SMALL, width), f32),
        ],
        [
            vmem(*wide), vmem(length, hidden), vmem(rows, hidden, dtype=f32), vmem(*wide),
            vmem(length, hidden), vmem(2, hidden, width), vmem(hidden, width),
            dma((2 * chunks + 1,)),
        ],
        us=26,
    )
    def open_sum(parts):
        several = len(parts) // 2
        *others, last = [
            Sum(order, stages, sizes, [keep, send])
            for keep, send in zip(parts[:several], parts[several:])
        ]
        for one in others:
            last.join(one)
        return last

    ffn_sum = open_sum([keep, send])
    (do2,) = order(back_start_kernel, 1, [dz2, inv_cross, cross_out], [(tall, bf16)], us=3)
    ffn_sum.step()
    parts = [((width // 2, 2 * width), bf16, None)] * 4
    dkv, dz1, small_grad, p0, p1, p2, p3 = order(
        functools.partial(cross_backward_kernel, holders),
        pairs,
        [
            scores_in(e_cross), pair_in(do2), pair_in(o2), pair_in(q2), pair_in(kv), pair_in(kv, 1),
            small, small_grad, (z1,), (h1,), (x,), (cross_q,), (dz2,),
            *[(piece,) for piece in pieces],
        ],
        [((2 * width, count), bf16, None), (wide, f32, None), ((SMALL, width), f32)] + parts,
        [
            vmem(*wide, dtype=f32), vmem(*wide), vmem(*wide), vmem(width, width),
            vmem(*wide, dtype=f32), vmem(*memory.shape), vmem(*tall), vmem(*tall),
            vmem(2 * width, count), vmem(*wide, dtype=f32), vmem(width, 4 * width),
            dma((5 + holders + 5 + 2 * pairs,)),
        ],
        us=26,
    )
    cross_sum = open_sum([p0, p1, p2, p3])
    ffn_sum.step()
    cross_sum.step()
    total = 4 * width + LANES
    pair_out = (tall, bf16, (pair, length), lambda i: (i, 0))
    dq, dk, dv = order(
        self_backward_kernel,
        pairs,
        [
            scores_in(e_self), inv_self, pair_in(o), pair_in(qkv), pair_in(qkv, 1), pair_in(qkv, 2),
            dz1, self_out,
        ],
        [pair_out] * 3,
        [vmem(*tall)],
        us=16,
    )
    for _ in range(first_ctx - 2):
        cross_sum.step()
    cross_sum.settle()
    ffn_sum.step()
    parts = [((width // 2, some), bf16, None) for some in (2 * width, 2 * width + LANES)] * 2
    self_sum = open_sum(
        order(
            self_weights_kernel,
            1,
            [small_grad, (x,), (dq,), (dk,), (dv,), (dz1,), (o,)],
            parts,
            [
                vmem(*wide), vmem(*tall), vmem(*tall), vmem(*tall), vmem(*wide, dtype=f32),
                vmem(*tall), vmem(width, total), dma((6 + 10,)),
            ],
            us=7,
        )
    )
    mem_parts = order(
        memory_kernel, 1, [dkv, cross_kv], [((part_rows, width), bf16)] * holders, us=3
    )
    for _ in range(first_ctx - 1):
        self_sum.step()
    self_sum.join(cross_sum)
    self_sum.step()
    ffn_sum.step()
    self_sum.step()
    turned = ((width, rows), lambda i: (0, i))
    (token_grad,) = order(
        token_kernel,
        length // rows,
        [(dq, *turned), (dk, *turned), (dv, *turned), (dz1, *row_block), small, self_qkv],
        [(wide, bf16, *row_block)],
        us=6,
    )
    while not ffn_sum.last:
        ffn_sum.step()
    while len(self_sum.spread) > 2 or self_sum.stage < len(stages):
        self_sum.step()
    mem_parts = trade(order.after(mem_parts))
    (memory_grad,) = order(
        functools.partial(spread_kernel, first_ctx), 1, mem_parts, [(memory.shape, bf16)],
        vmem=SMALL_VMEM,
    )
    self_sum.step()
    while not self_sum.last:
        self_sum.step()
    square = (width, width)
    grad_ffn_out, grad_ffn_in = order(
        ffn_finish_kernel,
        1,
        [(ffn_sum.pieces[0],), (ffn_sum.got[0],)],
        [((hidden, width), f32, None), ((width, hidden), f32, None)],
        [
            vmem(2, hidden, width), vmem(chunks, *square, dtype=f32),
            vmem(chunks, *square, dtype=f32), dma((2 * chunks + 2,)),
        ],
        vmem=SMALL_VMEM,
    )
    shapes = [(width, several * width) for several in (1, 1, 2, 1, 3)]
    shapes += [(several, width) for several in (2, 1, 2, 1, chunks, 1, 3, 3, 3)]
    large = [shape for shape in shapes if shape[0] == width]
    grad_cross_q, grad_cross_out, grad_cross_kv, grad_out, grad_qkv, *smalls = order(
        finish_kernel,
        1,
        [(self_sum.pieces[0],), (self_sum.got[0],)],
        [(shape, f32, None) if shape in large else (shape, f32) for shape in shapes],
        [
            vmem(2, width // 2, 8 * width + LANES), vmem(width, LANES),
            *[vmem(2, width // 2, shape[1], dtype=f32) for shape in large], dma((12,)),
        ],
        vmem=SMALL_VMEM,
    )
    (
        self_bias, self_out_bias, cross_bias, cross_out_bias, in_bias, out_bias, omega, gain, shift
    ) = smalls
    return (
        activations.reshape(tokens.shape),
        token_grad.reshape(tokens.shape),
        memory_grad,
        grad_qkv,
        self_bias,
        grad_out,
        self_out_bias.reshape(-1),
        grad_cross_q,
        grad_cross_kv,
        cross_bias,
        grad_cross_out,
        cross_out_bias.reshape(-1),
        grad_ffn_in,
        in_bias.reshape(-1),
        grad_ffn_out,
        out_bias.reshape(-1),
        omega,
        gain,
        shift,
    )


def solution(mesh):
    sizes = dict(mesh.shape)
    both = P(("dp", "ctx"), None, None)
    return jax.shard_map(
        functools.partial(local, sizes),
        mesh=mesh,
        in_specs=(both, P("dp", "ctx", None), P("dp", "ctx"), P(("dp", "ctx"), None), both)
        + (P(),) * 16,
        out_specs=(both, both, P("dp", "ctx", None)) + (P(),) * 16,
        check_vma=False,
    )
```

```python
import functools

import jax
import jax.numpy as jnp
from jax import lax
from jax.experimental import pallas as pl
from jax.experimental.pallas import tpu as pltpu
from jax.sharding import PartitionSpec as P

HEADS = 8
PAIR = 2
LOG2E = 1.4426950408889634
LN2 = 0.6931471805599453
UNSEEN = -1e30
BLOCK = 256
REACH = 2
PAD = 16
VMEM = 60 * 2**20
SMALL_VMEM = 24 * 2**20
bf16, f32 = jnp.bfloat16, jnp.float32

SELF_BIAS, SELF_OUT_BIAS, CROSS_BIAS, CROSS_OUT_BIAS = 0, 2, 3, 5
FFN_IN_BIAS, FFN_OUT_BIAS, OMEGA, GAIN, SHIFT, SMALL = 6, 10, 11, 14, 17, 24
LANES = 128


def dot(left, right, left_dim, right_dim):
    return lax.dot_general(
        left, right, (((left_dim,), (right_dim,)), ((), ())), preferred_element_type=f32
    )


def column(row):
    return jnp.transpose(jnp.broadcast_to(row, (8, row.shape[1])))[:, :1]


def row_sum(value):
    return jnp.sum(value.astype(f32), axis=0, keepdims=True)


def feature_sum(value):
    ones = jnp.ones((PAD, value.shape[1]), bf16)
    return dot(ones, value, 1, 1)[:1]


def normalize(value):
    centered = value - jnp.mean(value, axis=-1, keepdims=True)
    spread = jnp.mean(centered * centered, axis=-1, keepdims=True)
    inverse = lax.rsqrt(spread + 1e-05)
    return centered * inverse, inverse


def normalize_back(grad, gain, normal, inverse):
    scaled = grad * gain
    mean = jnp.mean(scaled, axis=-1, keepdims=True)
    slope = jnp.mean(scaled * normal, axis=-1, keepdims=True)
    return (scaled - mean - normal * slope) * inverse


def with_ones(rows):
    return jnp.concatenate((rows, jnp.ones((PAD, rows.shape[1]), bf16)), axis=0)


def start(copies):
    for copy in copies:
        copy.start()


def wait(copies):
    for copy in copies:
        copy.wait()


def score_copies(step, buf, hbm, sems):
    slot = lax.rem(step, 2)
    return [
        pltpu.make_async_copy(buf.at[slot, one], hbm.at[step * PAIR + one], sems.at[slot, one])
        for one in range(PAIR)
    ]


def far_first(place, count):
    return (count - place) % count


def prepare_kernel(stage, digit_ref, memory_ref, mask_ref, *refs):
    _, part_rows, width = memory_ref.shape
    params, par_ref, pieces = refs[:9], refs[9], refs[10:]
    row = 0
    for ref in params:
        value = ref[...].astype(f32)
        if value.ndim == 2:
            par_ref[row : row + value.shape[0], :] = value
            row += value.shape[0]
        else:
            for begin in range(0, value.shape[0], width):
                par_ref[row : row + 1, :] = value[begin : begin + width].reshape(1, width)
                row += 1
    par_ref[row:, :] = jnp.zeros((par_ref.shape[0] - row, width), f32)
    for d, piece in enumerate(pieces):
        index = digit_ref[stage] ^ far_first(d, len(pieces))
        piece[:part_rows, :] = memory_ref[index]
        mask = mask_ref[pl.ds(index, 1), :].astype(f32)
        mask = jnp.concatenate((mask, jnp.zeros((1, width - part_rows), f32)), axis=1)
        piece[part_rows:, :] = jnp.broadcast_to(mask, (PAD, width)).astype(bf16)


def self_forward_kernel(
    digit_ref, x_ref, seg_ref, par_ref, qkv_w, out_hbm, cross_hbm,
    qkv_hbm, e_hbm, inv_ref, o_hbm, z_hbm, h_hbm, q_hbm,
    qkv_ref, e_ref, o_ref, z_ref, h_ref, q_ref, out_w, cross_w, q_mask, k_mask, sems, e_sems,
):
    step = pl.program_id(0)
    last = pl.num_programs(0) - 1
    length, width = x_ref.shape
    size = width // HEADS
    scale = size**-0.5 * LOG2E
    copy = pltpu.make_async_copy
    loads = [copy(out_hbm, out_w, sems.at[0]), copy(cross_hbm, cross_w, sems.at[1])]
    projected = copy(qkv_ref, qkv_hbm, sems.at[2])

    @pl.when(step == 0)
    def _():
        start(loads)
        x = x_ref[...]
        for part, row in ((0, 0), (1, None), (2, 1)):
            columns = slice(part * width, (part + 1) * width)
            value = dot(qkv_w[:, columns], x, 0, 1)
            if row is not None:
                value = value + column(par_ref[SELF_BIAS + row : SELF_BIAS + row + 1])
            if part == 0:
                value = value * scale
            qkv_ref[columns, :] = value.astype(bf16)
        projected.start()
        same = lax.broadcasted_iota(jnp.int32, (PAD, length), 0) == seg_ref[...]
        q_mask[...] = jnp.where(same, 1.0, 0.0).astype(bf16)
        k_mask[...] = jnp.where(same, 0.0, UNSEEN).astype(bf16)

    causal = lax.broadcasted_iota(jnp.int32, (BLOCK, BLOCK), 0) <= lax.broadcasted_iota(
        jnp.int32, (BLOCK, BLOCK), 1
    )
    blocks = length // BLOCK
    slot = lax.rem(step, 2)

    @pl.when(step >= 2)
    def _():
        wait(score_copies(step - 2, e_ref, e_hbm, e_sems))

    for one in range(PAIR):
        head = step * PAIR + one
        base = pl.multiple_of(head * size, size)
        q = jnp.concatenate((qkv_ref[pl.ds(base, size), :], q_mask[...]), axis=0)
        k = jnp.concatenate((qkv_ref[pl.ds(width + base, size), :], k_mask[...]), axis=0)
        v = with_ones(qkv_ref[pl.ds(2 * width + base, size), :])
        scores, tops, mixed = [], [None] * blocks, [None] * blocks
        for i in range(blocks):
            s = dot(k[:, i * BLOCK : (i + 1) * BLOCK], q[:, i * BLOCK : (i + REACH + 1) * BLOCK], 0, 0)
            diagonal = jnp.where(causal, s[:, :BLOCK], UNSEEN)
            if s.shape[1] > BLOCK:
                diagonal = jnp.concatenate((diagonal, s[:, BLOCK:]), axis=1)
            scores.append(diagonal)
            top = jnp.max(diagonal, axis=0, keepdims=True)
            for b in range(s.shape[1] // BLOCK):
                part = top[:, b * BLOCK : (b + 1) * BLOCK]
                old = tops[i + b]
                tops[i + b] = part if old is None else jnp.maximum(old, part)
        for i, s in enumerate(scores):
            several = s.shape[1] // BLOCK
            weights = jnp.exp2(s - jnp.concatenate(tops[i : i + several], axis=1)).astype(bf16)
            e_ref[slot, one, i, :, : several * BLOCK] = weights
            part = dot(v[:, i * BLOCK : (i + 1) * BLOCK], weights, 1, 0)
            for b in range(several):
                piece = part[:, b * BLOCK : (b + 1) * BLOCK]
                mixed[i + b] = piece if mixed[i + b] is None else mixed[i + b] + piece
        for j, value in enumerate(mixed):
            mine = slice(j * BLOCK, (j + 1) * BLOCK)
            inverse = 1.0 / value[size : size + 1]
            o_ref[pl.ds(base, size), mine] = (value[:size] * inverse).astype(bf16)
            inv_ref[pl.ds(head, 1), mine] = inverse
    start(score_copies(step, e_ref, e_hbm, e_sems))

    @pl.when(step == last)
    def _():
        outs = [
            copy(o_ref, o_hbm, sems.at[3]),
            copy(z_ref, z_hbm, sems.at[4]),
            copy(h_ref, h_hbm, sems.at[5]),
            copy(q_ref, q_hbm, sems.at[6]),
        ]
        outs[0].start()
        wait(loads)
        z = (
            par_ref[OMEGA : OMEGA + 1] * x_ref[...].astype(f32)
            + dot(o_ref[...], out_w[...], 0, 0)
            + par_ref[SELF_OUT_BIAS : SELF_OUT_BIAS + 1]
        )
        z_ref[...] = z
        outs[1].start()
        normal, _ = normalize(z)
        h = (normal * par_ref[GAIN : GAIN + 1] + par_ref[SHIFT : SHIFT + 1]).astype(bf16)
        h_ref[...] = h
        outs[2].start()
        value = dot(cross_w[...], h, 0, 1) + column(par_ref[CROSS_BIAS : CROSS_BIAS + 1])
        q_ref[...] = (value * scale).astype(bf16)
        outs[3].start()
        wait([projected, *outs])
        wait(score_copies(step - 1, e_ref, e_hbm, e_sems))
        wait(score_copies(step, e_ref, e_hbm, e_sems))


def cross_forward_kernel(
    holders, digit_ref, q_ref, par_ref, kv_w, h1_hbm, out_hbm, *refs
):
    pieces, refs = refs[:holders], refs[holders:]
    kv_hbm, e_hbm, inv_ref, o_hbm, z_hbm, h_hbm, *refs = refs
    kv_ref, e_ref, o_ref, z_ref, h_ref, h1_ref, out_w, k_mask, sems, e_sems = refs
    step = pl.program_id(0)
    last = pl.num_programs(0) - 1
    length, width = h1_ref.shape
    size = width // HEADS
    part_rows = pieces[0].shape[0] - PAD
    copy = pltpu.make_async_copy
    loads = [copy(h1_hbm, h1_ref, sems.at[0]), copy(out_hbm, out_w, sems.at[1])]
    projected = copy(kv_ref, kv_hbm, sems.at[2])

    @pl.when(step == 0)
    def _():
        start(loads)
        shift = column(par_ref[CROSS_BIAS + 1 : CROSS_BIAS + 2])
        first = lax.broadcasted_iota(jnp.int32, (PAD, part_rows), 0) == 0
        for b, piece in enumerate(pieces):
            columns = slice(b * part_rows, (b + 1) * part_rows)
            m = piece[:part_rows, :]
            kv_ref[:width, columns] = dot(kv_w[:, :width], m, 0, 1).astype(bf16)
            kv_ref[width:, columns] = (dot(kv_w[:, width:], m, 0, 1) + shift).astype(bf16)
            seen = piece[part_rows:, :part_rows].astype(f32) > 0.5
            k_mask[:, columns] = jnp.where(first & ~seen, UNSEEN, 0.0).astype(bf16)
        projected.start()

    slot = lax.rem(step, 2)

    @pl.when(step >= 2)
    def _():
        wait(score_copies(step - 2, e_ref, e_hbm, e_sems))

    heads = []
    for one in range(PAIR):
        base = pl.multiple_of((step * PAIR + one) * size, size)
        heads.append(
            (
                with_ones(q_ref[one * size : (one + 1) * size, :]),
                jnp.concatenate((kv_ref[pl.ds(base, size), :], k_mask[...]), axis=0),
                with_ones(kv_ref[pl.ds(width + base, size), :]),
            )
        )
    blocks = [slice(i, i + BLOCK) for i in range(0, kv_ref.shape[1], BLOCK)]

    def block_scores(one, block):
        q, k, _ = heads[one]
        scores = dot(k[:, block], q, 0, 0)
        return scores, jnp.max(scores, axis=0, keepdims=True)

    now = [block_scores(0, block) for block in blocks]
    for one in range(PAIR):
        top = functools.reduce(jnp.maximum, [each for _, each in now])
        later, weights = [], []
        for (scores, _), block in zip(now, blocks):
            if one + 1 < PAIR:
                later.append(block_scores(one + 1, block))
            weights.append(jnp.exp2(scores - top).astype(bf16))
            e_ref[slot, one, block, :] = weights[-1]
        mixed = None
        for weight, block in zip(weights, blocks):
            part = dot(heads[one][2][:, block], weight, 1, 0)
            mixed = part if mixed is None else mixed + part
        inverse = 1.0 / mixed[size : size + 1]
        head = step * PAIR + one
        o_ref[pl.ds(pl.multiple_of(head * size, size), size), :] = (mixed[:size] * inverse).astype(
            bf16
        )
        inv_ref[pl.ds(head, 1), :] = inverse
        now = later
    start(score_copies(step, e_ref, e_hbm, e_sems))

    @pl.when(step == last)
    def _():
        outs = [
            copy(o_ref, o_hbm, sems.at[3]),
            copy(z_ref, z_hbm, sems.at[4]),
            copy(h_ref, h_hbm, sems.at[5]),
        ]
        outs[0].start()
        wait(loads)
        z = (
            par_ref[OMEGA + 1 : OMEGA + 2] * h1_ref[...].astype(f32)
            + dot(o_ref[...], out_w[...], 0, 0)
            + par_ref[CROSS_OUT_BIAS : CROSS_OUT_BIAS + 1]
        )
        z_ref[...] = z
        outs[1].start()
        normal, _ = normalize(z)
        h_ref[...] = (
            normal * par_ref[GAIN + 1 : GAIN + 2] + par_ref[SHIFT + 1 : SHIFT + 2]
        ).astype(bf16)
        outs[2].start()
        wait([projected, *outs])
        wait(score_copies(step - 1, e_ref, e_hbm, e_sems))
        wait(score_copies(step, e_ref, e_hbm, e_sems))


def ffn_kernel(
    digit_ref, h2_ref, h1_ref, z2_ref, cot_ref, par_ref, in_w, out_hbm,
    act_ref, dz_ref, keep_hbm, send_hbm, small_ref,
    h_buf, g_buf, slope_buf, e_buf, eu_buf, grad_buf, out_w, sems,
):
    step = pl.program_id(0)
    rows, width = cot_ref.shape
    hidden = in_w.shape[1]
    chunks = hidden // width
    begin = pl.multiple_of(step * rows, rows)
    mine = pl.ds(begin, rows)
    load = pltpu.make_async_copy(out_hbm, out_w, sems.at[2 * chunks])

    @pl.when(step == 0)
    def _():
        load.start()
        small_ref[...] = jnp.zeros_like(small_ref)

    def add(row, value):
        small_ref[row : row + 1] += row_sum(value)

    h2 = h2_ref[...]
    h_buf[mine, :] = h2
    h2_wide = h2.astype(f32)
    for c in range(chunks):
        columns = slice(c * width, (c + 1) * width)
        u = dot(h2, in_w[:, columns], 1, 0) + par_ref[FFN_IN_BIAS + c : FFN_IN_BIAS + c + 1]
        rate = 0.7978845608028654
        square = u * u
        t = jnp.tanh(u * (rate + (rate * 0.044715) * square))
        half = 0.5 + 0.5 * t
        g_buf[mine, columns] = (u * half).astype(bf16)
        slope_buf[:, columns] = half + (0.5 * u) * (1.0 - t * t) * (
            rate + (3 * rate * 0.044715) * square
        )

    @pl.when(step == 0)
    def _():
        load.wait()

    z3 = (
        par_ref[OMEGA + 2 : OMEGA + 3] * h2_wide
        + dot(g_buf[mine, :], out_w[...], 1, 0)
        + par_ref[FFN_OUT_BIAS : FFN_OUT_BIAS + 1]
    )
    normal, inverse = normalize(z3)
    gain = par_ref[GAIN + 2 : GAIN + 3]
    act_ref[...] = (normal * gain + par_ref[SHIFT + 2 : SHIFT + 3]).astype(bf16)
    dy = cot_ref[...].astype(f32)
    add(GAIN + 2, dy * normal)
    add(SHIFT + 2, dy)
    dz3 = normalize_back(dy, gain, normal, inverse)
    add(OMEGA + 2, dz3 * h2_wide)
    e3 = dz3.astype(bf16)
    e_buf[mine, :] = e3
    add(FFN_OUT_BIAS, e3)
    for c in range(chunks):
        columns = slice(c * width, (c + 1) * width)
        eu = (dot(e3, out_w[columns, :], 1, 1) * slope_buf[:, columns]).astype(bf16)
        eu_buf[mine, columns] = eu
        add(FFN_IN_BIAS + c, eu)
    dh2 = par_ref[OMEGA + 2 : OMEGA + 3] * dz3 + dot(eu_buf[mine, :], in_w[...], 1, 1)
    normal, inverse = normalize(z2_ref[...])
    add(GAIN + 1, dh2 * normal)
    add(SHIFT + 1, dh2)
    dz2 = normalize_back(dh2, par_ref[GAIN + 1 : GAIN + 2], normal, inverse)
    add(OMEGA + 1, dz2 * h1_ref[...].astype(f32))
    add(CROSS_OUT_BIAS, dz2.astype(bf16))
    dz_ref[...] = dz2

    @pl.when(step == pl.num_programs(0) - 1)
    def _():
        outs = []
        for half in range(2):
            mine = [c for c in range(chunks) if c // (chunks // 2) == half]
            for i, c in enumerate(mine + [chunks + c for c in mine]):
                columns = slice(c % chunks * width, (c % chunks + 1) * width)
                if c < chunks:
                    value = dot(g_buf[:, columns], e_buf[...], 0, 0)
                else:
                    value = dot(h_buf[...], eu_buf[:, columns], 0, 0)
                place = slice(i * width, (i + 1) * width)
                grad_buf[half, place, :] = value.astype(bf16)
                sem = sems.at[half * chunks + i]
                source = grad_buf.at[half, place]
                keep = pltpu.make_async_copy(source, keep_hbm.at[place], sem)
                send = pltpu.make_async_copy(source, send_hbm.at[place], sem)
                pl.when(digit_ref[0] == half)(keep.start)
                pl.when(digit_ref[0] != half)(send.start)
                outs.append(keep)
        wait(outs)


def back_heads(do_ref, out_w, e, inv_ref):
    value = dot(out_w[...], e, 1, 1)
    size = value.shape[0] // HEADS
    for i in range(HEADS):
        rows = slice(i * size, (i + 1) * size)
        do_ref[rows, :] = (value[rows] * inv_ref[i : i + 1]).astype(bf16)


def back_head(do_rows, o_rows):
    length = do_rows.shape[1]
    delta = jnp.sum(do_rows.astype(f32) * o_rows.astype(f32), axis=0, keepdims=True)
    high = delta.astype(bf16).astype(f32)
    row = lax.broadcasted_iota(jnp.int32, (PAD, length), 0)
    extra = jnp.where(row == 0, -high, jnp.where(row == 1, high - delta, 0.0))
    return jnp.concatenate((do_rows, extra.astype(bf16)), axis=0)


def cross_backward_kernel(
    holders, digit_ref, e_ref, do_ref, o_ref, q_ref, k_ref, v_ref, par_ref, old_ref,
    z1_hbm, h1_hbm, x_hbm, qw_hbm, dz2_hbm, *refs
):
    m_hbm, refs = refs[:holders], refs[holders:]
    dkv_hbm, dz1_hbm, small_ref, *refs = refs
    keeps, sends, refs = refs[:2], refs[2:4], refs[4:]
    z1_ref, h1_ref, x_ref, q_w, dz2_ref, m_ref, *refs = refs
    o_buf, dq_buf, dkv_buf, dz_buf, grad_buf, sems = refs
    step = pl.program_id(0)
    last = pl.num_programs(0) - 1
    length, width = x_ref.shape
    size = width // HEADS
    count = k_ref.shape[1]
    pair = PAIR * size
    part_rows = m_ref.shape[1]
    copy = pltpu.make_async_copy
    pairs_of = [(z1_hbm, z1_ref), (h1_hbm, h1_ref), (x_hbm, x_ref), (qw_hbm, q_w)]
    pairs_of += [(dz2_hbm, dz2_ref)]
    pairs_of += [(source.at[:part_rows], m_ref.at[b]) for b, source in enumerate(m_hbm)]
    loads = [copy(source, target, sems.at[i]) for i, (source, target) in enumerate(pairs_of)]

    def part_out(at, which):
        rows = pl.ds(pl.multiple_of(which * width + at * pair, pair), pair)
        return copy(dkv_buf.at[rows], dkv_hbm.at[rows], sems.at[len(loads) + 5 + 2 * at + which])

    @pl.when(step == 0)
    def _():
        start(loads)
        small_ref[...] = old_ref[...]

    base = pl.multiple_of(step * pair, pair)
    o_buf[pl.ds(base, pair), :] = o_ref[...]
    heads = []
    for one in range(PAIR):
        here = slice(one * size, (one + 1) * size)
        heads.append(
            (
                back_head(do_ref[here, :], o_ref[here, :]),
                q_ref[here, :],
                k_ref[here, :],
                with_ones(v_ref[here, :]),
            )
        )
    dq = [None] * PAIR
    for i in range(count // BLOCK):
        mine = slice(i * BLOCK, (i + 1) * BLOCK)
        for one, (do, q, k, v) in enumerate(heads):
            weights = e_ref[one, mine, :]
            ds = (weights.astype(f32) * dot(v[:, mine], do, 0, 0)).astype(bf16)
            begin = base + one * size
            dkv_buf[pl.ds(width + begin, size), mine] = dot(do[:size], weights, 1, 1).astype(bf16)
            dkv_buf[pl.ds(begin, size), mine] = (dot(q, ds, 1, 1) * LN2).astype(bf16)
            part = dot(k[:, mine], ds, 1, 0)
            dq[one] = part if i == 0 else dq[one] + part
    for one in range(PAIR):
        dq_buf[pl.ds(base + one * size, size), :] = (dq[one] * size**-0.5).astype(bf16)
    start([part_out(step, 0), part_out(step, 1)])

    @pl.when(step == last)
    def _():
        wait(loads)
        after = len(loads)
        dq_all = dq_buf[...]
        dh1 = par_ref[OMEGA + 1 : OMEGA + 2] * dz2_ref[...] + dot(dq_all, q_w[...], 0, 1)
        normal, inverse = normalize(z1_ref[...])
        small_ref[GAIN : GAIN + 1] = row_sum(dh1 * normal)
        small_ref[SHIFT : SHIFT + 1] = row_sum(dh1)
        dz1 = normalize_back(dh1, par_ref[GAIN : GAIN + 1], normal, inverse)
        small_ref[OMEGA : OMEGA + 1] = row_sum(dz1 * x_ref[...].astype(f32))
        small_ref[SELF_OUT_BIAS : SELF_OUT_BIAS + 1] = row_sum(dz1.astype(bf16))
        dz_buf[...] = dz1
        outs = [copy(dz_buf, dz1_hbm, sems.at[after])]
        outs[0].start()
        small_ref[CROSS_BIAS : CROSS_BIAS + 1] = feature_sum(dq_all)
        small_ref[CROSS_BIAS + 1 : CROSS_BIAS + 2] = feature_sum(dkv_buf[width:, :])
        grad_buf[:, :width] = dot(h1_ref[...], dq_all, 0, 1).astype(bf16)
        grad_buf[:, width : 2 * width] = dot(
            o_buf[...], dz2_ref[...].astype(bf16), 1, 0
        ).astype(bf16)
        key_grad = value_grad = None
        for b in range(holders):
            columns = slice(b * part_rows, (b + 1) * part_rows)
            dkv = dkv_buf[:, columns]
            k_part = dot(m_ref[b], dkv[:width], 0, 1)
            v_part = dot(m_ref[b], dkv[width:], 0, 1)
            key_grad = k_part if b == 0 else key_grad + k_part
            value_grad = v_part if b == 0 else value_grad + v_part
        grad_buf[:, 2 * width : 3 * width] = key_grad.astype(bf16)
        grad_buf[:, 3 * width :] = value_grad.astype(bf16)
        outs += halves(digit_ref, grad_buf, keeps, sends, sems, after + 1)
        outs += [part_out(at, which) for at in range(HEADS // PAIR) for which in range(2)]
        wait(outs)


def halves(digit_ref, grad_buf, keeps, sends, sems, at):
    rows = grad_buf.shape[0] // 2
    result, begin = [], 0
    for keep, send in zip(keeps, sends):
        columns = slice(begin, begin + keep.shape[1])
        begin += keep.shape[1]
        for i, target in enumerate((keep, send)):
            mine = pl.ds(pl.multiple_of((digit_ref[0] ^ i) * rows, rows), rows)
            sem = sems.at[at + len(result)]
            result.append(pltpu.make_async_copy(grad_buf.at[mine, columns], target, sem))
            result[-1].start()
    return result


def back_start_kernel(digit_ref, dz_ref, inv_ref, out_w, do_ref):
    back_heads(do_ref, out_w, dz_ref[...].astype(bf16), inv_ref)


def self_backward_kernel(
    digit_ref, e_ref, inv_ref, o_ref, q_ref, k_ref, v_ref, dz1_ref, out_w,
    dq_ref, dk_ref, dv_ref, do_buf,
):
    step = pl.program_id(0)
    pair, length = q_ref.shape
    size = pair // PAIR
    blocks = length // BLOCK

    @pl.when(step == 0)
    def _():
        back_heads(do_buf, out_w, dz1_ref[...].astype(bf16), inv_ref)

    base = pl.multiple_of(step * pair, pair)
    for one in range(PAIR):
        here = slice(one * size, (one + 1) * size)
        do = back_head(do_buf[pl.ds(base + one * size, size), :], o_ref[here, :])
        q, k, v = q_ref[here, :], k_ref[here, :], with_ones(v_ref[here, :])
        dq = [None] * blocks
        for i in range(blocks):
            mine = slice(i * BLOCK, (i + 1) * BLOCK)
            several = min(blocks - i, REACH + 1)
            seen = slice(i * BLOCK, (i + several) * BLOCK)
            weights = e_ref[one, i, :, : several * BLOCK]
            ds = (weights.astype(f32) * dot(v[:, mine], do[:, seen], 0, 0)).astype(bf16)
            dv_ref[here, mine] = dot(do[:size, seen], weights, 1, 1).astype(bf16)
            dk_ref[here, mine] = (dot(q[:, seen], ds, 1, 1) * LN2).astype(bf16)
            part = dot(k[:, mine], ds, 1, 0)
            for b in range(several):
                piece = part[:, b * BLOCK : (b + 1) * BLOCK]
                dq[i + b] = piece if dq[i + b] is None else dq[i + b] + piece
        for j in range(blocks):
            dq_ref[here, j * BLOCK : (j + 1) * BLOCK] = (dq[j] * size**-0.5).astype(bf16)


def self_weights_kernel(
    digit_ref, old_ref, x_hbm, dq_hbm, dk_hbm, dv_hbm, dz1_hbm, o_hbm, *refs
):
    keeps, sends, refs = refs[:1], refs[1:2], refs[2:]
    (
        x_ref, dq_ref, dk_ref, dv_ref, dz1_ref, o_ref, grad_buf, sems,
    ) = refs
    width = x_ref.shape[1]
    refs = (x_ref, dq_ref, dk_ref, dv_ref, dz1_ref, o_ref)
    loads = [
        pltpu.make_async_copy(source, target, sems.at[i])
        for i, (source, target) in enumerate(
            zip((x_hbm, dq_hbm, dk_hbm, dv_hbm, dz1_hbm, o_hbm), refs)
        )
    ]
    start(loads)
    loads[0].wait()
    sums = []
    for part, ref in enumerate((dq_ref, dk_ref, dv_ref)):
        loads[1 + part].wait()
        d = ref[...]
        grad_buf[:, (part + 1) * width : (part + 2) * width] = dot(x_ref[...], d, 0, 1).astype(bf16)
        sums.append(feature_sum(d) if part != 1 else None)
    row = lax.broadcasted_iota(jnp.int32, old_ref.shape, 0)
    small = jnp.where(row == SELF_BIAS, sums[0], old_ref[...])
    small = jnp.where(row == SELF_BIAS + 1, sums[2], small)
    small = jnp.concatenate((small, jnp.zeros((LANES - SMALL, width), f32)), axis=0)
    grad_buf[:, 4 * width :] = jnp.transpose(small).astype(bf16)
    wait(loads[4:])
    grad_buf[:, :width] = dot(o_ref[...], dz1_ref[...].astype(bf16), 1, 0).astype(bf16)
    wait(halves(digit_ref, grad_buf, keeps, sends, sems, len(loads)))


def memory_kernel(digit_ref, dkv_ref, kv_w, *mem_refs):
    rows = mem_refs[0].shape[0]
    for b, mem_ref in enumerate(mem_refs):
        part = dkv_ref[:, b * rows : (b + 1) * rows]
        mem_ref[...] = dot(part, kv_w[...], 0, 1).astype(bf16)


def token_kernel(digit_ref, dq_ref, dk_ref, dv_ref, dz1_ref, par_ref, qkv_w, token_ref):
    width = dz1_ref.shape[1]
    total = par_ref[OMEGA : OMEGA + 1] * dz1_ref[...]
    for part, ref in enumerate((dq_ref, dk_ref, dv_ref)):
        total = total + dot(ref[...], qkv_w[:, part * width : (part + 1) * width], 0, 1)
    token_ref[...] = total.astype(bf16)


def tree_sum(values):
    while len(values) > 1:
        values = [a + b for a, b in zip(values[::2], values[1::2])]
    return values[0]


def combine_kernel(stage, outs, groups, *refs):
    sources, results = refs[1 : 1 + sum(groups)], refs[1 + sum(groups) :]
    rows = results[0].shape[0]
    for d in range(outs):
        begin = 0 if outs == 1 else pl.multiple_of((refs[0][stage] ^ d) * rows, rows)
        left, column = list(sources), 0
        for count in groups:
            group, left = left[:count], left[count:]
            total = tree_sum([ref[pl.ds(begin, rows), :].astype(f32) for ref in group])
            width = total.shape[1]
            results[d][:, column : column + width] = total.astype(bf16)
            column += width


def place_kernel(stage, ins, *refs):
    digit, sources, result = refs[0][stage], refs[1 : 1 + ins], refs[1 + ins]
    rows = sources[0].shape[0]
    for d in range(ins):
        result[pl.ds(pl.multiple_of((digit ^ d) * rows, rows), rows), :] = sources[d][...]


def finish_kernel(
    digit_ref, mine_hbm, other_hbm, cross_q, cross_out, cross_kv, self_out, self_qkv,
    self_bias, self_out_bias, cross_bias, cross_out_bias, in_bias, out_bias, omega, gain, shift,
    buf, last, *refs
):
    targets = (cross_q, cross_out, cross_kv, self_out, self_qkv)
    bufs, sems = refs[: len(targets)], refs[len(targets)]
    rows = mine_hbm.shape[0]
    loads = [
        pltpu.make_async_copy(source, buf.at[i], sems.at[2 * len(targets) + i])
        for i, source in enumerate((mine_hbm, other_hbm))
    ]
    start(loads)
    outs = []
    for half, load in enumerate(loads):
        load.wait()
        here = pl.ds(pl.multiple_of((digit_ref[0] ^ half) * rows, rows), rows)
        begin = 0
        for i, (target, wide) in enumerate(zip(targets, bufs)):
            count = target.shape[1]
            wide[half] = buf[half, :, begin : begin + count].astype(f32)
            sem = sems.at[2 * i + half]
            outs.append(pltpu.make_async_copy(wide.at[half], target.at[here], sem))
            outs[-1].start()
            begin += count
        last[here, :] = buf[half, :, begin:]
    part = jnp.transpose(last[...].astype(f32))
    begin = 0
    for target in (
        self_bias, self_out_bias, cross_bias, cross_out_bias, in_bias, out_bias, omega, gain, shift,
    ):
        count = target.shape[0]
        target[...] = part[begin : begin + count]
        begin += count
    wait(outs)


def spread_kernel(stage, digit_ref, *refs):
    *sources, target = refs
    for d, source in enumerate(sources):
        target[digit_ref[stage] ^ far_first(d, len(sources))] = source[...]


def ffn_finish_kernel(digit_ref, mine_hbm, other_hbm, out_hbm, in_hbm, buf, out_buf, in_buf, sems):
    rows, width = mine_hbm.shape
    chunks = out_hbm.shape[0] // width
    loads = [
        pltpu.make_async_copy(source, buf.at[digit_ref[0] ^ i], sems.at[2 * chunks + i])
        for i, source in enumerate((mine_hbm, other_hbm))
    ]
    start(loads)
    wait(loads)
    outs = []
    for c in range(chunks):
        half, place = c // (chunks // 2), c % (chunks // 2) * width
        out_buf[c] = buf[half, place : place + width, :].astype(f32)
        place += rows // 2
        in_buf[c] = buf[half, place : place + width, :].astype(f32)
        here = slice(c * width, (c + 1) * width)
        outs.append(pltpu.make_async_copy(out_buf.at[c], out_hbm.at[here], sems.at[2 * c]))
        outs.append(pltpu.make_async_copy(in_buf.at[c], in_hbm.at[:, here], sems.at[2 * c + 1]))
        start(outs[-2:])
    wait(outs)


class Order:
    def __init__(self, digits):
        self.digits = digits

    def after(self, value):
        return lax.optimization_barrier((value, self.digits))[0]

    def through(self, value):
        value, self.digits = lax.optimization_barrier((value, self.digits))
        return value

    def __call__(self, kernel, steps, ins, outs, scratch=(), vmem=VMEM, us=1):
        def whole(shape):
            return pl.BlockSpec(shape, lambda i: (0,) * len(shape), pipeline_mode=pl.Buffered(1))

        arrays, in_specs, shapes, out_specs = (
            [self.digits], [pl.BlockSpec(memory_space=pltpu.SMEM)], [], []
        )
        anywhere = pl.BlockSpec(memory_space=pl.ANY)
        for item in ins:
            if isinstance(item, tuple):
                arrays.append(item[0])
                in_specs.append(pl.BlockSpec(*item[1:]) if item[1:] else anywhere)
            else:
                arrays.append(item)
                in_specs.append(whole(item.shape))
        for shape, dtype, *block in outs:
            shapes.append(jax.ShapeDtypeStruct(shape, dtype))
            if block == [None]:
                out_specs.append(anywhere)
            elif block:
                out_specs.append(pl.BlockSpec(*block))
            else:
                out_specs.append(pl.BlockSpec(shape, lambda i, n=len(shape): (0,) * n))
        result = pl.pallas_call(
            kernel,
            grid=(steps,),
            in_specs=in_specs,
            out_specs=out_specs,
            out_shape=shapes,
            scratch_shapes=list(scratch),
            compiler_params=pltpu.CompilerParams(
                dimension_semantics=("arbitrary",), vmem_limit_bytes=vmem
            ),
            cost_estimate=pl.CostEstimate(flops=us * 10**9, bytes_accessed=0, transcendentals=0),
        )(*arrays)
        self.digits = lax.optimization_barrier((self.digits, result[0]))[0]
        return result


def stages_of(sizes):
    result = []
    for axis in ("dp", "ctx"):
        stride = 1
        while stride < sizes[axis]:
            left = sizes[axis] // stride
            count = 2 if (axis == "dp" and stride == 1) or left % 4 else 4
            result.append((axis, stride, count))
            stride *= count
    return result


class Sum:
    def __init__(self, order, stages, sizes, pieces):
        self.order, self.stages, self.sizes = order, stages, sizes
        self.stage, self.spread, self.pieces, self.others = 0, [], pieces, []
        self.send(0)

    def send(self, stage):
        axis, stride, count = self.stages[stage]
        pieces = self.pieces if len(self.pieces) > 1 else self.pieces * count
        self.got = [
            lax.ppermute(
                pieces[d], axis, [(i, i ^ (d * stride)) for i in range(self.sizes[axis])]
            )
            for d in range(1, count)
        ]

    def settle(self):
        self.spread.append(self.stage)
        self.stage += 1
        group = [self.pieces[0], *self.got]
        self.pieces, self.got = self.order(
            functools.partial(combine_kernel, self.stage, 1, [len(group)]), 1, group,
            [(group[0].shape, bf16)], vmem=SMALL_VMEM,
        ), []

    def join(self, other):
        self.others.append(other)

    def step(self):
        groups = [[one.pieces[0], *one.got] for one in (*self.others, self)]
        rows = groups[0][0].shape[0]
        width = sum(group[0].shape[1] for group in groups)
        outs = 1
        if self.stage < len(self.stages):
            if len(self.pieces) > 1:
                self.spread.append(self.stage)
            self.stage += 1
            if self.stage < len(self.stages):
                count = self.stages[self.stage][2]
                outs = count if rows % (PAD * count) == 0 else 1
            kernel = functools.partial(
                combine_kernel, self.stage, outs, [len(group) for group in groups]
            )
            rows //= outs
        else:
            stage = self.spread.pop()
            kernel = functools.partial(place_kernel, stage, len(groups[0]))
            rows *= len(groups[0])
        self.others = []
        self.pieces = self.order(
            kernel, 1, sum(groups, []), [((rows, width), bf16)] * outs, vmem=SMALL_VMEM
        )
        self.send(self.stage if self.stage < len(self.stages) else self.spread[-1])

    @property
    def last(self):
        return self.stage == len(self.stages) and len(self.spread) == 1


def local(sizes, *args):
    (
        tokens, memory, mem_mask, segment_ids, cotangent, self_qkv, self_bias, self_out,
        self_out_bias, cross_q, cross_kv, cross_bias, cross_out, cross_out_bias, ffn_in,
        ffn_in_bias, ffn_out, ffn_out_bias, omegas, ln_gains, ln_biases,
    ) = args
    length, width = tokens.shape[1:]
    hidden = ffn_in.shape[1]
    size = width // HEADS
    holders, part_rows = memory.shape[:2]
    count = holders * part_rows
    x = tokens.reshape(length, width)
    cot = cotangent.reshape(length, width)
    seg = segment_ids.reshape(1, length)
    stages = stages_of(sizes)
    digits = [(lax.axis_index(axis) // stride) % several for axis, stride, several in stages]
    first_ctx = [axis for axis, _, _ in stages].index("ctx")
    order = Order(jnp.stack(digits).astype(jnp.int32))

    blocks = length // BLOCK
    reach = (REACH + 1) * BLOCK

    pairs, pair = HEADS // PAIR, PAIR * size

    def scores_in(array):
        shape = (PAIR, *array.shape[1:])
        return (array, shape, lambda i: (i,) + (0,) * (len(shape) - 1))

    def scores_out(*shape):
        return ((HEADS, *shape), bf16, None)

    def pair_in(array, part=0):
        return (array, (pair, array.shape[1]), lambda i: (part * pairs + i, 0))

    def vmem(*shape, dtype=bf16):
        return pltpu.VMEM(shape, dtype)

    dma = pltpu.SemaphoreType.DMA
    tall, wide = (width, length), (length, width)
    small, *pieces = order(
        functools.partial(prepare_kernel, first_ctx),
        1,
        [
            memory, mem_mask, self_bias, self_out_bias, cross_bias, cross_out_bias, ffn_in_bias,
            ffn_out_bias, omegas, ln_gains, ln_biases,
        ],
        [((SMALL, width), f32)] + [((part_rows + PAD, width), bf16)] * holders,
    )

    def trade(pieces):
        return [pieces[0]] + [
            lax.ppermute(
                pieces[j], "ctx", [(i, i ^ far_first(j, holders)) for i in range(holders)]
            )
            for j in range(1, holders)
        ]

    pieces = trade(pieces)
    qkv, e_self, inv_self, o, z1, h1, q2 = order(
        self_forward_kernel,
        pairs,
        [x, seg, small, self_qkv, (self_out,), (cross_q,)],
        [
            ((3 * width, length), bf16, None),
            scores_out(blocks, BLOCK, reach),
            ((HEADS, length), f32),
            (tall, bf16, None),
            (wide, f32, None),
            (wide, bf16, None),
            (tall, bf16, None),
        ],
        [
            vmem(3 * width, length), vmem(2, PAIR, blocks, BLOCK, reach), vmem(*tall),
            vmem(*wide, dtype=f32), vmem(*wide), vmem(*tall),
            vmem(width, width), vmem(width, width), vmem(PAD, length), vmem(PAD, length), dma((7,)),
            dma((2, PAIR)),
        ],
        us=15,
    )
    kv, e_cross, inv_cross, o2, z2, h2 = order(
        functools.partial(cross_forward_kernel, holders),
        pairs,
        [pair_in(q2), small, cross_kv, (h1,), (cross_out,), *pieces],
        [
            ((2 * width, count), bf16, None),
            scores_out(count, length),
            ((HEADS, length), f32),
            (tall, bf16, None),
            (wide, f32, None),
            (wide, bf16, None),
        ],
        [
            vmem(2 * width, count), vmem(2, PAIR, count, length), vmem(*tall),
            vmem(*wide, dtype=f32), vmem(*wide), vmem(*wide), vmem(width, width), vmem(PAD, count),
            dma((6,)), dma((2, PAIR)),
        ],
        us=22,
    )
    rows = BLOCK
    chunks = hidden // width
    row_block = ((rows, width), lambda i: (i, 0))
    activations, dz2, keep, send, small_grad = order(
        ffn_kernel,
        length // rows,
        [
            (h2, *row_block), (h1, *row_block), (z2, *row_block), (cot, *row_block), small, ffn_in,
            (ffn_out,),
        ],
        [
            (wide, bf16, *row_block),
            (wide, f32, *row_block),
            ((hidden, width), bf16, None),
            ((hidden, width), bf16, None),
            ((SMALL, width), f32),
        ],
        [
            vmem(*wide), vmem(length, hidden), vmem(rows, hidden, dtype=f32), vmem(*wide),
            vmem(length, hidden), vmem(2, hidden, width), vmem(hidden, width),
            dma((2 * chunks + 1,)),
        ],
        us=26,
    )
    def open_sum(parts):
        several = len(parts) // 2
        *others, last = [
            Sum(order, stages, sizes, [keep, send])
            for keep, send in zip(parts[:several], parts[several:])
        ]
        for one in others:
            last.join(one)
        return last

    ffn_sum = open_sum([keep, send])
    (do2,) = order(back_start_kernel, 1, [dz2, inv_cross, cross_out], [(tall, bf16)], us=3)
    ffn_sum.step()
    parts = [((width // 2, 2 * width), bf16, None)] * 4
    dkv, dz1, small_grad, p0, p1, p2, p3 = order(
        functools.partial(cross_backward_kernel, holders),
        pairs,
        [
            scores_in(e_cross), pair_in(do2), pair_in(o2), pair_in(q2), pair_in(kv), pair_in(kv, 1),
            small, small_grad, (z1,), (h1,), (x,), (cross_q,), (dz2,),
            *[(piece,) for piece in pieces],
        ],
        [((2 * width, count), bf16, None), (wide, f32, None), ((SMALL, width), f32)] + parts,
        [
            vmem(*wide, dtype=f32), vmem(*wide), vmem(*wide), vmem(width, width),
            vmem(*wide, dtype=f32), vmem(*memory.shape), vmem(*tall), vmem(*tall),
            vmem(2 * width, count), vmem(*wide, dtype=f32), vmem(width, 4 * width),
            dma((5 + holders + 5 + 2 * pairs,)),
        ],
        us=26,
    )
    cross_sum = open_sum([p0, p1, p2, p3])
    ffn_sum.step()
    cross_sum.step()
    total = 4 * width + LANES
    pair_out = (tall, bf16, (pair, length), lambda i: (i, 0))
    dq, dk, dv = order(
        self_backward_kernel,
        pairs,
        [
            scores_in(e_self), inv_self, pair_in(o), pair_in(qkv), pair_in(qkv, 1), pair_in(qkv, 2),
            dz1, self_out,
        ],
        [pair_out] * 3,
        [vmem(*tall)],
        us=16,
    )
    for _ in range(first_ctx - 2):
        cross_sum.step()
    cross_sum.settle()
    ffn_sum.step()
    parts = [((width // 2, total), bf16, None)] * 2
    self_sum = open_sum(
        order(
            self_weights_kernel,
            1,
            [small_grad, (x,), (dq,), (dk,), (dv,), (dz1,), (o,)],
            parts,
            [
                vmem(*wide), vmem(*tall), vmem(*tall), vmem(*tall), vmem(*wide, dtype=f32),
                vmem(*tall), vmem(width, total), dma((6 + 10,)),
            ],
            us=7,
        )
    )
    mem_parts = order(
        memory_kernel, 1, [dkv, cross_kv], [((part_rows, width), bf16)] * holders, us=3
    )
    for _ in range(first_ctx - 1):
        self_sum.step()
    self_sum.join(cross_sum)
    self_sum.step()
    ffn_sum.step()
    self_sum.step()
    turned = ((width, rows), lambda i: (0, i))
    (token_grad,) = order(
        token_kernel,
        length // rows,
        [(dq, *turned), (dk, *turned), (dv, *turned), (dz1, *row_block), small, self_qkv],
        [(wide, bf16, *row_block)],
        us=6,
    )
    while not ffn_sum.last:
        ffn_sum.step()
    while len(self_sum.spread) > 2 or self_sum.stage < len(stages):
        self_sum.step()
    mem_parts = trade(order.after(mem_parts))
    (memory_grad,) = order(
        functools.partial(spread_kernel, first_ctx), 1, mem_parts, [(memory.shape, bf16)],
        vmem=SMALL_VMEM,
    )
    self_sum.step()
    while not self_sum.last:
        self_sum.step()
    square = (width, width)
    grad_ffn_out, grad_ffn_in = order(
        ffn_finish_kernel,
        1,
        [(ffn_sum.pieces[0],), (ffn_sum.got[0],)],
        [((hidden, width), f32, None), ((width, hidden), f32, None)],
        [
            vmem(2, hidden, width), vmem(chunks, *square, dtype=f32),
            vmem(chunks, *square, dtype=f32), dma((2 * chunks + 2,)),
        ],
        vmem=SMALL_VMEM,
    )
    shapes = [(width, several * width) for several in (1, 1, 2, 1, 3)]
    shapes += [(several, width) for several in (2, 1, 2, 1, chunks, 1, 3, 3, 3)]
    large = [shape for shape in shapes if shape[0] == width]
    grad_cross_q, grad_cross_out, grad_cross_kv, grad_out, grad_qkv, *smalls = order(
        finish_kernel,
        1,
        [(self_sum.pieces[0],), (self_sum.got[0],)],
        [(shape, f32, None) if shape in large else (shape, f32) for shape in shapes],
        [
            vmem(2, width // 2, 8 * width + LANES), vmem(width, LANES),
            *[vmem(2, width // 2, shape[1], dtype=f32) for shape in large], dma((12,)),
        ],
        vmem=SMALL_VMEM,
    )
    (
        self_bias, self_out_bias, cross_bias, cross_out_bias, in_bias, out_bias, omega, gain, shift
    ) = smalls
    return (
        activations.reshape(tokens.shape),
        token_grad.reshape(tokens.shape),
        memory_grad,
        grad_qkv,
        self_bias,
        grad_out,
        self_out_bias.reshape(-1),
        grad_cross_q,
        grad_cross_kv,
        cross_bias,
        grad_cross_out,
        cross_out_bias.reshape(-1),
        grad_ffn_in,
        in_bias.reshape(-1),
        grad_ffn_out,
        out_bias.reshape(-1),
        omega,
        gain,
        shift,
    )


def solution(mesh):
    sizes = dict(mesh.shape)
    both = P(("dp", "ctx"), None, None)
    return jax.shard_map(
        functools.partial(local, sizes),
        mesh=mesh,
        in_specs=(both, P("dp", "ctx", None), P("dp", "ctx"), P(("dp", "ctx"), None), both)
        + (P(),) * 16,
        out_specs=(both, both, P("dp", "ctx", None)) + (P(),) * 16,
        check_vma=False,
    )
```
